32 devices in a mesh: loop: 2 (over x), row: 4 (over y, core), col: 4 (over z).
Axes of the slice: x: 2, y: 2, z: 4, core: 2. Of those that a mesh axis runs over, the one named last changes fastest.
Arguments:
- interval_blocks: bfloat16 [2, 4, 2048, 2048], P('loop', None, 'row', 'col'), may hold values from -0.15625 to 0.15625
- interval_pivots: int32 [2, 3, 2048], P('loop'), may hold values from 0 to 2047, each once within a row
- boundary_pivots: int32 [2, 2048], replicated, may hold values from 0 to 2047, each once within a row
- interval_residuals: bfloat16 [2, 4, 2048], P('loop', None, ('row', 'col')), may hold values from -0.23925781 to 0.23925781
Outputs:
- reduced_block: bfloat16 [2, 2048, 2048], P('loop', 'row', 'col')
- reduced_rhs: float32 [2, 2048], P('loop', ('row', 'col'))
The draws below stay inside these ranges and needn't reach their ends.
Inputs may be any that keep to these rules, and one draw needn't show every extreme that they name: Each row of interval_pivots is a permutation of 0 to 2047. Each row of boundary_pivots is a permutation of 0 to 2047.
All inputs are finite; a program needn't handle non-finite values.
Results may differ from the reference program's by a relative error of at most 0.018.
Values may be sent and summed in bfloat16 or wider, within the bound.
No kernel may reach another device: no remote copies, remote signals or barrier semaphores. Data moves between devices by JAX's collectives and lax.ppermute only.
A program may use at most 64 MiB of HBM per device.

```python
import jax
import jax.numpy as jnp
from jax import lax

STATE = 2048
INTERVALS = 4
POSITIONS = 2


def block_levels(rng, shape, split, low, high):
    def one(dim, shards_of):
        draws = jax.random.uniform(jax.random.fold_in(jax.random.fold_in(rng, 6), dim), (shards_of,), jnp.float32, low / len(split), high / len(split))
        return jnp.repeat(jnp.exp(draws), shape[dim] // shards_of).reshape((-1,) + (1,) * (len(shape) - dim - 1))

    loudness = one(*split[0])
    for cut in split[1:]:
        loudness = loudness * one(*cut)
    return loudness


def centred(key, shape, deviation, most, split=(), dtype=jnp.bfloat16):
    loudness = block_levels(key, shape, split, -0.22, 0.18) if split else 1.0
    drawn = jax.random.normal(key, shape, jnp.float32) * deviation * loudness
    return jnp.minimum(jnp.maximum(drawn, -most), most).astype(dtype)


def setup_inputs(seed: int = 0) -> dict:
    splits = jax.random.split(jax.random.key(seed), 5)
    interval_blocks = centred(splits[0], (POSITIONS, INTERVALS, STATE, STATE), (STATE * 11 // 16) ** -0.5, 0.15625, ((0, 2), (2, 4), (3, 4)))
    interval_pivots = jax.vmap(lambda own: jax.random.permutation(own, STATE))(jax.random.split(splits[1], POSITIONS * (INTERVALS - 1))).reshape((POSITIONS, INTERVALS - 1, STATE)).astype(jnp.int32)
    boundary_pivots = jax.vmap(lambda own: jax.random.permutation(own, STATE))(jax.random.split(splits[2], POSITIONS)).reshape((POSITIONS, STATE)).astype(jnp.int32)
    interval_residuals = centred(splits[3], (POSITIONS, INTERVALS, STATE), 0.04, 0.23925781, ((0, 2), (2, 16)))
    return {"interval_blocks": interval_blocks, "interval_pivots": interval_pivots, "boundary_pivots": boundary_pivots, "interval_residuals": interval_residuals}


def compose(left_block, right_block, right_vector, pivots, added):
    permuted = jnp.take(right_block, pivots, axis=0)
    moved = jnp.take(right_vector, pivots, axis=0)
    product = jnp.dot(left_block, permuted, preferred_element_type=jnp.float32)
    applied = jnp.dot(left_block, moved, preferred_element_type=jnp.float32) + added.astype(jnp.float32)
    return product, applied


def condense(inputs):
    blocks, pivots, residuals = inputs
    matrix = blocks[0]
    vector = residuals[0]
    for interval in range(1, INTERVALS):
        product, applied = compose(blocks[interval], matrix, vector, pivots[interval - 1], residuals[interval])
        matrix = product.astype(jnp.bfloat16)
        vector = applied.astype(jnp.bfloat16)
    return matrix, vector


def level_first(inputs):
    current, current_vector, earlier, earlier_vector, pivots = inputs
    product, applied = compose(current, earlier, earlier_vector, pivots, current_vector)
    return product.astype(jnp.bfloat16), applied.astype(jnp.bfloat16)


def level_second(inputs):
    current, current_vector, earlier, earlier_vector, pivots = inputs
    product, applied = compose(current, earlier, earlier_vector, pivots, current_vector)
    return product.astype(jnp.bfloat16), applied


def reference(interval_blocks, interval_pivots, boundary_pivots, interval_residuals):
    cond_matrix, cond_vector = lax.map(condense, (interval_blocks, interval_pivots, interval_residuals))
    halved, halved_vector = lax.map(level_first, (cond_matrix, cond_vector, jnp.roll(cond_matrix, 1, axis=0), jnp.roll(cond_vector, 1, axis=0), boundary_pivots))
    reduced_block, reduced_rhs = lax.map(level_second, (halved, halved_vector, jnp.roll(halved, 2, axis=0), jnp.roll(halved_vector, 2, axis=0), jnp.roll(boundary_pivots, 1, axis=0)))
    return reduced_block, reduced_rhs
```

```python
import jax
import jax.numpy as jnp
from jax import lax
from jax.experimental import pallas as pl
from jax.experimental.pallas import tpu as pltpu
from jax.sharding import PartitionSpec as P

EXTRA = 16
VMEM = 48 * 1024 * 1024
NT = (((1,), (1,)), ((), ()))


def from_behind(value, axis, by):
    devices = lax.axis_size(axis)
    if by % devices == 0:
        return value
    return lax.ppermute(value, axis, [(i, (i + by) % devices) for i in range(devices)])


def swap_rows(value, flip):
    rows, cols = lax.axis_size("row"), lax.axis_size("col")
    pairs = [(r * cols + c, (r ^ flip) * cols + c) for r in range(rows) for c in (1, 2)]
    return lax.ppermute(value, ("row", "col"), pairs)


def swap_middle(value):
    return lax.ppermute(value, "col", [(1, 2), (2, 1)])


def inward(value):
    return lax.ppermute(value, "col", [(0, 1), (3, 2)])


def outward(value):
    return lax.ppermute(value, "col", [(1, 0), (2, 3)])


def row_tiles(tile):
    across = swap_rows(tile, 2)
    return [tile, swap_rows(tile, 1), across, swap_rows(across, 1)]


def spread(tiles, q_ref, first, size, count):
    def block(n):
        total = None
        for b, tile in enumerate(tiles):
            at = lax.broadcasted_iota(jnp.int32, (size, size), 0) + n * size
            hot = jnp.where(at == q_ref[first + b : first + b + 1, :], 1.0, 0.0).astype(jnp.bfloat16)
            part = lax.dot_general(tile[0:size, :], hot, NT, preferred_element_type=jnp.float32)
            total = part if total is None else total + part
        return total

    return block


def spread_kernel(q_ref, own_o, own_e, out):
    size = out.shape[0]
    count = out.shape[1] // size
    block = spread((own_o, own_e), q_ref, 0, size, count)

    @pl.loop(0, count)
    def _(n):
        out[:, pl.ds(pl.multiple_of(n * size, size), size)] = block(n).astype(out.dtype)


def compose_kernel(riding, q_ref, partial, other_o, other_e, added, *rest):
    if riding:
        vector = None
    else:
        vector, rest = rest[0], rest[1:]
    right_o, right_e = rest[0:4], rest[4:8]
    out_o, out_e, out_v, left = rest[8:]
    size = partial.shape[0]
    count = partial.shape[1] // size
    block = spread((other_o, other_e), q_ref, 2, size, count)

    @pl.loop(0, count)
    def _(n):
        here = pl.ds(pl.multiple_of(n * size, size), size)
        left[:, here] = partial[:, here] + block(n).astype(left.dtype)

    applied = added[...]
    for right, out in ((right_o, out_o), (right_e, out_e)):
        total = None
        for b in range(count):
            part = jnp.dot(
                left[:, b * size : (b + 1) * size],
                right[b][0:size, :],
                preferred_element_type=jnp.float32,
            )
            total = part if total is None else total + part
        out[0:size, :] = total.astype(out.dtype)
    for b in range(count):
        if riding:
            rows = right_o[b][size : size + EXTRA, :]
        else:
            rows = vector[:, b * size : (b + 1) * size]
        applied = applied + lax.dot_general(
            rows, left[:, b * size : (b + 1) * size], NT, preferred_element_type=jnp.float32
        )
    out_v[...] = applied
    out_o[size : size + EXTRA, :] = applied.astype(out_o.dtype)


def spread_own(pivots, own_o, own_e, size, count):
    return pl.pallas_call(
        spread_kernel,
        out_shape=jax.ShapeDtypeStruct((size, size * count), jnp.bfloat16),
        compiler_params=pltpu.CompilerParams(vmem_limit_bytes=VMEM),
        cost_estimate=pl.CostEstimate(
            flops=4 * size * size * size * count, bytes_accessed=8 * size * size, transcendentals=0
        ),
    )(pivots, own_o, own_e)


def compose(pivots, partial, other, added, right_o, right_e, vector=None):
    size = partial.shape[0]
    count = partial.shape[1] // size
    riding = vector is None

    def body(*refs):
        compose_kernel(riding, *refs)

    extra = () if riding else (vector,)
    return pl.pallas_call(
        body,
        out_shape=(
            jax.ShapeDtypeStruct((size + EXTRA, size), jnp.bfloat16),
            jax.ShapeDtypeStruct((size, size), jnp.bfloat16),
            jax.ShapeDtypeStruct((EXTRA, size), jnp.float32),
        ),
        scratch_shapes=[pltpu.VMEM((size, size * count), jnp.bfloat16)],
        compiler_params=pltpu.CompilerParams(vmem_limit_bytes=VMEM),
        cost_estimate=pl.CostEstimate(
            flops=8 * size * size * size * count, bytes_accessed=24 * size * size, transcendentals=0
        ),
    )(pivots, partial, *other, added, *extra, *right_o, *right_e)


def shards(interval_blocks, interval_pivots, boundary_pivots, interval_residuals):
    blocks = interval_blocks[0]
    size = blocks.shape[1]
    row, col = lax.axis_index("row"), lax.axis_index("col")
    count = lax.axis_size("row")
    position = lax.axis_index("loop")
    positions = lax.axis_size("loop")

    own = lax.dynamic_index_in_dim(boundary_pivots, position, 0, keepdims=True)
    back = lax.dynamic_index_in_dim(
        boundary_pivots, (position + positions - 1) % positions, 0, keepdims=True
    )
    pivots = jnp.concatenate([interval_pivots[0], own, back], axis=0)
    pivots = (((pivots // size) ^ row) * size + pivots % size).reshape(pivots.shape[0], count, size)
    order = [
        lax.dynamic_index_in_dim(pivots, col ^ flip, 1, keepdims=True) for flip in (0, 1, 3, 2)
    ]
    pivots = jnp.concatenate(order, axis=1)

    residuals = lax.all_gather(interval_residuals[0], ("row", "col"), axis=0)
    residuals = residuals.reshape(count, -1, *interval_residuals.shape[1:])
    residuals = jnp.moveaxis(residuals, 2, 0).reshape(blocks.shape[0], count, size)
    tiles = [
        lax.dynamic_index_in_dim(residuals, row ^ flip, 1, keepdims=False) for flip in range(count)
    ]
    full = jnp.concatenate(tiles, axis=1)
    vectors = [jnp.broadcast_to(full[k][None], (EXTRA, full.shape[1])) for k in (0, 2)]
    adds = [
        jnp.broadcast_to(tiles[0][k][None], (EXTRA, size)).astype(jnp.float32) for k in (1, 3)
    ]

    ends = {k: inward(blocks[k]) for k in (3, 2, 1, 0)}

    def first(left, right, turn, vector, added):
        other = [swap_middle(blocks[left]), swap_middle(ends[left])]
        partial = spread_own(pivots[turn], blocks[left], ends[left], size, count)
        right_o, right_e = row_tiles(blocks[right]), row_tiles(ends[right])
        return compose(pivots[turn], partial, other, added, right_o, right_e, vector)

    def later(left, right, turn):
        left_o, left_e, added = left
        right_o, right_e = right
        other = [swap_middle(left_o), swap_middle(left_e)]
        partial = spread_own(pivots[turn], left_o, left_e, size, count)
        return compose(
            pivots[turn], partial, other, added, row_tiles(right_o), row_tiles(right_e)
        )

    upper = first(3, 2, 2, vectors[1], adds[1])
    lower = first(1, 0, 0, vectors[0], adds[0])
    whole = later(upper, lower[:2], 1)
    earlier = [from_behind(tile, "loop", 1) for tile in whole[:2]]
    halved = later(whole, earlier, 3)
    distant = [from_behind(tile, "loop", 2) for tile in halved[:2]]
    reduced_o, reduced_e, applied = later(halved, distant, 4)

    middle = (col == 1) | (col == 2)
    block = jnp.where(middle, reduced_o[:size], outward(reduced_e))
    vector = applied[:1]
    vector = jnp.where(middle, vector, outward(vector))
    share = interval_residuals.shape[2]
    return (block[None], lax.dynamic_slice_in_dim(vector, col * share, share, 1))


def solution(mesh):
    placed = (
        P("loop", None, "row", "col"),
        P("loop", None, None),
        P(),
        P("loop", None, ("row", "col")),
    )
    return jax.shard_map(
        shards,
        mesh=mesh,
        in_specs=placed,
        out_specs=(P("loop", "row", "col"), P("loop", ("row", "col"))),
        check_vma=False,
    )
```

```python
import jax
import jax.numpy as jnp
from jax import lax
from jax.experimental import pallas as pl
from jax.experimental.pallas import tpu as pltpu
from jax.sharding import PartitionSpec as P

EXTRA = 16
VMEM = 24 * 1024 * 1024
NT = (((1,), (1,)), ((), ()))


def from_behind(value, axis, by):
    devices = lax.axis_size(axis)
    if by % devices == 0:
        return value
    return lax.ppermute(value, axis, [(i, (i + by) % devices) for i in range(devices)])


def swap_rows(value, flip):
    rows, cols = lax.axis_size("row"), lax.axis_size("col")
    pairs = [(r * cols + c, (r ^ flip) * cols + c) for r in range(rows) for c in (1, 2)]
    return lax.ppermute(value, ("row", "col"), pairs)


def swap_middle(value):
    return lax.ppermute(value, "col", [(1, 2), (2, 1)])


def inward(value):
    return lax.ppermute(value, "col", [(0, 1), (3, 2)])


def outward(value):
    return lax.ppermute(value, "col", [(1, 0), (2, 3)])


class Operands:
    def __init__(self):
        self.arrays = []

    def add(self, view):
        array, lead, column = view
        for i, known in enumerate(self.arrays):
            if known is array:
                return i, lead, column
        self.arrays.append(array)
        return len(self.arrays) - 1, lead, column


def read(refs, view, size, rows=None):
    which, lead, column = view
    ref = refs[which] if lead is None else refs[which].at[lead]
    return ref[rows or slice(0, size), column : column + size]


def spread(refs, views, q_ref, first, size, n):
    total = None
    for b, view in enumerate(views):
        at = lax.broadcasted_iota(jnp.int32, (size, size), 0) + n * size
        hot = jnp.where(at == q_ref[first + b : first + b + 1, :], 1.0, 0.0).astype(jnp.bfloat16)
        part = lax.dot_general(
            read(refs, view, size), hot, NT, preferred_element_type=jnp.float32
        )
        total = part if total is None else total + part
    return total


def spread_own(pivots, own, size, count):
    operands = Operands()
    views = [operands.add(view) for view in own]

    def kernel(q_ref, *refs):
        out = refs[-1]

        @pl.loop(0, count)
        def _(n):
            here = pl.ds(pl.multiple_of(n * size, size), size)
            out[:, here] = spread(refs, views, q_ref, 0, size, n).astype(out.dtype)

    return pl.pallas_call(
        kernel,
        out_shape=jax.ShapeDtypeStruct((size, size * count), jnp.bfloat16),
        compiler_params=pltpu.CompilerParams(vmem_limit_bytes=VMEM),
        cost_estimate=pl.CostEstimate(
            flops=4 * size * size * size * count, bytes_accessed=8 * size * size, transcendentals=0
        ),
    )(pivots, *operands.arrays)


def compose(pivots, partial, other, added, right, vector, form, size):
    count = partial.shape[1] // size
    operands = Operands()
    left_views = [operands.add(view) for view in other]
    right_views = [[operands.add(view) for view in half] for half in right]
    tall, wide = size + EXTRA, 2 * size
    shapes = {
        "joint": [(tall, wide)],
        "both": [(tall, wide), (tall, size), (size, size)],
        "split": [(size, size), (size, size)],
    }[form]
    outs = [jax.ShapeDtypeStruct(shape, jnp.bfloat16) for shape in shapes]
    outs.append(jax.ShapeDtypeStruct((EXTRA, size), jnp.float32))
    extra = [] if vector is None else [vector]

    def kernel(q_ref, partial_ref, added_ref, *rest):
        vector_ref = None if vector is None else rest[0]
        rest = rest[len(extra) :]
        refs = rest[: len(operands.arrays)]
        results = rest[len(refs) : -1]
        left = rest[-1]

        @pl.loop(0, count)
        def _(n):
            here = pl.ds(pl.multiple_of(n * size, size), size)
            moved = spread(refs, left_views, q_ref, 2, size, n)
            left[:, here] = partial_ref[:, here] + moved.astype(left.dtype)

        for half in range(2):
            total = None
            for b in range(count):
                part = jnp.dot(
                    left[:, b * size : (b + 1) * size],
                    read(refs, right_views[half][b], size),
                    preferred_element_type=jnp.float32,
                )
                total = part if total is None else total + part
            total = total.astype(jnp.bfloat16)
            if form != "split":
                results[0][0:size, half * size : (half + 1) * size] = total
            if form != "joint":
                results[half + len(results) - 3][0:size, :] = total

        applied = added_ref[...]
        for b in range(count):
            if vector is None:
                rows = read(refs, right_views[0][b], size, slice(size, tall))
            else:
                rows = vector_ref[:, b * size : (b + 1) * size]
            applied = applied + lax.dot_general(
                rows, left[:, b * size : (b + 1) * size], NT, preferred_element_type=jnp.float32
            )
        results[-1][...] = applied
        if form != "split":
            results[0][size:tall, 0:size] = applied.astype(jnp.bfloat16)
            results[0][size:tall, size:wide] = applied.astype(jnp.bfloat16)
        if form == "both":
            results[1][size:tall, :] = applied.astype(jnp.bfloat16)

    return pl.pallas_call(
        kernel,
        out_shape=tuple(outs),
        scratch_shapes=[pltpu.VMEM((size, size * count), jnp.bfloat16)],
        compiler_params=pltpu.CompilerParams(vmem_limit_bytes=VMEM),
        cost_estimate=pl.CostEstimate(
            flops=8 * size * size * size * count, bytes_accessed=24 * size * size, transcendentals=0
        ),
    )(pivots, partial, added, *extra, *operands.arrays)


def shards(interval_blocks, interval_pivots, boundary_pivots, interval_residuals):
    blocks = interval_blocks[0]
    size = blocks.shape[1]
    row, col = lax.axis_index("row"), lax.axis_index("col")
    count = lax.axis_size("row")
    position = lax.axis_index("loop")
    positions = lax.axis_size("loop")

    def halves(array):
        return [(array, None, 0), (array, None, size)]

    lefts, rights = blocks[1::2], blocks[0::2]
    ends_upper = inward(blocks[2:4])
    lefts_other = swap_middle(lefts)
    rights_across = swap_rows(rights, 2)
    residuals = interval_residuals[0]
    beside = lax.ppermute(residuals, "col", [(0, 1), (1, 0), (2, 3), (3, 2)])
    ends_lower_left = inward(blocks[1])
    ends_lower_right = inward(blocks[0])
    rights_beside = swap_rows(rights, 1)
    rights_last = swap_rows(rights_across, 1)

    beyond = swap_middle(jnp.stack([residuals, beside]))
    near = (residuals, beside, beyond[0], beyond[1])
    residuals = jnp.where(
        col == 1,
        jnp.concatenate([near[i] for i in (1, 0, 2, 3)], axis=1),
        jnp.concatenate([near[i] for i in (3, 2, 0, 1)], axis=1),
    )
    vectors = residuals[0::2]
    vectors = jnp.concatenate([vectors, swap_rows(vectors, 1)], axis=1)
    vectors = jnp.concatenate([vectors, swap_rows(vectors, 2)], axis=1)
    vectors = [jnp.broadcast_to(vectors[k][None], (EXTRA, vectors.shape[1])) for k in (0, 1)]
    adds = [
        jnp.broadcast_to(residuals[k][None], (EXTRA, size)).astype(jnp.float32) for k in (1, 3)
    ]

    own = lax.dynamic_index_in_dim(boundary_pivots, position, 0, keepdims=True)
    back = lax.dynamic_index_in_dim(
        boundary_pivots, (position + positions - 1) % positions, 0, keepdims=True
    )
    pivots = jnp.concatenate([interval_pivots[0], own, back], axis=0)
    pivots = (((pivots // size) ^ row) * size + pivots % size).reshape(pivots.shape[0], count, size)
    order = [
        lax.dynamic_index_in_dim(pivots, col ^ flip, 1, keepdims=True) for flip in (0, 1, 3, 2)
    ]
    pivots = jnp.concatenate(order, axis=1)

    def first(turn, k, end_left, end_right, vector, added, form):
        other = [(lefts_other, k, 0), (swap_middle(end_left), None, 0)]
        across = swap_rows(end_right, 2)
        ends = [end_right, swap_rows(end_right, 1), across, swap_rows(across, 1)]
        right = [
            [(tile, k, 0) for tile in (rights, rights_beside, rights_across, rights_last)],
            [(tile, None, 0) for tile in ends],
        ]
        partial = spread_own(pivots[turn], [(lefts, k, 0), (end_left, None, 0)], size, count)
        return compose(pivots[turn], partial, other, added, right, vector, form, size)

    upper, upper_vector = first(2, 1, ends_upper[1], ends_upper[0], vectors[1], adds[1], "joint")
    lower, _ = first(0, 0, ends_lower_left, ends_lower_right, vectors[0], adds[0], "joint")

    def later(turn, left, added, right, form):
        other = swap_middle(left)
        parts = []
        for tile in right:
            across = swap_rows(tile, 2)
            parts.append([tile, swap_rows(tile, 1), across, swap_rows(across, 1)])
        if len(parts) == 1:
            views = [[(tile, None, column) for tile in parts[0]] for column in (0, size)]
        else:
            views = [[(tile, None, 0) for tile in part] for part in parts]
        partial = spread_own(pivots[turn], halves(left), size, count)
        return compose(pivots[turn], partial, halves(other), added, views, None, form, size)

    whole, whole_o, whole_e, whole_vector = later(1, upper, upper_vector, [lower], "both")
    earlier = [from_behind(tile, "loop", 1) for tile in (whole_o, whole_e)]
    halved, halved_vector = later(3, whole, whole_vector, earlier, "joint")
    distant = from_behind(halved, "loop", 2)
    reduced_o, reduced_e, applied = later(4, halved, halved_vector, [distant], "split")

    middle = (col == 1) | (col == 2)
    block = jnp.where(middle, reduced_o, outward(reduced_e))
    vector = applied[:1]
    vector = jnp.where(middle, vector, outward(vector))
    share = interval_residuals.shape[2]
    return (block[None], lax.dynamic_slice_in_dim(vector, col * share, share, 1))


def solution(mesh):
    placed = (
        P("loop", None, "row", "col"),
        P("loop", None, None),
        P(),
        P("loop", None, ("row", "col")),
    )
    return jax.shard_map(
        shards,
        mesh=mesh,
        in_specs=placed,
        out_specs=(P("loop", "row", "col"), P("loop", ("row", "col"))),
        check_vma=False,
    )
```

```python
import jax
import jax.numpy as jnp
from jax import lax
from jax.experimental import pallas as pl
from jax.experimental.pallas import tpu as pltpu
from jax.sharding import PartitionSpec as P

EXTRA = 16
VMEM = 24 * 1024 * 1024
NT = (((1,), (1,)), ((), ()))


def from_behind(value, axis, by):
    devices = lax.axis_size(axis)
    if by % devices == 0:
        return value
    return lax.ppermute(value, axis, [(i, (i + by) % devices) for i in range(devices)])


def swap_rows(value, flip):
    rows, cols = lax.axis_size("row"), lax.axis_size("col")
    pairs = [(r * cols + c, (r ^ flip) * cols + c) for r in range(rows) for c in (1, 2)]
    return lax.ppermute(value, ("row", "col"), pairs)


def swap_middle(value):
    return lax.ppermute(value, "col", [(1, 2), (2, 1)])


def inward(value):
    return lax.ppermute(value, "col", [(0, 1), (3, 2)])


def outward(value):
    return lax.ppermute(value, "col", [(1, 0), (2, 3)])


class Operands:
    def __init__(self):
        self.arrays = []

    def add(self, view):
        array, lead, column = view
        for i, known in enumerate(self.arrays):
            if known is array:
                return i, lead, column
        self.arrays.append(array)
        return len(self.arrays) - 1, lead, column


def read(refs, view, size, rows=None):
    which, lead, column = view
    ref = refs[which] if lead is None else refs[which].at[lead]
    return ref[rows or slice(0, size), column : column + size]


def spread(refs, views, q_ref, first, size, n):
    total = None
    for b, view in enumerate(views):
        at = lax.broadcasted_iota(jnp.int32, (size, size), 0) + n * size
        hot = jnp.where(at == q_ref[first + b : first + b + 1, :], 1.0, 0.0).astype(jnp.bfloat16)
        part = lax.dot_general(
            read(refs, view, size), hot, NT, preferred_element_type=jnp.float32
        )
        total = part if total is None else total + part
    return total


def spread_columns(pivots, first, tiles, size, count, onto=None):
    operands = Operands()
    views = [operands.add(view) for view in tiles]
    extra = [] if onto is None else [onto]

    def kernel(q_ref, *refs):
        out = refs[-1]

        @pl.loop(0, count)
        def _(n):
            here = pl.ds(pl.multiple_of(n * size, size), size)
            moved = spread(refs[len(extra) :], views, q_ref, first, size, n).astype(out.dtype)
            out[:, here] = moved if onto is None else moved + refs[0][:, here]

    return pl.pallas_call(
        kernel,
        out_shape=jax.ShapeDtypeStruct((size, size * count), jnp.bfloat16),
        compiler_params=pltpu.CompilerParams(vmem_limit_bytes=VMEM),
        cost_estimate=pl.CostEstimate(
            flops=4 * size * size * size * count, bytes_accessed=12 * size * size, transcendentals=0
        ),
    )(pivots, *extra, *operands.arrays)


def product(left, right, added, form, size, share=None, turn=0):
    count = left.shape[1] // size
    operands = Operands()
    views = [[operands.add(view) for view in half] for half in right]
    tall, wide = size + EXTRA, 2 * size
    shapes = {
        "joint": [(tall, wide)],
        "both": [(tall, wide), (tall, size), (size, size)],
        "split": [(size, size), (size, size)],
    }[form]
    outs = [jax.ShapeDtypeStruct(shape, jnp.bfloat16) for shape in shapes]
    outs.append(jax.ShapeDtypeStruct((EXTRA, size), jnp.float32))

    def kernel(left_ref, added_ref, *rest):
        refs = rest[: len(operands.arrays)]
        results = rest[len(refs) :]

        for half in range(2):
            total = None
            for b in range(count):
                part = jnp.dot(
                    left_ref[:, b * size : (b + 1) * size],
                    read(refs, views[half][b], size),
                    preferred_element_type=jnp.float32,
                )
                total = part if total is None else total + part
            total = total.astype(jnp.bfloat16)
            if form != "split":
                results[0][0:size, half * size : (half + 1) * size] = total
            if form != "joint":
                results[half + len(results) - 3][0:size, :] = total

        def pieces(b, k):
            here = slice(k * share, (k + 1) * share)
            own, end = (read(refs, views[half][b], size, slice(size, tall))[:, here] for half in (0, 1))
            return jnp.concatenate([end, own, own, end], axis=1) * added_ref[...]

        applied = added_ref[...] if share is None else pieces(0, turn + 1).astype(jnp.float32)
        for b in range(count):
            if share is None:
                rows = read(refs, views[0][b], size, slice(size, tall))
            else:
                rows = pieces(b, turn)
            applied = applied + lax.dot_general(
                rows, left_ref[:, b * size : (b + 1) * size], NT, preferred_element_type=jnp.float32
            )
        results[-1][...] = applied
        if form != "split":
            results[0][size:tall, 0:size] = applied.astype(jnp.bfloat16)
            results[0][size:tall, size:wide] = applied.astype(jnp.bfloat16)
        if form == "both":
            results[1][size:tall, :] = applied.astype(jnp.bfloat16)

    return pl.pallas_call(
        kernel,
        out_shape=tuple(outs),
        compiler_params=pltpu.CompilerParams(vmem_limit_bytes=VMEM),
        cost_estimate=pl.CostEstimate(
            flops=4 * size * size * size * count, bytes_accessed=24 * size * size, transcendentals=0
        ),
    )(left, added, *operands.arrays)


def after(value, *others):
    return lax.optimization_barrier((value, *others))[0]


def shards(interval_blocks, interval_pivots, boundary_pivots, interval_residuals):
    blocks = interval_blocks[0]
    size, share = blocks.shape[1], interval_residuals.shape[2]
    row, col = lax.axis_index("row"), lax.axis_index("col")
    count = lax.axis_size("row")
    position = lax.axis_index("loop")
    positions = lax.axis_size("loop")

    lefts = blocks[1::2]
    riding = jnp.broadcast_to(interval_residuals[0].reshape(1, -1), (EXTRA, size))
    tiles = [jnp.concatenate([blocks[k], riding], axis=0) for k in (0, 2)]
    rights = jnp.stack(tiles)
    ends_left = inward(lefts)
    lefts_other = swap_middle(lefts)
    rights_across = swap_rows(rights, 2)
    ends_right = {2: inward(tiles[1])}
    ends_right[0] = inward(tiles[0])
    rights_beside = swap_rows(rights, 1)

    own = lax.dynamic_index_in_dim(boundary_pivots, position, 0, keepdims=True)
    back = lax.dynamic_index_in_dim(
        boundary_pivots, (position + positions - 1) % positions, 0, keepdims=True
    )
    pivots = jnp.concatenate([interval_pivots[0], own, back], axis=0)
    pivots = (((pivots // size) ^ row) * size + pivots % size).reshape(pivots.shape[0], count, size)
    order = [
        lax.dynamic_index_in_dim(pivots, col ^ flip, 1, keepdims=True) for flip in (0, 1, 3, 2)
    ]
    pivots = jnp.concatenate(order, axis=1)
    places = lax.broadcasted_iota(jnp.int32, (EXTRA, size), 1)
    held = ((places < 2 * share) == (col == 1)).astype(jnp.bfloat16)

    ends_other = swap_middle(ends_left)
    rights_last = swap_rows(rights_across, 1)

    def panel(turn, k):
        own_tiles = [(lefts, k, 0), (ends_left, k, 0)]
        other_tiles = [(lefts_other, k, 0), (ends_other, k, 0)]
        partial = spread_columns(pivots[turn], 0, own_tiles, size, count)
        return spread_columns(pivots[turn], 2, other_tiles, size, count, partial)

    def first(turn, k, left):
        end = ends_right[turn]
        across = swap_rows(end, 2)
        ends = [end, swap_rows(end, 1), across, swap_rows(across, 1)]
        right = [
            [(tile, k, 0) for tile in (rights, rights_beside, rights_across, rights_last)],
            [(tile, None, 0) for tile in ends],
        ]
        return product(left, right, held, "joint", size, share, turn)

    upper, upper_vector = first(2, 1, panel(2, 1))
    lower, _ = first(0, 0, panel(0, 0))

    def later(turn, left, added, right, form):
        other = swap_middle(left)
        partial = spread_columns(pivots[turn], 0, [(left, None, 0), (left, None, size)], size, count)
        parts = []
        for tile in right:
            beside, across = swap_rows(tile, 1), swap_rows(tile, 2)
            parts.append([tile, beside, across, swap_rows(after(across, partial), 1)])
        if len(parts) == 1:
            views = [[(tile, None, column) for tile in parts[0]] for column in (0, size)]
        else:
            views = [[(tile, None, 0) for tile in part] for part in parts]
        other_tiles = [(other, None, 0), (other, None, size)]
        moved = spread_columns(pivots[turn], 2, other_tiles, size, count, partial)
        return product(moved, views, added, form, size)

    whole, whole_o, whole_e, whole_vector = later(1, upper, upper_vector, [lower], "both")
    earlier = [from_behind(tile, "loop", 1) for tile in (whole_o, whole_e)]
    halved, halved_vector = later(3, whole, whole_vector, earlier, "joint")
    distant = from_behind(halved, "loop", 2)
    reduced_o, reduced_e, applied = later(4, halved, halved_vector, [distant], "split")

    middle = (col == 1) | (col == 2)
    block = jnp.where(middle, reduced_o, outward(reduced_e))
    vector = applied[:1]
    vector = vector + swap_middle(vector)
    vector = jnp.where(middle, vector, outward(vector))
    return (block[None], lax.dynamic_slice_in_dim(vector, col * share, share, 1))


def solution(mesh):
    placed = (
        P("loop", None, "row", "col"),
        P("loop", None, None),
        P(),
        P("loop", None, ("row", "col")),
    )
    return jax.shard_map(
        shards,
        mesh=mesh,
        in_specs=placed,
        out_specs=(P("loop", "row", "col"), P("loop", ("row", "col"))),
        check_vma=False,
    )
```

```python
import jax
import jax.numpy as jnp
from jax import lax
from jax.experimental import pallas as pl
from jax.experimental.pallas import tpu as pltpu
from jax.sharding import PartitionSpec as P

EXTRA = 16
VMEM = 24 * 1024 * 1024
LIGHT = pl.CostEstimate(flops=1, bytes_accessed=1, transcendentals=0)
NT = (((1,), (1,)), ((), ()))


def from_behind(value, axis, by):
    devices = lax.axis_size(axis)
    if by % devices == 0:
        return value
    return lax.ppermute(value, axis, [(i, (i + by) % devices) for i in range(devices)])


def swap_rows(value, flip):
    rows, cols = lax.axis_size("row"), lax.axis_size("col")
    pairs = [(r * cols + c, (r ^ flip) * cols + c) for r in range(rows) for c in (1, 2)]
    return lax.ppermute(value, ("row", "col"), pairs)


def swap_middle(value):
    return lax.ppermute(value, "col", [(1, 2), (2, 1)])


def inward(value):
    return lax.ppermute(value, "col", [(0, 1), (3, 2)])


def outward(value):
    return lax.ppermute(value, "col", [(1, 0), (2, 3)])


class Operands:
    def __init__(self):
        self.arrays = []

    def add(self, view):
        array, lead, column = view
        for i, known in enumerate(self.arrays):
            if known is array:
                return i, lead, column
        self.arrays.append(array)
        return len(self.arrays) - 1, lead, column


def read(refs, view, size, rows=None):
    which, lead, column = view
    ref = refs[which] if lead is None else refs[which].at[lead]
    return ref[rows or slice(0, size), column : column + size]


def spread(refs, views, q_ref, size, n):
    total = None
    for (block, _), view in views:
        at = lax.broadcasted_iota(jnp.int32, (size, size), 0) + n * size
        hot = jnp.where(at == q_ref[block : block + 1, :], 1.0, 0.0).astype(jnp.bfloat16)
        part = lax.dot_general(
            read(refs, view, size), hot, NT, preferred_element_type=jnp.float32
        )
        total = part if total is None else total + part
    return total


def spread_columns(pivots, tiles, size, count, onto=None):
    operands = Operands()
    views = [((block, None), operands.add(view)) for block, view in tiles]
    extra = [] if onto is None else [onto]

    def kernel(q_ref, *refs):
        out = refs[-1]

        @pl.loop(0, count)
        def _(n):
            here = pl.ds(pl.multiple_of(n * size, size), size)
            moved = spread(refs[len(extra) :], views, q_ref, size, n).astype(out.dtype)
            out[:, here] = moved if onto is None else moved + refs[0][:, here]

    return pl.pallas_call(
        kernel,
        out_shape=jax.ShapeDtypeStruct((size, size * count), jnp.bfloat16),
        compiler_params=pltpu.CompilerParams(vmem_limit_bytes=VMEM),
        cost_estimate=pl.CostEstimate(
            flops=2 * len(tiles) * size * size * size * count,
            bytes_accessed=8 * size * size,
            transcendentals=0,
        ),
    )(pivots, *extra, *operands.arrays)


def product(left, right, size, vector=None, held=None, turn=0):
    count = left.shape[1] // size
    operands = Operands()
    views = [operands.add(view) for view in right]
    tall = size if vector is None else size + EXTRA
    outs = [jax.ShapeDtypeStruct((tall, size), jnp.bfloat16)]
    extra = []
    if held is not None:
        own_views = [operands.add(view) for view in vector]
        share = size // 4
        extra = [held]
    elif vector is not None:
        extra = [vector]
    if vector is not None:
        outs.append(jax.ShapeDtypeStruct((EXTRA, size), jnp.float32))

    def kernel(left_ref, *rest):
        extra_refs = rest[: len(extra)]
        refs = rest[len(extra) : len(extra) + len(operands.arrays)]
        results = rest[len(extra) + len(refs) :]

        total = None
        for b in range(count):
            part = jnp.dot(
                left_ref[:, b * size : (b + 1) * size],
                read(refs, views[b], size),
                preferred_element_type=jnp.float32,
            )
            total = part if total is None else total + part
        results[0][0:size, :] = total.astype(jnp.bfloat16)
        if vector is None:
            return

        def pieces(b, k):
            here = slice(k * share, (k + 1) * share)
            own, end = (
                read(refs, kind[b], size, slice(size, tall))[:, here] for kind in (own_views, views)
            )
            return jnp.concatenate([end, own, own, end], axis=1) * extra_refs[0][...]

        applied = extra_refs[0][...] if held is None else pieces(0, turn + 1).astype(jnp.float32)
        for b in range(count):
            if held is None:
                rows = read(refs, views[b], size, slice(size, tall))
            else:
                rows = pieces(b, turn)
            applied = applied + lax.dot_general(
                rows, left_ref[:, b * size : (b + 1) * size], NT, preferred_element_type=jnp.float32
            )
        results[1][...] = applied
        results[0][size:tall, :] = applied.astype(jnp.bfloat16)

    found = pl.pallas_call(
        kernel,
        out_shape=tuple(outs),
        compiler_params=pltpu.CompilerParams(vmem_limit_bytes=VMEM),
        cost_estimate=LIGHT,
    )(left, *extra, *operands.arrays)
    return found[0] if vector is None else found


def after(value, *others):
    return lax.optimization_barrier((value, *others))[0]


def plain(*tiles):
    return [(tile, None, 0) for tile in tiles]


def shards(interval_blocks, interval_pivots, boundary_pivots, interval_residuals):
    blocks = interval_blocks[0]
    size, share = blocks.shape[1], interval_residuals.shape[2]
    row, col = lax.axis_index("row"), lax.axis_index("col")
    count = lax.axis_size("row")
    position = lax.axis_index("loop")
    positions = lax.axis_size("loop")

    lefts = blocks[1::2]
    riding = jnp.broadcast_to(interval_residuals[0].reshape(1, -1), (EXTRA, size))
    tiles = [jnp.concatenate([blocks[k], riding], axis=0) for k in (0, 2)]
    rights = jnp.stack(tiles)
    ends_left = inward(lefts)
    lefts_other = swap_middle(lefts)
    rights_across = swap_rows(rights, 2)
    end_upper = inward(tiles[1])
    rights_beside = swap_rows(rights, 1)

    own = lax.dynamic_index_in_dim(boundary_pivots, position, 0, keepdims=True)
    back = lax.dynamic_index_in_dim(
        boundary_pivots, (position + positions - 1) % positions, 0, keepdims=True
    )
    pivots = jnp.concatenate([interval_pivots[0], own, back], axis=0)
    pivots = (((pivots // size) ^ row) * size + pivots % size).reshape(pivots.shape[0], count, size)
    order = [
        lax.dynamic_index_in_dim(pivots, col ^ flip, 1, keepdims=True) for flip in (0, 1, 3, 2)
    ]
    pivots = jnp.concatenate(order, axis=1)
    places = lax.broadcasted_iota(jnp.int32, (EXTRA, size), 1)
    held = ((places < 2 * share) == (col == 1)).astype(jnp.bfloat16)

    def tile_row(tile, across):
        return [tile, swap_rows(tile, 1), across, swap_rows(across, 1)]

    own_panels = [spread_columns(pivots[t], [(0, (lefts, k, 0))], size, count) for t, k in ((0, 0), (2, 1))]
    end_lower = inward(after(tiles[0], own_panels[1]))
    ends_far = [swap_middle(ends_left[k]) for k in (1, 0)][::-1]
    rights_last = swap_rows(rights_across, 1)
    panels = [
        spread_columns(
            pivots[t], [(1, (ends_left, k, 0)), (2, (lefts_other, k, 0))], size, count, own_panels[k]
        )
        for t, k in ((0, 0), (2, 1))
    ]
    end_upper = after(end_upper, *panels)
    upper_across = swap_rows(end_upper, 2)

    def own_tiles(k):
        return [(tile, k, 0) for tile in (rights, rights_beside, rights_across, rights_last)]

    panel = spread_columns(pivots[2], [(3, (ends_far[1], None, 0))], size, count, panels[1])
    upper_o = product(panel, own_tiles(1), size)
    lower_panel = after(panels[0], upper_o)
    lower_panel = spread_columns(pivots[0], [(3, (ends_far[0], None, 0))], size, count, lower_panel)
    lower_o = product(lower_panel, own_tiles(0), size)
    end_lower = after(end_lower, lower_panel)
    lower_across = swap_rows(end_lower, 2)
    upper_ends = plain(*tile_row(end_upper, upper_across))
    upper_e, vector = product(after(panel, lower_o), upper_ends, size, own_tiles(1), held, 2)
    lower_ends = plain(*tile_row(end_lower, lower_across))
    lower_e, _ = product(after(lower_panel, upper_e), lower_ends, size, own_tiles(0), held, 0)

    def stage(turn, left_o, left_e, added, right_o, right_e):
        other_o = swap_middle(left_o)
        across_o = swap_rows(right_o, 2)
        other_e = swap_middle(left_e)
        across_e = swap_rows(right_e, 2)
        panel = spread_columns(pivots[turn], [(0, (left_o, None, 0))], size, count)
        panel = spread_columns(
            pivots[turn], [(1, (left_e, None, 0)), (2, (other_o, None, 0))], size, count, panel
        )
        panel = spread_columns(pivots[turn], [(3, (other_e, None, 0))], size, count, panel)
        product_o = product(panel, plain(*tile_row(right_o, across_o)), size)
        panel = after(panel, product_o)
        product_e, vector = product(panel, plain(*tile_row(right_e, across_e)), size, added)
        return product_o, product_e, vector

    whole_o, whole_e, vector = stage(1, upper_o, upper_e, vector, lower_o, lower_e)
    earlier_o, earlier_e = from_behind(whole_o, "loop", 1), from_behind(whole_e, "loop", 1)
    halved_o, halved_e, vector = stage(3, whole_o, whole_e, vector, earlier_o, earlier_e)
    distant_o, distant_e = from_behind(halved_o, "loop", 2), from_behind(halved_e, "loop", 2)
    reduced_o, reduced_e, vector = stage(4, halved_o, halved_e, vector, distant_o, distant_e)

    middle = (col == 1) | (col == 2)
    block = jnp.where(middle, reduced_o, outward(reduced_e)[:size])
    vector = vector[:1]
    vector = vector + swap_middle(vector)
    vector = jnp.where(middle, vector, outward(vector))
    return (block[None], lax.dynamic_slice_in_dim(vector, col * share, share, 1))


def solution(mesh):
    placed = (
        P("loop", None, "row", "col"),
        P("loop", None, None),
        P(),
        P("loop", None, ("row", "col")),
    )
    return jax.shard_map(
        shards,
        mesh=mesh,
        in_specs=placed,
        out_specs=(P("loop", "row", "col"), P("loop", ("row", "col"))),
        check_vma=False,
    )
```

```python
import jax
import jax.numpy as jnp
from jax import lax
from jax.experimental import pallas as pl
from jax.experimental.pallas import tpu as pltpu
from jax.sharding import PartitionSpec as P

EXTRA = 16
VMEM = 24 * 1024 * 1024
NT = (((1,), (1,)), ((), ()))


def from_behind(value, axis, by):
    devices = lax.axis_size(axis)
    if by % devices == 0:
        return value
    return lax.ppermute(value, axis, [(i, (i + by) % devices) for i in range(devices)])


def swap_rows(value, flip):
    rows, cols = lax.axis_size("row"), lax.axis_size("col")
    pairs = [(r * cols + c, (r ^ flip) * cols + c) for r in range(rows) for c in (1, 2)]
    return lax.ppermute(value, ("row", "col"), pairs)


def swap_middle(value):
    return lax.ppermute(value, "col", [(1, 2), (2, 1)])


def inward(value):
    return lax.ppermute(value, "col", [(0, 1), (3, 2)])


def outward(value):
    return lax.ppermute(value, "col", [(1, 0), (2, 3)])


class Operands:
    def __init__(self):
        self.arrays = []

    def add(self, view):
        array, lead, column = view
        for i, known in enumerate(self.arrays):
            if known is array:
                return i, lead, column
        self.arrays.append(array)
        return len(self.arrays) - 1, lead, column


def read(refs, view, size, rows=None):
    which, lead, column = view
    ref = refs[which] if lead is None else refs[which].at[lead]
    return ref[rows or slice(0, size), column : column + size]


def spread(refs, views, q_ref, size, n):
    total = None
    for block, view in views:
        at = lax.broadcasted_iota(jnp.int32, (size, size), 0) + n * size
        hot = jnp.where(at == q_ref[block : block + 1, :], 1.0, 0.0).astype(jnp.bfloat16)
        part = lax.dot_general(
            read(refs, view, size), hot, NT, preferred_element_type=jnp.float32
        )
        total = part if total is None else total + part
    return total


def spread_columns(pivots, tiles, size, count, onto=None):
    operands = Operands()
    views = [(block, operands.add(view)) for block, view in tiles]
    extra = [] if onto is None else [onto]

    def kernel(q_ref, *refs):
        out = refs[-1]

        @pl.loop(0, count)
        def _(n):
            here = pl.ds(pl.multiple_of(n * size, size), size)
            moved = spread(refs[len(extra) :], views, q_ref, size, n).astype(out.dtype)
            out[:, here] = moved if onto is None else moved + refs[0][:, here]

    return pl.pallas_call(
        kernel,
        out_shape=jax.ShapeDtypeStruct((size, size * count), jnp.bfloat16),
        compiler_params=pltpu.CompilerParams(vmem_limit_bytes=VMEM),
        cost_estimate=pl.CostEstimate(
            flops=2 * len(tiles) * size * size * size * count,
            bytes_accessed=8 * size * size,
            transcendentals=0,
        ),
    )(pivots, *extra, *operands.arrays)


def product(left, right, added, form, size, share=None, turn=0):
    count = left.shape[1] // size
    operands = Operands()
    views = [[operands.add(view) for view in half] for half in right]
    tall, wide = size + EXTRA, 2 * size
    shapes = {
        "joint": [(tall, wide)],
        "both": [(tall, wide), (tall, size), (size, size)],
        "split": [(size, size), (size, size)],
    }[form]
    outs = [jax.ShapeDtypeStruct(shape, jnp.bfloat16) for shape in shapes]
    outs.append(jax.ShapeDtypeStruct((EXTRA, size), jnp.float32))

    def kernel(left_ref, added_ref, *rest):
        refs = rest[: len(operands.arrays)]
        results = rest[len(refs) :]

        for half in range(2):
            total = None
            for b in range(count):
                part = jnp.dot(
                    left_ref[:, b * size : (b + 1) * size],
                    read(refs, views[half][b], size),
                    preferred_element_type=jnp.float32,
                )
                total = part if total is None else total + part
            total = total.astype(jnp.bfloat16)
            if form != "split":
                results[0][0:size, half * size : (half + 1) * size] = total
            if form != "joint":
                results[half + len(results) - 3][0:size, :] = total

        def pieces(b, k):
            here = slice(k * share, (k + 1) * share)
            own, end = (read(refs, views[half][b], size, slice(size, tall))[:, here] for half in (0, 1))
            return jnp.concatenate([end, own, own, end], axis=1) * added_ref[...]

        applied = added_ref[...] if share is None else pieces(0, turn + 1).astype(jnp.float32)
        for b in range(count):
            if share is None:
                rows = read(refs, views[0][b], size, slice(size, tall))
            else:
                rows = pieces(b, turn)
            applied = applied + lax.dot_general(
                rows, left_ref[:, b * size : (b + 1) * size], NT, preferred_element_type=jnp.float32
            )
        results[-1][...] = applied
        if form != "split":
            results[0][size:tall, 0:size] = applied.astype(jnp.bfloat16)
            results[0][size:tall, size:wide] = applied.astype(jnp.bfloat16)
        if form == "both":
            results[1][size:tall, :] = applied.astype(jnp.bfloat16)

    return pl.pallas_call(
        kernel,
        out_shape=tuple(outs),
        compiler_params=pltpu.CompilerParams(vmem_limit_bytes=VMEM),
        cost_estimate=pl.CostEstimate(
            flops=4 * size * size * size * count, bytes_accessed=24 * size * size, transcendentals=0
        ),
    )(left, added, *operands.arrays)


def after(value, *others):
    return lax.optimization_barrier((value, *others))[0]


def shards(interval_blocks, interval_pivots, boundary_pivots, interval_residuals):
    blocks = interval_blocks[0]
    size, share = blocks.shape[1], interval_residuals.shape[2]
    row, col = lax.axis_index("row"), lax.axis_index("col")
    count = lax.axis_size("row")
    position = lax.axis_index("loop")
    positions = lax.axis_size("loop")

    lefts = blocks[1::2]
    riding = jnp.broadcast_to(interval_residuals[0].reshape(1, -1), (EXTRA, size))
    tiles = [jnp.concatenate([blocks[k], riding], axis=0) for k in (0, 2)]
    rights = jnp.stack(tiles)
    ends_left = inward(lefts)
    lefts_other = swap_middle(lefts)
    rights_across = swap_rows(rights, 2)
    end_upper, end_lower = inward(tiles[1]), inward(tiles[0])
    rights_beside = swap_rows(rights, 1)

    own = lax.dynamic_index_in_dim(boundary_pivots, position, 0, keepdims=True)
    back = lax.dynamic_index_in_dim(
        boundary_pivots, (position + positions - 1) % positions, 0, keepdims=True
    )
    pivots = jnp.concatenate([interval_pivots[0], own, back], axis=0)
    pivots = (((pivots // size) ^ row) * size + pivots % size).reshape(pivots.shape[0], count, size)
    order = [
        lax.dynamic_index_in_dim(pivots, col ^ flip, 1, keepdims=True) for flip in (0, 1, 3, 2)
    ]
    pivots = jnp.concatenate(order, axis=1)
    places = lax.broadcasted_iota(jnp.int32, (EXTRA, size), 1)
    held = ((places < 2 * share) == (col == 1)).astype(jnp.bfloat16)

    def panel(turn, tiles, onto=None):
        return spread_columns(pivots[turn], tiles, size, count, onto)

    ends_other = swap_middle(ends_left)
    rights_last = swap_rows(rights_across, 1)
    upper_panel, lower_panel = panel(2, [(0, (lefts, 1, 0))]), panel(0, [(0, (lefts, 0, 0))])
    upper_panel = panel(2, [(1, (ends_left, 1, 0)), (2, (lefts_other, 1, 0))], upper_panel)
    end_upper = after(end_upper, upper_panel)
    upper_across = swap_rows(end_upper, 2)
    lower_panel = panel(0, [(1, (ends_left, 0, 0)), (2, (lefts_other, 0, 0))], lower_panel)
    end_lower = after(end_lower, lower_panel)
    lower_across = swap_rows(end_lower, 2)
    upper_panel = panel(2, [(3, (ends_other, 1, 0))], upper_panel)
    lower_panel = panel(0, [(3, (ends_other, 0, 0))], lower_panel)

    def first(turn, k, left, end, across):
        ends = [end, swap_rows(end, 1), across, swap_rows(across, 1)]
        right = [
            [(tile, k, 0) for tile in (rights, rights_beside, rights_across, rights_last)],
            [(tile, None, 0) for tile in ends],
        ]
        return product(left, right, held, "joint", size, share, turn)

    upper, upper_vector = first(2, 1, upper_panel, end_upper, upper_across)
    lower, _ = first(0, 0, lower_panel, end_lower, after(lower_across, upper))

    def later(turn, left, added, right, form):
        other = swap_middle(left)
        partial = panel(turn, [(0, (left, None, 0)), (1, (left, None, size))])
        parts = []
        for tile in right:
            beside, across = swap_rows(tile, 1), swap_rows(tile, 2)
            parts.append([tile, beside, across, swap_rows(after(across, partial), 1)])
        if len(parts) == 1:
            views = [[(tile, None, column) for tile in parts[0]] for column in (0, size)]
        else:
            views = [[(tile, None, 0) for tile in part] for part in parts]
        moved = panel(turn, [(2, (other, None, 0)), (3, (other, None, size))], partial)
        return product(moved, views, added, form, size)

    whole, whole_o, whole_e, whole_vector = later(1, upper, upper_vector, [lower], "both")
    earlier = [from_behind(tile, "loop", 1) for tile in (whole_o, whole_e)]
    halved, halved_vector = later(3, whole, whole_vector, earlier, "joint")
    distant = from_behind(halved, "loop", 2)
    reduced_o, reduced_e, applied = later(4, halved, halved_vector, [distant], "split")

    middle = (col == 1) | (col == 2)
    block = jnp.where(middle, reduced_o, outward(reduced_e))
    vector = applied[:1]
    vector = vector + swap_middle(vector)
    vector = jnp.where(middle, vector, outward(vector))
    return (block[None], lax.dynamic_slice_in_dim(vector, col * share, share, 1))


def solution(mesh):
    placed = (
        P("loop", None, "row", "col"),
        P("loop", None, None),
        P(),
        P("loop", None, ("row", "col")),
    )
    return jax.shard_map(
        shards,
        mesh=mesh,
        in_specs=placed,
        out_specs=(P("loop", "row", "col"), P("loop", ("row", "col"))),
        check_vma=False,
    )
```

```python
import jax
import jax.numpy as jnp
from jax import lax
from jax.experimental import pallas as pl
from jax.experimental.pallas import tpu as pltpu
from jax.sharding import PartitionSpec as P

EXTRA = 16
VMEM = 14 * 1024 * 1024
NT = (((1,), (1,)), ((), ()))


def from_behind(value, axis, by):
    devices = lax.axis_size(axis)
    if by % devices == 0:
        return value
    return lax.ppermute(value, axis, [(i, (i + by) % devices) for i in range(devices)])


def swap_rows(value, flip):
    rows, cols = lax.axis_size("row"), lax.axis_size("col")
    pairs = [(r * cols + c, (r ^ flip) * cols + c) for r in range(rows) for c in (1, 2)]
    return lax.ppermute(value, ("row", "col"), pairs)


def swap_middle(value):
    return lax.ppermute(value, "col", [(1, 2), (2, 1)])


def inward(value):
    return lax.ppermute(value, "col", [(0, 1), (3, 2)])


def outward(value):
    return lax.ppermute(value, "col", [(1, 0), (2, 3)])


class Operands:
    def __init__(self):
        self.arrays = []

    def add(self, view):
        array, lead, column = view
        for i, known in enumerate(self.arrays):
            if known is array:
                return i, lead, column
        self.arrays.append(array)
        return len(self.arrays) - 1, lead, column


def read(refs, view, size, rows=None):
    which, lead, column = view
    ref = refs[which] if lead is None else refs[which].at[lead]
    return ref[rows or slice(0, size), column : column + size]


def spread(refs, views, q_ref, size, n):
    total = None
    for block, view in views:
        at = lax.broadcasted_iota(jnp.int32, (size, size), 0) + n * size
        hot = jnp.where(at == q_ref[block : block + 1, :], 1.0, 0.0).astype(jnp.bfloat16)
        part = lax.dot_general(
            read(refs, view, size), hot, NT, preferred_element_type=jnp.float32
        )
        total = part if total is None else total + part
    return total


def spread_columns(pivots, tiles, size, count, onto=None):
    operands = Operands()
    views = [(block, operands.add(view)) for block, view in tiles]
    extra = [] if onto is None else [onto]

    def kernel(q_ref, *refs):
        out = refs[-1]

        @pl.loop(0, count)
        def _(n):
            here = pl.ds(pl.multiple_of(n * size, size), size)
            moved = spread(refs[len(extra) :], views, q_ref, size, n).astype(out.dtype)
            out[:, here] = moved if onto is None else moved + refs[0][:, here]

    return pl.pallas_call(
        kernel,
        out_shape=jax.ShapeDtypeStruct((size, size * count), jnp.bfloat16),
        compiler_params=pltpu.CompilerParams(vmem_limit_bytes=VMEM),
        cost_estimate=pl.CostEstimate(
            flops=2 * len(tiles) * size * size * size * count,
            bytes_accessed=8 * size * size,
            transcendentals=0,
        ),
    )(pivots, *extra, *operands.arrays)


def product(left, halves, form, size, added=None, own=None, turn=0):
    count = left.shape[1] // size
    operands = Operands()
    views = [[operands.add(view) for view in half] for half in halves]
    own_views = [operands.add(view) for view in own or []]
    extra = [] if added is None else [added]
    tall, wide = size + (EXTRA if extra else 0), size * len(halves)
    shapes = [] if form == "apart" else [(tall, wide)]
    if form != "joint":
        shapes += [(size, size)] * (len(halves) - 1) + [(tall, size)]
    outs = [jax.ShapeDtypeStruct(shape, jnp.bfloat16) for shape in shapes]
    if extra:
        outs.append(jax.ShapeDtypeStruct((EXTRA, size), jnp.float32))

    def kernel(left_ref, *rest):
        refs = rest[len(extra) : len(extra) + len(operands.arrays)]
        results = rest[len(extra) + len(refs) :]
        joint = None if form == "apart" else results[0]
        single = [] if form == "joint" else results[len(shapes) - len(halves) : len(shapes)]

        for i, half in enumerate(views):
            total = None
            for b in range(count):
                part = jnp.dot(
                    left_ref[:, b * size : (b + 1) * size],
                    read(refs, half[b], size),
                    preferred_element_type=jnp.float32,
                )
                total = part if total is None else total + part
            total = total.astype(jnp.bfloat16)
            if joint is not None:
                joint[0:size, i * size : (i + 1) * size] = total
            if single:
                single[i][0:size, :] = total
        if not extra:
            return

        def pieces(b, k):
            here = slice(k * (size // 4), (k + 1) * (size // 4))
            near, end = (
                read(refs, kind[b], size, slice(size, tall))[:, here] for kind in (own_views, views[-1])
            )
            return jnp.concatenate([end, near, near, end], axis=1) * rest[0][...]

        applied = rest[0][...] if own is None else pieces(0, turn + 1).astype(jnp.float32)
        for b in range(count):
            if own is None:
                rows = read(refs, views[-1][b], size, slice(size, tall))
            else:
                rows = pieces(b, turn)
            applied = applied + lax.dot_general(
                rows, left_ref[:, b * size : (b + 1) * size], NT, preferred_element_type=jnp.float32
            )
        results[-1][...] = applied
        applied = applied.astype(jnp.bfloat16)
        if joint is not None:
            for i in range(len(halves)):
                joint[size:tall, i * size : (i + 1) * size] = applied
        if single:
            single[-1][size:tall, :] = applied

    return pl.pallas_call(
        kernel,
        out_shape=tuple(outs),
        compiler_params=pltpu.CompilerParams(vmem_limit_bytes=VMEM),
        cost_estimate=pl.CostEstimate(
            flops=2 * len(halves) * size * size * size * count,
            bytes_accessed=12 * len(halves) * size * size,
            transcendentals=0,
        ),
    )(left, *extra, *operands.arrays)


def after(value, *others):
    return lax.optimization_barrier((value, *others))[0]


def plain(*tiles):
    return [(tile, None, 0) for tile in tiles]


def shards(interval_blocks, interval_pivots, boundary_pivots, interval_residuals):
    blocks = interval_blocks[0]
    size, share = blocks.shape[1], interval_residuals.shape[2]
    row, col = lax.axis_index("row"), lax.axis_index("col")
    count = lax.axis_size("row")
    position = lax.axis_index("loop")
    positions = lax.axis_size("loop")

    lefts = blocks[1::2]
    riding = jnp.broadcast_to(interval_residuals[0].reshape(1, -1), (EXTRA, size))
    tiles = [jnp.concatenate([blocks[k], riding], axis=0) for k in (0, 2)]
    rights = jnp.stack(tiles)
    ends_left = inward(lefts)
    lefts_other = swap_middle(lefts)
    rights_across = swap_rows(rights, 2)
    end_lower = inward(tiles[0])
    end_upper = inward(tiles[1])
    rights_beside = swap_rows(rights, 1)

    own = lax.dynamic_index_in_dim(boundary_pivots, position, 0, keepdims=True)
    back = lax.dynamic_index_in_dim(
        boundary_pivots, (position + positions - 1) % positions, 0, keepdims=True
    )
    pivots = jnp.concatenate([interval_pivots[0], own, back], axis=0)
    pivots = (((pivots // size) ^ row) * size + pivots % size).reshape(pivots.shape[0], count, size)
    order = [
        lax.dynamic_index_in_dim(pivots, col ^ flip, 1, keepdims=True) for flip in (0, 1, 3, 2)
    ]
    pivots = jnp.concatenate(order, axis=1)
    places = lax.broadcasted_iota(jnp.int32, (EXTRA, size), 1)
    held = ((places < 2 * share) == (col == 1)).astype(jnp.bfloat16)

    def panel(turn, tiles, onto=None):
        return spread_columns(pivots[turn], tiles, size, count, onto)

    upper_panel, lower_panel = panel(2, [(0, (lefts, 1, 0))]), panel(0, [(0, (lefts, 0, 0))])
    ends_other = swap_middle(after(ends_left, upper_panel, lower_panel))
    rights_last = swap_rows(rights_across, 1)
    lower_panel = panel(0, [(1, (ends_left, 0, 0)), (2, (lefts_other, 0, 0))], lower_panel)
    upper_panel = panel(2, [(1, (ends_left, 1, 0)), (2, (lefts_other, 1, 0))], upper_panel)
    end_lower = after(end_lower, lower_panel, upper_panel)
    lower_across = swap_rows(end_lower, 2)
    lower_ends = [end_lower, swap_rows(end_lower, 1), lower_across, swap_rows(lower_across, 1)]
    upper_across = swap_rows(end_upper, 2)
    upper_ends = [end_upper, swap_rows(end_upper, 1), upper_across]
    lower_panel = panel(0, [(3, (ends_other, 0, 0))], lower_panel)
    upper_panel = panel(2, [(3, (ends_other, 1, 0))], upper_panel)

    def own_tiles(k):
        return [(tile, k, 0) for tile in (rights, rights_beside, rights_across, rights_last)]

    lower, _ = product(
        lower_panel, [own_tiles(0), plain(*lower_ends)], "joint", size, held, own_tiles(0), 0
    )
    upper_panel = after(upper_panel, lower)
    (upper_o,) = product(upper_panel, [own_tiles(1)], "apart", size)
    upper_ends.append(swap_rows(after(upper_across, upper_o), 1))
    upper_e, vector = product(
        upper_panel, [plain(*upper_ends)], "apart", size, held, own_tiles(1), 2
    )

    def right_views(right, tie):
        parts = []
        for tile in right:
            beside, across = swap_rows(tile, 1), swap_rows(tile, 2)
            parts.append([tile, beside, across, swap_rows(after(across, *tie), 1)])
        if len(parts) == 1:
            return [[(tile, None, column) for tile in parts[0]] for column in (0, size)]
        return [plain(*part) for part in parts]

    other_o, other_e = swap_middle(upper_o), swap_middle(upper_e)
    moved = panel(1, [(0, (upper_o, None, 0)), (1, (upper_e, None, 0))])
    moved = panel(1, [(2, (other_o, None, 0))], moved)
    views = right_views([lower], (moved, other_e))
    moved = panel(1, [(3, (other_e, None, 0))], moved)
    whole, whole_o, whole_e, vector = product(moved, views, "both", size, vector)

    def left_panel(turn, left):
        other = swap_middle(left)
        partial = panel(turn, [(0, (left, None, 0)), (1, (left, None, size))])
        return partial, panel(turn, [(2, (other, None, 0)), (3, (other, None, size))], partial)

    earlier = [from_behind(tile, "loop", 1) for tile in (whole_o, whole_e)]
    partial, moved = left_panel(3, whole)
    views = right_views(earlier, (partial,))
    halved, vector = product(moved, views, "joint", size, vector)
    partial, moved = left_panel(4, halved)
    views = right_views([from_behind(halved, "loop", 2)], (partial,))
    reduced_e, vector = product(moved, views[1:], "apart", size, vector)
    (reduced_o,) = product(after(moved, reduced_e), views[:1], "apart", size)

    middle = (col == 1) | (col == 2)
    block = jnp.where(middle, reduced_o, outward(reduced_e)[:size])
    vector = vector[:1]
    vector = vector + swap_middle(vector)
    vector = jnp.where(middle, vector, outward(vector))
    return (block[None], lax.dynamic_slice_in_dim(vector, col * share, share, 1))


def solution(mesh):
    placed = (
        P("loop", None, "row", "col"),
        P("loop", None, None),
        P(),
        P("loop", None, ("row", "col")),
    )
    return jax.shard_map(
        shards,
        mesh=mesh,
        in_specs=placed,
        out_specs=(P("loop", "row", "col"), P("loop", ("row", "col"))),
        check_vma=False,
    )
```

```python
import jax
import jax.numpy as jnp
from jax import lax
from jax.experimental import pallas as pl
from jax.experimental.pallas import tpu as pltpu
from jax.sharding import PartitionSpec as P

EXTRA = 16
VMEM = 14 * 1024 * 1024
NT = (((1,), (1,)), ((), ()))


def from_behind(value, axis, by):
    devices = lax.axis_size(axis)
    if by % devices == 0:
        return value
    return lax.ppermute(value, axis, [(i, (i + by) % devices) for i in range(devices)])


def swap_rows(value, flip):
    rows, cols = lax.axis_size("row"), lax.axis_size("col")
    pairs = [(r * cols + c, (r ^ flip) * cols + c) for r in range(rows) for c in (1, 2)]
    return lax.ppermute(value, ("row", "col"), pairs)


def swap_middle(value):
    return lax.ppermute(value, "col", [(1, 2), (2, 1)])


def inward(value):
    return lax.ppermute(value, "col", [(0, 1), (3, 2)])


def outward(value):
    return lax.ppermute(value, "col", [(1, 0), (2, 3)])


class Operands:
    def __init__(self):
        self.arrays = []

    def add(self, view):
        array, lead, column = view
        for i, known in enumerate(self.arrays):
            if known is array:
                return i, lead, column
        self.arrays.append(array)
        return len(self.arrays) - 1, lead, column


def near(arrays):
    return [pltpu.with_memory_space_constraint(array, pltpu.VMEM) for array in arrays]


def read(refs, view, size, rows=None):
    which, lead, column = view
    ref = refs[which] if lead is None else refs[which].at[lead]
    return ref[rows or slice(0, size), column : column + size]


def spread(refs, views, q_ref, size, n):
    total = None
    for block, view in views:
        at = lax.broadcasted_iota(jnp.int32, (size, size), 0) + n * size
        hot = jnp.where(at == q_ref[block : block + 1, :], 1.0, 0.0).astype(jnp.bfloat16)
        part = lax.dot_general(
            read(refs, view, size), hot, NT, preferred_element_type=jnp.float32
        )
        total = part if total is None else total + part
    return total


def spread_columns(pivots, tiles, size, count, onto=None):
    operands = Operands()
    views = [(block, operands.add(view)) for block, view in tiles]
    extra = [] if onto is None else [onto]

    def kernel(q_ref, *refs):
        out = refs[-1]

        @pl.loop(0, count)
        def _(n):
            here = pl.ds(pl.multiple_of(n * size, size), size)
            moved = spread(refs[len(extra) :], views, q_ref, size, n).astype(out.dtype)
            out[:, here] = moved if onto is None else moved + refs[0][:, here]

    return pl.pallas_call(
        kernel,
        out_shape=pltpu.VMEM((size, size * count), jnp.bfloat16),
        compiler_params=pltpu.CompilerParams(vmem_limit_bytes=VMEM),
        cost_estimate=pl.CostEstimate(
            flops=2 * len(tiles) * size * size * size * count,
            bytes_accessed=8 * size * size,
            transcendentals=0,
        ),
    )(pivots, *near(extra), *near(operands.arrays))


def product(left, halves, form, size, added=None, own=None, turn=0):
    count = left.shape[1] // size
    operands = Operands()
    views = [[operands.add(view) for view in half] for half in halves]
    own_views = [operands.add(view) for view in own or []]
    extra = [] if added is None else [added]
    tall, wide = size + (EXTRA if extra else 0), size * len(halves)
    shapes = [] if form == "apart" else [(tall, wide)]
    if form != "joint":
        shapes += [(size, size)] * (len(halves) - 1) + [(tall, size)]
    outs = [pltpu.VMEM(shape, jnp.bfloat16) for shape in shapes]
    if extra:
        outs.append(pltpu.VMEM((EXTRA, size), jnp.float32))

    def kernel(left_ref, *rest):
        refs = rest[len(extra) : len(extra) + len(operands.arrays)]
        results = rest[len(extra) + len(refs) :]
        joint = None if form == "apart" else results[0]
        single = [] if form == "joint" else results[len(shapes) - len(halves) : len(shapes)]

        for i, half in enumerate(views):
            total = None
            for b in range(count):
                part = jnp.dot(
                    left_ref[:, b * size : (b + 1) * size],
                    read(refs, half[b], size),
                    preferred_element_type=jnp.float32,
                )
                total = part if total is None else total + part
            total = total.astype(jnp.bfloat16)
            if joint is not None:
                joint[0:size, i * size : (i + 1) * size] = total
            if single:
                single[i][0:size, :] = total
        if not extra:
            return

        def pieces(b, k):
            here = slice(k * (size // 4), (k + 1) * (size // 4))
            near, end = (
                read(refs, kind[b], size, slice(size, tall))[:, here] for kind in (own_views, views[-1])
            )
            return jnp.concatenate([end, near, near, end], axis=1) * rest[0][...]

        applied = rest[0][...] if own is None else pieces(0, turn + 1).astype(jnp.float32)
        for b in range(count):
            if own is None:
                rows = read(refs, views[-1][b], size, slice(size, tall))
            else:
                rows = pieces(b, turn)
            applied = applied + lax.dot_general(
                rows, left_ref[:, b * size : (b + 1) * size], NT, preferred_element_type=jnp.float32
            )
        results[-1][...] = applied
        applied = applied.astype(jnp.bfloat16)
        if joint is not None:
            for i in range(len(halves)):
                joint[size:tall, i * size : (i + 1) * size] = applied
        if single:
            single[-1][size:tall, :] = applied

    return pl.pallas_call(
        kernel,
        out_shape=tuple(outs),
        compiler_params=pltpu.CompilerParams(vmem_limit_bytes=VMEM),
        cost_estimate=pl.CostEstimate(
            flops=2 * len(halves) * size * size * size * count,
            bytes_accessed=12 * len(halves) * size * size,
            transcendentals=0,
        ),
    )(*near([left]), *extra, *near(operands.arrays))


def after(value, *others):
    return lax.optimization_barrier((value, *others))[0]


def plain(*tiles):
    return [(tile, None, 0) for tile in tiles]


def shards(interval_blocks, interval_pivots, boundary_pivots, interval_residuals):
    blocks = interval_blocks[0]
    size, share = blocks.shape[1], interval_residuals.shape[2]
    row, col = lax.axis_index("row"), lax.axis_index("col")
    count = lax.axis_size("row")
    position = lax.axis_index("loop")
    positions = lax.axis_size("loop")

    lefts = blocks[1::2]
    riding = jnp.broadcast_to(interval_residuals[0].reshape(1, -1), (EXTRA, size))
    tiles = [jnp.concatenate([blocks[k], riding], axis=0) for k in (0, 2)]
    rights = jnp.stack(tiles)
    ends_left = inward(lefts)
    lefts_other = swap_middle(lefts)
    rights_across = swap_rows(rights, 2)
    end_lower = inward(tiles[0])
    end_upper = inward(tiles[1])

    own = lax.dynamic_index_in_dim(boundary_pivots, position, 0, keepdims=True)
    back = lax.dynamic_index_in_dim(
        boundary_pivots, (position + positions - 1) % positions, 0, keepdims=True
    )
    pivots = jnp.concatenate([interval_pivots[0], own, back], axis=0)
    pivots = (((pivots // size) ^ row) * size + pivots % size).reshape(pivots.shape[0], count, size)
    order = [
        lax.dynamic_index_in_dim(pivots, col ^ flip, 1, keepdims=True) for flip in (0, 1, 3, 2)
    ]
    pivots = jnp.concatenate(order, axis=1)
    places = lax.broadcasted_iota(jnp.int32, (EXTRA, size), 1)
    held = ((places < 2 * share) == (col == 1)).astype(jnp.bfloat16)

    def panel(turn, tiles, onto=None):
        return spread_columns(pivots[turn], tiles, size, count, onto)

    upper_panel, lower_panel = panel(2, [(0, (lefts, 1, 0))]), panel(0, [(0, (lefts, 0, 0))])
    ends_other = swap_middle(ends_left)
    rights_last = swap_rows(rights_across, 1)
    rights_beside = swap_rows(after(rights, upper_panel, lower_panel), 1)
    lower_across = swap_rows(end_lower, 2)
    lower_panel = after(lower_panel, end_lower)
    lower_panel = panel(0, [(1, (ends_left, 0, 0)), (2, (lefts_other, 0, 0))], lower_panel)
    upper_panel = after(upper_panel, end_lower)
    upper_panel = panel(2, [(1, (ends_left, 1, 0)), (2, (lefts_other, 1, 0))], upper_panel)
    upper_across = swap_rows(end_upper, 2)
    upper_ends = [end_upper, swap_rows(end_upper, 1), upper_across]
    lower_panel = after(lower_panel, upper_panel, end_upper)
    lower_panel = panel(0, [(3, (ends_other, 0, 0))], lower_panel)
    lower_last = swap_rows(after(lower_across, lower_panel), 1)
    lower_ends = [end_lower, swap_rows(end_lower, 1), lower_across, lower_last]
    upper_panel = panel(2, [(3, (ends_other, 1, 0))], upper_panel)

    def own_tiles(k):
        return [(tile, k, 0) for tile in (rights, rights_beside, rights_across, rights_last)]

    lower, _ = product(
        lower_panel, [own_tiles(0), plain(*lower_ends)], "joint", size, held, own_tiles(0), 0
    )
    upper_panel = after(upper_panel, lower)
    (upper_o,) = product(upper_panel, [own_tiles(1)], "apart", size)
    upper_ends.append(swap_rows(after(upper_across, upper_o), 1))
    upper_e, vector = product(
        upper_panel, [plain(*upper_ends)], "apart", size, held, own_tiles(1), 2
    )

    def right_views(right, tie):
        parts = []
        for tile in right:
            beside, across = swap_rows(tile, 1), swap_rows(tile, 2)
            parts.append([tile, beside, across, swap_rows(after(across, *tie), 1)])
        if len(parts) == 1:
            return [[(tile, None, column) for tile in parts[0]] for column in (0, size)]
        return [plain(*part) for part in parts]

    other_o, other_e = swap_middle(upper_o), swap_middle(upper_e)
    moved = panel(1, [(0, (upper_o, None, 0)), (1, (upper_e, None, 0))])
    moved = panel(1, [(2, (other_o, None, 0))], moved)
    views = right_views([lower], (moved, other_e))
    moved = panel(1, [(3, (other_e, None, 0))], moved)
    whole, whole_o, whole_e, vector = product(moved, views, "both", size, vector)

    def left_panel(turn, left):
        other = swap_middle(left)
        partial = panel(turn, [(0, (left, None, 0)), (1, (left, None, size))])
        return partial, panel(turn, [(2, (other, None, 0)), (3, (other, None, size))], partial)

    earlier = [from_behind(tile, "loop", 1) for tile in (whole_o, whole_e)]
    partial, moved = left_panel(3, whole)
    views = right_views(earlier, (partial,))
    halved, vector = product(moved, views, "joint", size, vector)
    partial, moved = left_panel(4, halved)
    views = right_views([from_behind(halved, "loop", 2)], (partial,))
    reduced_e, vector = product(moved, views[1:], "apart", size, vector)
    (reduced_o,) = product(after(moved, reduced_e), views[:1], "apart", size)

    middle = (col == 1) | (col == 2)
    block = jnp.where(middle, reduced_o, outward(reduced_e)[:size])
    vector = vector[:1]
    vector = vector + swap_middle(vector)
    vector = jnp.where(middle, vector, outward(vector))
    return (block[None], lax.dynamic_slice_in_dim(vector, col * share, share, 1))


def solution(mesh):
    placed = (
        P("loop", None, "row", "col"),
        P("loop", None, None),
        P(),
        P("loop", None, ("row", "col")),
    )
    return jax.shard_map(
        shards,
        mesh=mesh,
        in_specs=placed,
        out_specs=(P("loop", "row", "col"), P("loop", ("row", "col"))),
        check_vma=False,
    )
```

```python
import jax
import jax.numpy as jnp
from jax import lax
from jax.experimental import pallas as pl
from jax.experimental.pallas import tpu as pltpu
from jax.sharding import PartitionSpec as P

EXTRA = 16
VMEM = 14 * 1024 * 1024
NT = (((1,), (1,)), ((), ()))


def from_behind(value, axis, by):
    devices = lax.axis_size(axis)
    if by % devices == 0:
        return value
    return lax.ppermute(value, axis, [(i, (i + by) % devices) for i in range(devices)])


def swap_rows(value, flip):
    rows, cols = lax.axis_size("row"), lax.axis_size("col")
    pairs = [(r * cols + c, (r ^ flip) * cols + c) for r in range(rows) for c in (1, 2)]
    return lax.ppermute(value, ("row", "col"), pairs)


def swap_middle(value):
    return lax.ppermute(value, "col", [(1, 2), (2, 1)])


def inward(value):
    return lax.ppermute(value, "col", [(0, 1), (3, 2)])


def outward(value):
    return lax.ppermute(value, "col", [(1, 0), (2, 3)])


class Operands:
    def __init__(self):
        self.keys, self.arrays, self.specs = [], [], []

    def add(self, view):
        array, which, column = view
        part = which if isinstance(which, int) else None
        for i, (known, known_part) in enumerate(self.keys):
            if known is array and known_part == part:
                return i, which, column
        self.keys.append((array, part))
        self.arrays.append(array)
        if part is None:
            self.specs.append(pl.BlockSpec(memory_space=pltpu.VMEM))
        else:
            self.specs.append(pl.BlockSpec(memory_space=pl.ANY))
        return len(self.keys) - 1, which, column

    def scratch(self):
        parts = [array for array, part in self.keys if part is not None]
        return [pltpu.VMEM(array.shape[1:], array.dtype) for array in parts] + [
            pltpu.SemaphoreType.DMA((max(len(parts), 1),))
        ]

    def load(self, refs, scratch):
        found, copies = [], []
        for ref, (_, part) in zip(refs, self.keys):
            if part is not None:
                i = len(copies)
                copies.append(pltpu.make_async_copy(ref.at[part], scratch[i], scratch[-1].at[i]))
                copies[-1].start()
                ref = scratch[i]
            found.append(ref)
        for copy in copies:
            copy.wait()
        return found


def read(refs, view, size, rows=None, row=None):
    i, which, column = view
    ref = refs[i].at[row ^ which[0]] if isinstance(which, tuple) else refs[i]
    return ref[rows or slice(0, size), column : column + size]


def spread(refs, views, q_ref, size, n):
    total = None
    for block, view in views:
        at = lax.broadcasted_iota(jnp.int32, (size, size), 0) + n * size
        hot = jnp.where(at == q_ref[block : block + 1, :], 1.0, 0.0).astype(jnp.bfloat16)
        part = lax.dot_general(
            read(refs, view, size), hot, NT, preferred_element_type=jnp.float32
        )
        total = part if total is None else total + part
    return total


def spread_columns(pivots, tiles, size, count, onto=None):
    operands = Operands()
    views = [(block, operands.add(view)) for block, view in tiles]
    extra = [] if onto is None else [onto]

    def kernel(q_ref, *rest):
        onto_ref, rest = rest[0], rest[len(extra) :]
        refs, (out, *scratch) = rest[: len(operands.keys)], rest[len(operands.keys) :]
        refs = operands.load(refs, scratch)

        @pl.loop(0, count)
        def _(n):
            here = pl.ds(pl.multiple_of(n * size, size), size)
            moved = spread(refs, views, q_ref, size, n).astype(out.dtype)
            out[:, here] = moved if onto is None else moved + onto_ref[:, here]

    return pl.pallas_call(
        kernel,
        out_shape=jax.ShapeDtypeStruct((size, size * count), jnp.bfloat16),
        in_specs=[pl.BlockSpec(memory_space=pltpu.VMEM)] * (1 + len(extra)) + operands.specs,
        out_specs=pl.BlockSpec(memory_space=pltpu.VMEM),
        scratch_shapes=operands.scratch(),
        compiler_params=pltpu.CompilerParams(vmem_limit_bytes=VMEM),
        cost_estimate=pl.CostEstimate(
            flops=2 * len(tiles) * size * size * size * count,
            bytes_accessed=8 * size * size,
            transcendentals=0,
        ),
    )(pivots, *extra, *operands.arrays)


def product(left, halves, form, size, added=None, own=None, turn=0, row=None):
    count = left.shape[1] // size
    operands = Operands()
    views = [[operands.add(view) for view in half] for half in halves]
    own_views = [operands.add(view) for view in own or []]
    extra = [] if added is None else [added]
    scalar = [] if row is None else [row.reshape(1)]
    tall, wide = size + (EXTRA if extra else 0), size * len(halves)
    shapes = [] if form == "apart" else [(tall, wide)]
    if form != "joint":
        shapes += [(size, size)] * (len(halves) - 1) + [(tall, size)]
    outs = [jax.ShapeDtypeStruct(shape, jnp.bfloat16) for shape in shapes]
    if extra:
        outs.append(jax.ShapeDtypeStruct((EXTRA, size), jnp.float32))

    def kernel(left_ref, *rest):
        here = None
        if scalar:
            here, rest = rest[0][0], rest[1:]
        refs = rest[len(extra) : len(extra) + len(operands.arrays)]
        results = rest[len(extra) + len(refs) :]
        joint = None if form == "apart" else results[0]
        single = [] if form == "joint" else results[len(shapes) - len(halves) : len(shapes)]

        for i, half in enumerate(views):
            total = None
            for b in range(count):
                part = jnp.dot(
                    left_ref[:, b * size : (b + 1) * size],
                    read(refs, half[b], size, row=here),
                    preferred_element_type=jnp.float32,
                )
                total = part if total is None else total + part
            total = total.astype(jnp.bfloat16)
            if joint is not None:
                joint[0:size, i * size : (i + 1) * size] = total
            if single:
                single[i][0:size, :] = total
        if not extra:
            return

        def pieces(b, k):
            lanes = slice(k * (size // 4), (k + 1) * (size // 4))
            near, end = (
                read(refs, kind[b], size, slice(size, tall), here)[:, lanes]
                for kind in (own_views, views[-1])
            )
            return jnp.concatenate([end, near, near, end], axis=1) * rest[0][...]

        applied = rest[0][...] if own is None else pieces(0, turn + 1).astype(jnp.float32)
        for b in range(count):
            if own is None:
                rows = read(refs, views[-1][b], size, slice(size, tall))
            else:
                rows = pieces(b, turn)
            applied = applied + lax.dot_general(
                rows, left_ref[:, b * size : (b + 1) * size], NT, preferred_element_type=jnp.float32
            )
        results[-1][...] = applied
        applied = applied.astype(jnp.bfloat16)
        if joint is not None:
            for i in range(len(halves)):
                joint[size:tall, i * size : (i + 1) * size] = applied
        if single:
            single[-1][size:tall, :] = applied

    whole = pl.BlockSpec(memory_space=pltpu.VMEM)
    specs = [pl.BlockSpec(memory_space=pltpu.SMEM)] * len(scalar) + [whole] * len(extra)
    return pl.pallas_call(
        kernel,
        out_shape=tuple(outs),
        in_specs=[whole] + specs + operands.specs,
        out_specs=(whole,) * len(outs),
        compiler_params=pltpu.CompilerParams(vmem_limit_bytes=VMEM),
        cost_estimate=pl.CostEstimate(
            flops=2 * len(halves) * size * size * size * count,
            bytes_accessed=12 * len(halves) * size * size,
            transcendentals=0,
        ),
    )(left, *scalar, *extra, *operands.arrays)


def after(value, *others):
    return lax.optimization_barrier((value, *others))[0]


def plain(*tiles):
    return [(tile, None, 0) for tile in tiles]


def shards(interval_blocks, interval_pivots, boundary_pivots, interval_residuals):
    blocks = interval_blocks[0]
    size, share = blocks.shape[1], interval_residuals.shape[2]
    row, col = lax.axis_index("row"), lax.axis_index("col")
    count = lax.axis_size("row")
    position = lax.axis_index("loop")
    positions = lax.axis_size("loop")

    lefts = blocks[1::2]
    riding = jnp.broadcast_to(interval_residuals[0].reshape(1, -1), (EXTRA, size))
    tiles = [jnp.concatenate([blocks[k], riding], axis=0) for k in (0, 2)]
    ends_left = inward(lefts)
    lefts_other = swap_middle(lefts)
    rights = [lax.all_gather(tile, "row", axis=0) for tile in tiles]
    end_lower = inward(tiles[0])
    end_upper = inward(tiles[1])

    own = lax.dynamic_index_in_dim(boundary_pivots, position, 0, keepdims=True)
    back = lax.dynamic_index_in_dim(
        boundary_pivots, (position + positions - 1) % positions, 0, keepdims=True
    )
    pivots = jnp.concatenate([interval_pivots[0], own, back], axis=0)
    pivots = (((pivots // size) ^ row) * size + pivots % size).reshape(pivots.shape[0], count, size)
    order = [
        lax.dynamic_index_in_dim(pivots, col ^ flip, 1, keepdims=True) for flip in (0, 1, 3, 2)
    ]
    pivots = jnp.concatenate(order, axis=1)
    places = lax.broadcasted_iota(jnp.int32, (EXTRA, size), 1)
    held = ((places < 2 * share) == (col == 1)).astype(jnp.bfloat16)

    def panel(turn, tiles, onto=None):
        return spread_columns(pivots[turn], tiles, size, count, onto)

    upper_panel, lower_panel = panel(2, [(0, (lefts, 1, 0))]), panel(0, [(0, (lefts, 0, 0))])
    ends_other = swap_middle(after(ends_left, upper_panel, lower_panel))
    lower_panel = panel(0, [(1, (ends_left, 0, 0)), (2, (lefts_other, 0, 0))], lower_panel)
    upper_panel = panel(2, [(1, (ends_left, 1, 0)), (2, (lefts_other, 1, 0))], upper_panel)
    end_lower = after(end_lower, lower_panel, upper_panel)
    lower_across = swap_rows(end_lower, 2)
    lower_ends = [end_lower, swap_rows(end_lower, 1), lower_across, swap_rows(lower_across, 1)]
    upper_across = swap_rows(end_upper, 2)
    upper_ends = [end_upper, swap_rows(end_upper, 1), upper_across]
    lower_panel = panel(0, [(3, (ends_other, 0, 0))], lower_panel)

    def own_tiles(k):
        return [(rights[k], (b,), 0) for b in range(count)]

    lower, _ = product(
        lower_panel, [own_tiles(0), plain(*lower_ends)], "joint", size, held, own_tiles(0), 0, row
    )
    upper_panel = after(upper_panel, lower)
    upper_panel = panel(2, [(3, (ends_other, 1, 0))], upper_panel)
    (upper_o,) = product(upper_panel, [own_tiles(1)], "apart", size, row=row)
    upper_ends.append(swap_rows(after(upper_across, upper_o), 1))
    upper_e, vector = product(
        upper_panel, [plain(*upper_ends)], "apart", size, held, own_tiles(1), 2, row
    )

    def right_views(right, tie):
        parts = []
        for tile in right:
            beside, across = swap_rows(tile, 1), swap_rows(tile, 2)
            parts.append([tile, beside, across, swap_rows(after(across, *tie), 1)])
        if len(parts) == 1:
            return [[(tile, None, column) for tile in parts[0]] for column in (0, size)]
        return [plain(*part) for part in parts]

    other_o, other_e = swap_middle(upper_o), swap_middle(upper_e)
    moved = panel(1, [(0, (upper_o, None, 0)), (1, (upper_e, None, 0))])
    moved = panel(1, [(2, (other_o, None, 0))], moved)
    views = right_views([lower], (moved, other_e))
    moved = panel(1, [(3, (other_e, None, 0))], moved)
    whole, whole_o, whole_e, vector = product(moved, views, "both", size, vector)

    def left_panel(turn, left):
        other = swap_middle(left)
        partial = panel(turn, [(0, (left, None, 0)), (1, (left, None, size))])
        return partial, panel(turn, [(2, (other, None, 0)), (3, (other, None, size))], partial)

    earlier = [from_behind(tile, "loop", 1) for tile in (whole_o, whole_e)]
    partial, moved = left_panel(3, whole)
    views = right_views(earlier, (partial,))
    halved, vector = product(moved, views, "joint", size, vector)
    partial, moved = left_panel(4, halved)
    views = right_views([from_behind(halved, "loop", 2)], (partial,))
    reduced_e, vector = product(moved, views[1:], "apart", size, vector)
    (reduced_o,) = product(after(moved, reduced_e), views[:1], "apart", size)

    middle = (col == 1) | (col == 2)
    block = jnp.where(middle, reduced_o, outward(reduced_e)[:size])
    vector = vector[:1]
    vector = vector + swap_middle(vector)
    vector = jnp.where(middle, vector, outward(vector))
    return (block[None], lax.dynamic_slice_in_dim(vector, col * share, share, 1))


def solution(mesh):
    placed = (
        P("loop", None, "row", "col"),
        P("loop", None, None),
        P(),
        P("loop", None, ("row", "col")),
    )
    return jax.shard_map(
        shards,
        mesh=mesh,
        in_specs=placed,
        out_specs=(P("loop", "row", "col"), P("loop", ("row", "col"))),
        check_vma=False,
    )
```

```python
import jax
import jax.numpy as jnp
from jax import lax
from jax.experimental import pallas as pl
from jax.experimental.pallas import tpu as pltpu
from jax.sharding import PartitionSpec as P

EXTRA = 16
VMEM = 14 * 1024 * 1024
TOKEN = jax.ShapeDtypeStruct((8, 128), jnp.float32)
NT = (((1,), (1,)), ((), ()))


def from_behind(value, axis, by):
    devices = lax.axis_size(axis)
    if by % devices == 0:
        return value
    return lax.ppermute(value, axis, [(i, (i + by) % devices) for i in range(devices)])


def swap_rows(value, flip):
    rows, cols = lax.axis_size("row"), lax.axis_size("col")
    pairs = [(r * cols + c, (r ^ flip) * cols + c) for r in range(rows) for c in (1, 2)]
    return lax.ppermute(value, ("row", "col"), pairs)


def swap_middle(value):
    return lax.ppermute(value, "col", [(1, 2), (2, 1)])


def inward(value):
    return lax.ppermute(value, "col", [(0, 1), (3, 2)])


def outward(value):
    return lax.ppermute(value, "col", [(1, 0), (2, 3)])


class Operands:
    def __init__(self):
        self.keys, self.arrays, self.specs = [], [], []

    def add(self, view):
        array, which, column = view
        for i, (known, part) in enumerate(self.keys):
            if known is array and part == which:
                return i, column
        self.keys.append((array, which))
        self.arrays.append(array)
        if which is None:
            self.specs.append(pl.BlockSpec(memory_space=pltpu.VMEM))
        else:
            self.specs.append(pl.BlockSpec(memory_space=pl.ANY))
        return len(self.keys) - 1, column

    def scratch(self):
        parts = [array for array, part in self.keys if part is not None]
        return [pltpu.VMEM(array.shape[1:], array.dtype) for array in parts] + [
            pltpu.SemaphoreType.DMA((max(len(parts), 1),))
        ]

    def load(self, refs, scratch):
        found, copies = [], []
        for ref, (_, part) in zip(refs, self.keys):
            if part is not None:
                i = len(copies)
                copies.append(pltpu.make_async_copy(ref.at[part], scratch[i], scratch[-1].at[i]))
                copies[-1].start()
                ref = scratch[i]
            found.append(ref)
        for copy in copies:
            copy.wait()
        return found


def read(refs, view, size, rows=None):
    i, column = view
    return refs[i][rows or slice(0, size), column : column + size]


def spread(refs, views, q_ref, size, n):
    total = None
    for block, view in views:
        at = lax.broadcasted_iota(jnp.int32, (size, size), 0) + n * size
        hot = jnp.where(at == q_ref[block : block + 1, :], 1.0, 0.0).astype(jnp.bfloat16)
        part = lax.dot_general(
            read(refs, view, size), hot, NT, preferred_element_type=jnp.float32
        )
        total = part if total is None else total + part
    return total


def spread_columns(pivots, tiles, size, count, onto=None, wait=()):
    operands = Operands()
    views = [(block, operands.add(view)) for block, view in tiles]
    extra = [] if onto is None else [onto]

    def kernel(q_ref, *rest):
        onto_ref, rest = rest[0], rest[len(extra) :]
        token, out, *scratch = rest[len(operands.keys) + len(wait) :]
        refs = operands.load(rest[: len(operands.keys)], scratch)
        token[...] = jnp.zeros_like(token)

        @pl.loop(0, count)
        def _(n):
            here = pl.ds(pl.multiple_of(n * size, size), size)
            moved = spread(refs, views, q_ref, size, n).astype(out.dtype)
            out[:, here] = moved if onto is None else moved + onto_ref[:, here]

    return pl.pallas_call(
        kernel,
        out_shape=(TOKEN, jax.ShapeDtypeStruct((size, size * count), jnp.bfloat16)),
        in_specs=[pl.BlockSpec(memory_space=pltpu.VMEM)] * (1 + len(extra))
        + operands.specs
        + [pl.BlockSpec(memory_space=pl.ANY)] * len(wait),
        out_specs=(pl.BlockSpec(memory_space=pltpu.VMEM),) * 2,
        scratch_shapes=operands.scratch(),
        compiler_params=pltpu.CompilerParams(vmem_limit_bytes=VMEM),
        cost_estimate=pl.CostEstimate(
            flops=2 * len(tiles) * size * size * size * count,
            bytes_accessed=8 * size * size,
            transcendentals=0,
        ),
    )(pivots, *extra, *operands.arrays, *wait)


def product(left, halves, form, size, added=None, own=None, turn=0, wait=()):
    count = left.shape[1] // size
    operands = Operands()
    views = [[operands.add(view) for view in half] for half in halves]
    own_views = [operands.add(view) for view in own or []]
    extra = [] if added is None else [added]
    tall, wide = size + (EXTRA if extra else 0), size * len(halves)
    shapes = [] if form == "apart" else [(tall, wide)]
    if form != "joint":
        shapes += [(size, size)] * (len(halves) - 1) + [(tall, size)]
    outs = [TOKEN] + [jax.ShapeDtypeStruct(shape, jnp.bfloat16) for shape in shapes]
    if extra:
        outs.append(jax.ShapeDtypeStruct((EXTRA, size), jnp.float32))

    def kernel(left_ref, *rest):
        refs = rest[len(extra) : len(extra) + len(operands.keys)]
        token, *results = rest[len(extra) + len(refs) + len(wait) :]
        results, scratch = results[: len(outs) - 1], results[len(outs) - 1 :]
        refs = operands.load(refs, scratch)
        token[...] = jnp.zeros_like(token)
        joint = None if form == "apart" else results[0]
        single = [] if form == "joint" else results[len(shapes) - len(halves) : len(shapes)]

        for i, half in enumerate(views):
            total = None
            for b in range(count):
                part = jnp.dot(
                    left_ref[:, b * size : (b + 1) * size],
                    read(refs, half[b], size),
                    preferred_element_type=jnp.float32,
                )
                total = part if total is None else total + part
            total = total.astype(jnp.bfloat16)
            if joint is not None:
                joint[0:size, i * size : (i + 1) * size] = total
            if single:
                single[i][0:size, :] = total
        if not extra:
            return

        def pieces(b, k):
            lanes = slice(k * (size // 4), (k + 1) * (size // 4))
            near, end = (
                read(refs, kind[b], size, slice(size, tall))[:, lanes]
                for kind in (own_views, views[-1])
            )
            return jnp.concatenate([end, near, near, end], axis=1) * rest[0][...]

        applied = rest[0][...] if own is None else pieces(0, turn + 1).astype(jnp.float32)
        for b in range(count):
            if own is None:
                rows = read(refs, views[-1][b], size, slice(size, tall))
            else:
                rows = pieces(b, turn)
            applied = applied + lax.dot_general(
                rows, left_ref[:, b * size : (b + 1) * size], NT, preferred_element_type=jnp.float32
            )
        results[-1][...] = applied
        applied = applied.astype(jnp.bfloat16)
        if joint is not None:
            for i in range(len(halves)):
                joint[size:tall, i * size : (i + 1) * size] = applied
        if single:
            single[-1][size:tall, :] = applied

    whole = pl.BlockSpec(memory_space=pltpu.VMEM)
    waits = [pl.BlockSpec(memory_space=pl.ANY)] * len(wait)
    return pl.pallas_call(
        kernel,
        out_shape=tuple(outs),
        in_specs=[whole] * (1 + len(extra)) + operands.specs + waits,
        out_specs=(whole,) * len(outs),
        scratch_shapes=operands.scratch(),
        compiler_params=pltpu.CompilerParams(vmem_limit_bytes=VMEM),
        cost_estimate=pl.CostEstimate(
            flops=2 * len(halves) * size * size * size * count,
            bytes_accessed=12 * len(halves) * size * size,
            transcendentals=0,
        ),
    )(left, *extra, *operands.arrays, *wait)


def after(value, *others):
    return lax.optimization_barrier((value, *others))


def plain(*tiles):
    return [(tile, None, 0) for tile in tiles]


def shards(interval_blocks, interval_pivots, boundary_pivots, interval_residuals):
    blocks = interval_blocks[0]
    size, share = blocks.shape[1], interval_residuals.shape[2]
    row, col = lax.axis_index("row"), lax.axis_index("col")
    count = lax.axis_size("row")
    position = lax.axis_index("loop")
    positions = lax.axis_size("loop")

    lefts = blocks[1::2]
    riding = jnp.broadcast_to(interval_residuals[0].reshape(1, -1), (EXTRA, size))
    tiles = [jnp.concatenate([blocks[k], riding], axis=0) for k in (0, 2)]
    ends_left = inward(lefts)
    lefts_other = swap_middle(lefts)
    rights = jnp.stack(tiles)
    rights_across = swap_rows(rights, 2)
    end_lower = inward(tiles[0])
    end_upper = inward(tiles[1])
    rights_beside = swap_rows(rights, 1)

    own = lax.dynamic_index_in_dim(boundary_pivots, position, 0, keepdims=True)
    back = lax.dynamic_index_in_dim(
        boundary_pivots, (position + positions - 1) % positions, 0, keepdims=True
    )
    pivots = jnp.concatenate([interval_pivots[0], own, back], axis=0)
    pivots = (((pivots // size) ^ row) * size + pivots % size).reshape(pivots.shape[0], count, size)
    order = [
        lax.dynamic_index_in_dim(pivots, col ^ flip, 1, keepdims=True) for flip in (0, 1, 3, 2)
    ]
    pivots = jnp.concatenate(order, axis=1)
    places = lax.broadcasted_iota(jnp.int32, (EXTRA, size), 1)
    held = ((places < 2 * share) == (col == 1)).astype(jnp.bfloat16)

    def panel(turn, tiles, onto=None, wait=()):
        return spread_columns(pivots[turn], tiles, size, count, onto, wait)

    lower_done, lower_panel = panel(0, [(0, (lefts, 0, 0))])
    upper_done, upper_panel = panel(2, [(0, (lefts, 1, 0))])
    tied, *seen = after(ends_left, lower_done, upper_done)
    ends_other = swap_middle(tied)
    rights_last = swap_rows(rights_across, 1)
    lower_done, lower_panel = panel(
        0, [(1, (ends_left, 0, 0)), (2, (lefts_other, 0, 0))], lower_panel, seen
    )
    upper_done, upper_panel = panel(
        2, [(1, (ends_left, 1, 0)), (2, (lefts_other, 1, 0))], upper_panel
    )
    end_lower, *seen = after(end_lower, lower_done, upper_done)
    lower_across = swap_rows(end_lower, 2)
    lower_ends = [end_lower, swap_rows(end_lower, 1), lower_across, swap_rows(lower_across, 1)]
    upper_across = swap_rows(end_upper, 2)
    upper_ends = [end_upper, swap_rows(end_upper, 1), upper_across]

    def own_tiles(k):
        return [(tile, k, 0) for tile in (rights, rights_beside, rights_across, rights_last)]

    _, lower_panel = panel(0, [(3, (ends_other, 0, 0))], lower_panel, seen)
    lower_done, lower, _ = product(
        lower_panel, [own_tiles(0), plain(*lower_ends)], "joint", size, held, own_tiles(0), 0
    )
    _, upper_panel = panel(2, [(3, (ends_other, 1, 0))], upper_panel, [lower_done])
    upper_done, upper_o = product(upper_panel, [own_tiles(1)], "apart", size)
    tied, seen = after(upper_across, upper_done)
    upper_ends.append(swap_rows(tied, 1))
    _, upper_e, vector = product(
        upper_panel, [plain(*upper_ends)], "apart", size, held, own_tiles(1), 2, [seen]
    )

    def right_views(right, tie):
        parts, seen = [], []
        for tile in right:
            beside, across = swap_rows(tile, 1), swap_rows(tile, 2)
            tied, token, *_ = after(across, *tie)
            parts.append([tile, beside, across, swap_rows(tied, 1)])
            seen.append(token)
        if len(parts) == 1:
            return [[(tile, None, column) for tile in parts[0]] for column in (0, size)], seen
        return [plain(*part) for part in parts], seen

    other_o, other_e = swap_middle(upper_o), swap_middle(upper_e)
    _, moved = panel(1, [(0, (upper_o, None, 0)), (1, (upper_e, None, 0))])
    done, moved = panel(1, [(2, (other_o, None, 0))], moved)
    views, seen = right_views([lower], (done, other_e))
    _, moved = panel(1, [(3, (other_e, None, 0))], moved)
    _, whole, whole_o, whole_e, vector = product(moved, views, "both", size, vector, wait=seen)

    def left_panel(turn, left):
        other = swap_middle(left)
        done, moved = panel(turn, [(0, (left, None, 0)), (1, (left, None, size))])
        return done, panel(turn, [(2, (other, None, 0)), (3, (other, None, size))], moved)[1]

    earlier = [from_behind(tile, "loop", 1) for tile in (whole_o, whole_e)]
    done, moved = left_panel(3, whole)
    views, seen = right_views(earlier, (done,))
    _, halved, vector = product(moved, views, "joint", size, vector, wait=seen)
    done, moved = left_panel(4, halved)
    views, seen = right_views([from_behind(halved, "loop", 2)], (done,))
    done, reduced_e, vector = product(moved, views[1:], "apart", size, vector, wait=seen)
    _, reduced_o = product(moved, views[:1], "apart", size, wait=[done])

    middle = (col == 1) | (col == 2)
    block = jnp.where(middle, reduced_o, outward(reduced_e)[:size])
    vector = vector[:1]
    vector = vector + swap_middle(vector)
    vector = jnp.where(middle, vector, outward(vector))
    return (block[None], lax.dynamic_slice_in_dim(vector, col * share, share, 1))


def solution(mesh):
    placed = (
        P("loop", None, "row", "col"),
        P("loop", None, None),
        P(),
        P("loop", None, ("row", "col")),
    )
    return jax.shard_map(
        shards,
        mesh=mesh,
        in_specs=placed,
        out_specs=(P("loop", "row", "col"), P("loop", ("row", "col"))),
        check_vma=False,
    )
```

```python
import jax
import jax.numpy as jnp
from jax import lax
from jax.experimental import pallas as pl
from jax.experimental.pallas import tpu as pltpu
from jax.sharding import PartitionSpec as P

EXTRA = 16
VMEM = 14 * 1024 * 1024
NT = (((1,), (1,)), ((), ()))


def from_behind(value, axis, by):
    devices = lax.axis_size(axis)
    if by % devices == 0:
        return value
    return lax.ppermute(value, axis, [(i, (i + by) % devices) for i in range(devices)])


def swap_rows(value, flip):
    rows, cols = lax.axis_size("row"), lax.axis_size("col")
    pairs = [(r * cols + c, (r ^ flip) * cols + c) for r in range(rows) for c in (1, 2)]
    return lax.ppermute(value, ("row", "col"), pairs)


def swap_middle(value):
    return lax.ppermute(value, "col", [(1, 2), (2, 1)])


def inward(value):
    return lax.ppermute(value, "col", [(0, 1), (3, 2)])


def outward(value):
    return lax.ppermute(value, "col", [(1, 0), (2, 3)])


class Operands:
    def __init__(self):
        self.arrays = []

    def add(self, view):
        array, lead, column = view
        for i, known in enumerate(self.arrays):
            if known is array:
                return i, lead, column
        self.arrays.append(array)
        return len(self.arrays) - 1, lead, column


def read(refs, view, size, rows=None):
    which, lead, column = view
    ref = refs[which] if lead is None else refs[which].at[lead]
    return ref[rows or slice(0, size), column : column + size]


def spread(refs, views, q_ref, size, n):
    total = None
    for block, view in views:
        at = lax.broadcasted_iota(jnp.int32, (size, size), 0) + n * size
        hot = jnp.where(at == q_ref[block : block + 1, :], 1.0, 0.0).astype(jnp.bfloat16)
        part = lax.dot_general(
            read(refs, view, size), hot, NT, preferred_element_type=jnp.float32
        )
        total = part if total is None else total + part
    return total


def spread_columns(pivots, tiles, size, count, onto=None):
    operands = Operands()
    views = [(block, operands.add(view)) for block, view in tiles]
    extra = [] if onto is None else [onto]

    def kernel(q_ref, *refs):
        out = refs[-1]

        @pl.loop(0, count)
        def _(n):
            here = pl.ds(pl.multiple_of(n * size, size), size)
            moved = spread(refs[len(extra) :], views, q_ref, size, n).astype(out.dtype)
            out[:, here] = moved if onto is None else moved + refs[0][:, here]

    return pl.pallas_call(
        kernel,
        out_shape=jax.ShapeDtypeStruct((size, size * count), jnp.bfloat16),
        compiler_params=pltpu.CompilerParams(vmem_limit_bytes=VMEM),
        cost_estimate=pl.CostEstimate(
            flops=2 * len(tiles) * size * size * size * count,
            bytes_accessed=8 * size * size,
            transcendentals=0,
        ),
    )(pivots, *extra, *operands.arrays)


def product(left, halves, form, size, added=None, own=None, turn=0):
    count = left.shape[1] // size
    operands = Operands()
    views = [[operands.add(view) for view in half] for half in halves]
    own_views = [operands.add(view) for view in own or []]
    extra = [] if added is None else [added]
    tall, wide = size + (EXTRA if extra else 0), size * len(halves)
    shapes = [] if form == "apart" else [(tall, wide)]
    if form != "joint":
        shapes += [(size, size)] * (len(halves) - 1) + [(tall, size)]
    outs = [jax.ShapeDtypeStruct(shape, jnp.bfloat16) for shape in shapes]
    if extra:
        outs.append(jax.ShapeDtypeStruct((EXTRA, size), jnp.float32))

    def kernel(left_ref, *rest):
        refs = rest[len(extra) : len(extra) + len(operands.arrays)]
        results = rest[len(extra) + len(refs) :]
        joint = None if form == "apart" else results[0]
        single = [] if form == "joint" else results[len(shapes) - len(halves) : len(shapes)]

        for i, half in enumerate(views):
            total = None
            for b in range(count):
                part = jnp.dot(
                    left_ref[:, b * size : (b + 1) * size],
                    read(refs, half[b], size),
                    preferred_element_type=jnp.float32,
                )
                total = part if total is None else total + part
            total = total.astype(jnp.bfloat16)
            if joint is not None:
                joint[0:size, i * size : (i + 1) * size] = total
            if single:
                single[i][0:size, :] = total
        if not extra:
            return

        def pieces(b, k):
            here = slice(k * (size // 4), (k + 1) * (size // 4))
            near, end = (
                read(refs, kind[b], size, slice(size, tall))[:, here] for kind in (own_views, views[-1])
            )
            return jnp.concatenate([end, near, near, end], axis=1) * rest[0][...]

        applied = rest[0][...] if own is None else pieces(0, turn + 1).astype(jnp.float32)
        for b in range(count):
            if own is None:
                rows = read(refs, views[-1][b], size, slice(size, tall))
            else:
                rows = pieces(b, turn)
            applied = applied + lax.dot_general(
                rows, left_ref[:, b * size : (b + 1) * size], NT, preferred_element_type=jnp.float32
            )
        results[-1][...] = applied
        applied = applied.astype(jnp.bfloat16)
        if joint is not None:
            for i in range(len(halves)):
                joint[size:tall, i * size : (i + 1) * size] = applied
        if single:
            single[-1][size:tall, :] = applied

    return pl.pallas_call(
        kernel,
        out_shape=tuple(outs),
        compiler_params=pltpu.CompilerParams(vmem_limit_bytes=VMEM),
        cost_estimate=pl.CostEstimate(
            flops=2 * len(halves) * size * size * size * count,
            bytes_accessed=12 * len(halves) * size * size,
            transcendentals=0,
        ),
    )(left, *extra, *operands.arrays)


def after(value, *others):
    return lax.optimization_barrier((value, *others))[0]


def plain(*tiles):
    return [(tile, None, 0) for tile in tiles]


def shards(interval_blocks, interval_pivots, boundary_pivots, interval_residuals):
    blocks = interval_blocks[0]
    size, share = blocks.shape[1], interval_residuals.shape[2]
    row, col = lax.axis_index("row"), lax.axis_index("col")
    count = lax.axis_size("row")
    position = lax.axis_index("loop")
    positions = lax.axis_size("loop")

    lefts = blocks[1::2]
    riding = jnp.broadcast_to(interval_residuals[0].reshape(1, -1), (EXTRA, size))
    tiles = [jnp.concatenate([blocks[k], riding], axis=0) for k in (0, 2)]
    rights = jnp.stack(tiles)
    ends_left = inward(lefts)
    lefts_other = swap_middle(lefts)
    rights_across = swap_rows(rights, 2)
    end_lower = inward(tiles[0])
    end_upper = inward(tiles[1])
    rights_beside = swap_rows(rights, 1)

    own = lax.dynamic_index_in_dim(boundary_pivots, position, 0, keepdims=True)
    back = lax.dynamic_index_in_dim(
        boundary_pivots, (position + positions - 1) % positions, 0, keepdims=True
    )
    pivots = jnp.concatenate([interval_pivots[0], own, back], axis=0)
    pivots = (((pivots // size) ^ row) * size + pivots % size).reshape(pivots.shape[0], count, size)
    order = [
        lax.dynamic_index_in_dim(pivots, col ^ flip, 1, keepdims=True) for flip in (0, 1, 3, 2)
    ]
    pivots = jnp.concatenate(order, axis=1)
    places = lax.broadcasted_iota(jnp.int32, (1, size), 1)
    held = ((places < 2 * share) == (col == 1)).astype(jnp.bfloat16)
    held, *pivots = lax.optimization_barrier((held, *(pivots[turn] for turn in range(5))))

    def panel(turn, tiles, onto=None):
        return spread_columns(pivots[turn], tiles, size, count, onto)

    upper_panel, lower_panel = panel(2, [(0, (lefts, 1, 0))]), panel(0, [(0, (lefts, 0, 0))])
    ends_other = swap_middle(after(ends_left, upper_panel, lower_panel))
    rights_last = swap_rows(rights_across, 1)
    lower_panel = panel(0, [(1, (ends_left, 0, 0)), (2, (lefts_other, 0, 0))], lower_panel)
    upper_panel = panel(2, [(1, (ends_left, 1, 0)), (2, (lefts_other, 1, 0))], upper_panel)
    end_lower = after(end_lower, lower_panel, upper_panel)
    lower_across = swap_rows(end_lower, 2)
    lower_ends = [end_lower, swap_rows(end_lower, 1), lower_across, swap_rows(lower_across, 1)]
    upper_across = swap_rows(end_upper, 2)
    upper_ends = [end_upper, swap_rows(end_upper, 1), upper_across]
    lower_panel = panel(0, [(3, (ends_other, 0, 0))], lower_panel)
    upper_panel = panel(2, [(3, (ends_other, 1, 0))], upper_panel)

    def own_tiles(k):
        return [(tile, k, 0) for tile in (rights, rights_beside, rights_across, rights_last)]

    lower, _ = product(
        lower_panel, [own_tiles(0), plain(*lower_ends)], "joint", size, held, own_tiles(0), 0
    )
    upper_panel = after(upper_panel, lower)
    (upper_o,) = product(upper_panel, [own_tiles(1)], "apart", size)
    upper_ends.append(swap_rows(after(upper_across, upper_o), 1))
    upper_e, vector = product(
        upper_panel, [plain(*upper_ends)], "apart", size, held, own_tiles(1), 2
    )

    def right_views(right, tie):
        parts = []
        for tile in right:
            beside, across = swap_rows(tile, 1), swap_rows(tile, 2)
            parts.append([tile, beside, across, swap_rows(after(across, *tie), 1)])
        if len(parts) == 1:
            return [[(tile, None, column) for tile in parts[0]] for column in (0, size)]
        return [plain(*part) for part in parts]

    other_o, other_e = swap_middle(upper_o), swap_middle(upper_e)
    moved = panel(1, [(0, (upper_o, None, 0)), (1, (upper_e, None, 0))])
    moved = panel(1, [(2, (other_o, None, 0))], moved)
    views = right_views([lower], (moved, other_e))
    moved = panel(1, [(3, (other_e, None, 0))], moved)
    whole, whole_o, whole_e, vector = product(moved, views, "both", size, vector)

    def left_panel(turn, left):
        other = swap_middle(left)
        partial = panel(turn, [(0, (left, None, 0)), (1, (left, None, size))])
        return partial, panel(turn, [(2, (other, None, 0)), (3, (other, None, size))], partial)

    earlier = [from_behind(tile, "loop", 1) for tile in (whole_o, whole_e)]
    partial, moved = left_panel(3, whole)
    views = right_views(earlier, (partial,))
    halved, vector = product(moved, views, "joint", size, vector)
    partial, moved = left_panel(4, halved)
    views = right_views([from_behind(halved, "loop", 2)], (partial,))
    reduced_e, vector = product(moved, views[1:], "apart", size, vector)
    (reduced_o,) = product(after(moved, reduced_e), views[:1], "apart", size)

    middle = (col == 1) | (col == 2)
    block = jnp.where(middle, reduced_o, outward(reduced_e)[:size])
    vector = after(vector, reduced_o)[:1]
    vector = vector + swap_middle(vector)
    vector = jnp.where(middle, vector, outward(vector))
    return (block[None], lax.dynamic_slice_in_dim(vector, col * share, share, 1))


def solution(mesh):
    placed = (
        P("loop", None, "row", "col"),
        P("loop", None, None),
        P(),
        P("loop", None, ("row", "col")),
    )
    return jax.shard_map(
        shards,
        mesh=mesh,
        in_specs=placed,
        out_specs=(P("loop", "row", "col"), P("loop", ("row", "col"))),
        check_vma=False,
    )
```

```python
import jax
import jax.numpy as jnp
from jax import lax
from jax.experimental import pallas as pl
from jax.experimental.pallas import tpu as pltpu
from jax.sharding import PartitionSpec as P

EXTRA = 16
VMEM = 14 * 1024 * 1024
NT = (((1,), (1,)), ((), ()))


def from_behind(value, axis, by):
    devices = lax.axis_size(axis)
    if by % devices == 0:
        return value
    return lax.ppermute(value, axis, [(i, (i + by) % devices) for i in range(devices)])


def swap_rows(value, flip):
    rows, cols = lax.axis_size("row"), lax.axis_size("col")
    pairs = [(r * cols + c, (r ^ flip) * cols + c) for r in range(rows) for c in (1, 2)]
    return lax.ppermute(value, ("row", "col"), pairs)


def swap_middle(value):
    return lax.ppermute(value, "col", [(1, 2), (2, 1)])


def inward(value):
    return lax.ppermute(value, "col", [(0, 1), (3, 2)])


def outward(value):
    return lax.ppermute(value, "col", [(1, 0), (2, 3)])


class Operands:
    def __init__(self):
        self.arrays = []

    def add(self, view):
        array, lead, column = view
        for i, known in enumerate(self.arrays):
            if known is array:
                return i, lead, column
        self.arrays.append(array)
        return len(self.arrays) - 1, lead, column


def read(refs, view, size, rows=None):
    which, lead, column = view
    ref = refs[which] if lead is None else refs[which].at[lead]
    return ref[rows or slice(0, size), column : column + size]


def spread(refs, views, q_ref, size, n):
    total = None
    for block, view in views:
        at = lax.broadcasted_iota(jnp.int32, (size, size), 0) + n * size
        hot = jnp.where(at == q_ref[block : block + 1, :], 1.0, 0.0).astype(jnp.bfloat16)
        part = lax.dot_general(
            read(refs, view, size), hot, NT, preferred_element_type=jnp.float32
        )
        total = part if total is None else total + part
    return total


def spread_columns(pivots, tiles, size, count, onto=None):
    operands = Operands()
    views = [(block, operands.add(view)) for block, view in tiles]
    extra = [] if onto is None else [onto]

    def kernel(q_ref, *refs):
        out = refs[-1]

        @pl.loop(0, count)
        def _(n):
            here = pl.ds(pl.multiple_of(n * size, size), size)
            moved = spread(refs[len(extra) :], views, q_ref, size, n).astype(out.dtype)
            out[:, here] = moved if onto is None else moved + refs[0][:, here]

    return pl.pallas_call(
        kernel,
        out_shape=jax.ShapeDtypeStruct((size, size * count), jnp.bfloat16),
        compiler_params=pltpu.CompilerParams(vmem_limit_bytes=VMEM),
        cost_estimate=pl.CostEstimate(
            flops=2 * len(tiles) * size * size * size * count,
            bytes_accessed=8 * size * size,
            transcendentals=0,
        ),
    )(pivots, *extra, *operands.arrays)


def product(left, halves, form, size, added=None, own=None, turn=0):
    count = left.shape[1] // size
    operands = Operands()
    views = [[operands.add(view) for view in half] for half in halves]
    own_views = [operands.add(view) for view in own or []]
    extra = [] if added is None else [added]
    tall, wide = size + (EXTRA if extra else 0), size * len(halves)
    shapes = [] if form == "apart" else [(tall, wide)]
    if form != "joint":
        shapes += [(size, size)] * (len(halves) - 1) + [(tall, size)]
    outs = [jax.ShapeDtypeStruct(shape, jnp.bfloat16) for shape in shapes]
    if extra:
        outs.append(jax.ShapeDtypeStruct((EXTRA, size), jnp.float32))

    def kernel(left_ref, *rest):
        refs = rest[len(extra) : len(extra) + len(operands.arrays)]
        results = rest[len(extra) + len(refs) :]
        joint = None if form == "apart" else results[0]
        single = [] if form == "joint" else results[len(shapes) - len(halves) : len(shapes)]

        for i, half in enumerate(views):
            total = None
            for b in range(count):
                part = jnp.dot(
                    left_ref[:, b * size : (b + 1) * size],
                    read(refs, half[b], size),
                    preferred_element_type=jnp.float32,
                )
                total = part if total is None else total + part
            total = total.astype(jnp.bfloat16)
            if joint is not None:
                joint[0:size, i * size : (i + 1) * size] = total
            if single:
                single[i][0:size, :] = total
        if not extra:
            return

        def pieces(b, k):
            here = slice(k * (size // 4), (k + 1) * (size // 4))
            near, end = (
                read(refs, kind[b], size, slice(size, tall))[:, here] for kind in (own_views, views[-1])
            )
            return jnp.concatenate([end, near, near, end], axis=1) * rest[0][...]

        applied = rest[0][...] if own is None else pieces(0, turn + 1).astype(jnp.float32)
        for b in range(count):
            if own is None:
                rows = read(refs, views[-1][b], size, slice(size, tall))
            else:
                rows = pieces(b, turn)
            applied = applied + lax.dot_general(
                rows, left_ref[:, b * size : (b + 1) * size], NT, preferred_element_type=jnp.float32
            )
        results[-1][...] = applied
        applied = applied.astype(jnp.bfloat16)
        if joint is not None:
            for i in range(len(halves)):
                joint[size:tall, i * size : (i + 1) * size] = applied
        if single:
            single[-1][size:tall, :] = applied

    return pl.pallas_call(
        kernel,
        out_shape=tuple(outs),
        compiler_params=pltpu.CompilerParams(vmem_limit_bytes=VMEM),
        cost_estimate=pl.CostEstimate(
            flops=2 * len(halves) * size * size * size * count,
            bytes_accessed=12 * len(halves) * size * size,
            transcendentals=0,
        ),
    )(left, *extra, *operands.arrays)


def after(value, *others):
    return lax.optimization_barrier((value, *others))[0]


def plain(*tiles):
    return [(tile, None, 0) for tile in tiles]


def shards(interval_blocks, interval_pivots, boundary_pivots, interval_residuals):
    blocks = interval_blocks[0]
    size, share = blocks.shape[1], interval_residuals.shape[2]
    row, col = lax.axis_index("row"), lax.axis_index("col")
    count = lax.axis_size("row")
    position = lax.axis_index("loop")
    positions = lax.axis_size("loop")

    own = lax.dynamic_index_in_dim(boundary_pivots, position, 0, keepdims=True)
    back = lax.dynamic_index_in_dim(
        boundary_pivots, (position + positions - 1) % positions, 0, keepdims=True
    )
    pivots = jnp.concatenate([interval_pivots[0], own, back], axis=0)
    pivots = (((pivots // size) ^ row) * size + pivots % size).reshape(pivots.shape[0], count, size)
    order = [
        lax.dynamic_index_in_dim(pivots, col ^ flip, 1, keepdims=True) for flip in (0, 1, 3, 2)
    ]
    pivots = jnp.concatenate(order, axis=1)
    places = lax.broadcasted_iota(jnp.int32, (1, size), 1)
    held = ((places < 2 * share) == (col == 1)).astype(jnp.bfloat16)
    pivots = [pivots[turn] for turn in range(5)]

    lefts = blocks[1::2]
    riding = jnp.broadcast_to(interval_residuals[0].reshape(1, -1), (EXTRA, size))
    tiles = [jnp.concatenate([blocks[k], riding], axis=0) for k in (0, 2)]
    rights = jnp.stack(tiles)
    lefts, rights, tiles, held, pivots = lax.optimization_barrier(
        (lefts, rights, tiles, held, pivots)
    )
    ends_left = inward(lefts)
    lefts_other = swap_middle(lefts)
    rights_across = swap_rows(rights, 2)
    end_lower = inward(tiles[0])
    end_upper = inward(tiles[1])
    rights_beside = swap_rows(rights, 1)

    def panel(turn, tiles, onto=None):
        return spread_columns(pivots[turn], tiles, size, count, onto)

    upper_panel, lower_panel = panel(2, [(0, (lefts, 1, 0))]), panel(0, [(0, (lefts, 0, 0))])
    ends_other = swap_middle(after(ends_left, upper_panel, lower_panel))
    rights_last = swap_rows(rights_across, 1)
    lower_panel = panel(0, [(1, (ends_left, 0, 0)), (2, (lefts_other, 0, 0))], lower_panel)
    upper_panel = panel(2, [(1, (ends_left, 1, 0)), (2, (lefts_other, 1, 0))], upper_panel)
    end_lower = after(end_lower, lower_panel, upper_panel)
    lower_across = swap_rows(end_lower, 2)
    lower_ends = [end_lower, swap_rows(end_lower, 1), lower_across, swap_rows(lower_across, 1)]
    upper_across = swap_rows(end_upper, 2)
    upper_ends = [end_upper, swap_rows(end_upper, 1), upper_across]
    lower_panel = panel(0, [(3, (ends_other, 0, 0))], lower_panel)
    upper_panel = panel(2, [(3, (ends_other, 1, 0))], upper_panel)

    def own_tiles(k):
        return [(tile, k, 0) for tile in (rights, rights_beside, rights_across, rights_last)]

    lower, _ = product(
        lower_panel, [own_tiles(0), plain(*lower_ends)], "joint", size, held, own_tiles(0), 0
    )
    upper_panel = after(upper_panel, lower)
    (upper_o,) = product(upper_panel, [own_tiles(1)], "apart", size)
    upper_ends.append(swap_rows(after(upper_across, upper_o), 1))
    upper_e, vector = product(
        upper_panel, [plain(*upper_ends)], "apart", size, held, own_tiles(1), 2
    )

    def right_views(right, tie):
        parts = []
        for tile in right:
            beside, across = swap_rows(tile, 1), swap_rows(tile, 2)
            parts.append([tile, beside, across, swap_rows(after(across, *tie), 1)])
        if len(parts) == 1:
            return [[(tile, None, column) for tile in parts[0]] for column in (0, size)]
        return [plain(*part) for part in parts]

    other_o, other_e = swap_middle(upper_o), swap_middle(upper_e)
    moved = panel(1, [(0, (upper_o, None, 0)), (1, (upper_e, None, 0))])
    moved = panel(1, [(2, (other_o, None, 0))], moved)
    views = right_views([lower], (moved, other_e))
    moved = panel(1, [(3, (other_e, None, 0))], moved)
    whole, whole_o, whole_e, vector = product(moved, views, "both", size, vector)

    def left_panel(turn, left):
        other = swap_middle(left)
        partial = panel(turn, [(0, (left, None, 0)), (1, (left, None, size))])
        return partial, panel(turn, [(2, (other, None, 0)), (3, (other, None, size))], partial)

    earlier = [from_behind(tile, "loop", 1) for tile in (whole_o, whole_e)]
    partial, moved = left_panel(3, whole)
    views = right_views(earlier, (partial,))
    halved, vector = product(moved, views, "joint", size, vector)
    partial, moved = left_panel(4, halved)
    views = right_views([from_behind(halved, "loop", 2)], (partial,))
    reduced_e, vector = product(moved, views[1:], "apart", size, vector)
    (reduced_o,) = product(after(moved, reduced_e), views[:1], "apart", size)

    middle = (col == 1) | (col == 2)
    block = jnp.where(middle, reduced_o, outward(reduced_e)[:size])
    vector = after(vector, reduced_o)[:1]
    vector = vector + swap_middle(vector)
    vector = jnp.where(middle, vector, outward(vector))
    return (block[None], lax.dynamic_slice_in_dim(vector, col * share, share, 1))


def solution(mesh):
    placed = (
        P("loop", None, "row", "col"),
        P("loop", None, None),
        P(),
        P("loop", None, ("row", "col")),
    )
    return jax.shard_map(
        shards,
        mesh=mesh,
        in_specs=placed,
        out_specs=(P("loop", "row", "col"), P("loop", ("row", "col"))),
        check_vma=False,
    )
```

```python
import jax
import jax.numpy as jnp
from jax import lax
from jax.experimental import pallas as pl
from jax.experimental.pallas import tpu as pltpu
from jax.sharding import PartitionSpec as P

EXTRA = 16
VMEM = 14 * 1024 * 1024
NT = (((1,), (1,)), ((), ()))


def from_behind(value, axis, by):
    devices = lax.axis_size(axis)
    if by % devices == 0:
        return value
    return lax.ppermute(value, axis, [(i, (i + by) % devices) for i in range(devices)])


def swap_rows(value, flip):
    rows, cols = lax.axis_size("row"), lax.axis_size("col")
    pairs = [(r * cols + c, (r ^ flip) * cols + c) for r in range(rows) for c in (1, 2)]
    return lax.ppermute(value, ("row", "col"), pairs)


def swap_middle(value):
    return lax.ppermute(value, "col", [(1, 2), (2, 1)])


def inward(value):
    return lax.ppermute(value, "col", [(0, 1), (3, 2)])


def outward(value):
    return lax.ppermute(value, "col", [(1, 0), (2, 3)])


class Operands:
    def __init__(self):
        self.arrays = []

    def add(self, view):
        array, lead, column = view
        for i, known in enumerate(self.arrays):
            if known is array:
                return i, lead, column
        self.arrays.append(array)
        return len(self.arrays) - 1, lead, column


def read(refs, view, size, rows=None):
    which, lead, column = view
    ref = refs[which] if lead is None else refs[which].at[lead]
    return ref[rows or slice(0, size), column : column + size]


def spread(refs, views, q_ref, size, n):
    total = None
    for block, view in views:
        at = lax.broadcasted_iota(jnp.int32, (size, size), 0) + n * size
        hot = jnp.where(at == q_ref[block : block + 1, :], 1.0, 0.0).astype(jnp.bfloat16)
        part = lax.dot_general(
            read(refs, view, size), hot, NT, preferred_element_type=jnp.float32
        )
        total = part if total is None else total + part
    return total


def spread_columns(pivots, tiles, size, count, onto=None):
    operands = Operands()
    views = [(block, operands.add(view)) for block, view in tiles]
    extra = [] if onto is None else [onto]

    def kernel(q_ref, *refs):
        out = refs[-1]

        @pl.loop(0, count)
        def _(n):
            here = pl.ds(pl.multiple_of(n * size, size), size)
            moved = spread(refs[len(extra) :], views, q_ref, size, n).astype(out.dtype)
            out[:, here] = moved if onto is None else moved + refs[0][:, here]

    return pl.pallas_call(
        kernel,
        out_shape=jax.ShapeDtypeStruct((size, size * count), jnp.bfloat16),
        compiler_params=pltpu.CompilerParams(vmem_limit_bytes=VMEM),
        cost_estimate=pl.CostEstimate(
            flops=2 * len(tiles) * size * size * size * count,
            bytes_accessed=8 * size * size,
            transcendentals=0,
        ),
    )(pivots, *extra, *operands.arrays)


def product(left, halves, form, size, added=None, own=None, turn=0):
    count = left.shape[1] // size
    operands = Operands()
    views = [[operands.add(view) for view in half] for half in halves]
    own_views = [operands.add(view) for view in own or []]
    extra = [] if added is None else [added]
    tall, wide = size + (EXTRA if extra else 0), size * len(halves)
    shapes = [] if form == "apart" else [(tall, wide)]
    if form != "joint":
        shapes += [(size, size)] * (len(halves) - 1) + [(tall, size)]
    outs = [jax.ShapeDtypeStruct(shape, jnp.bfloat16) for shape in shapes]
    if extra:
        outs.append(jax.ShapeDtypeStruct((EXTRA, size), jnp.float32))

    def kernel(left_ref, *rest):
        refs = rest[len(extra) : len(extra) + len(operands.arrays)]
        results = rest[len(extra) + len(refs) :]
        joint = None if form == "apart" else results[0]
        single = [] if form == "joint" else results[len(shapes) - len(halves) : len(shapes)]

        for i, half in enumerate(views):
            total = None
            for b in range(count):
                part = jnp.dot(
                    left_ref[:, b * size : (b + 1) * size],
                    read(refs, half[b], size),
                    preferred_element_type=jnp.float32,
                )
                total = part if total is None else total + part
            total = total.astype(jnp.bfloat16)
            if joint is not None:
                joint[0:size, i * size : (i + 1) * size] = total
            if single:
                single[i][0:size, :] = total
        if not extra:
            return

        def pieces(b, k):
            here = slice(k * (size // 4), (k + 1) * (size // 4))
            near, end = (
                read(refs, kind[b], size, slice(size, tall))[:, here] for kind in (own_views, views[-1])
            )
            return jnp.concatenate([end, near, near, end], axis=1) * rest[0][...]

        applied = rest[0][...] if own is None else pieces(0, turn + 1).astype(jnp.float32)
        for b in range(count):
            if own is None:
                rows = read(refs, views[-1][b], size, slice(size, tall))
            else:
                rows = pieces(b, turn)
            applied = applied + lax.dot_general(
                rows, left_ref[:, b * size : (b + 1) * size], NT, preferred_element_type=jnp.float32
            )
        results[-1][...] = applied
        applied = applied.astype(jnp.bfloat16)
        if joint is not None:
            for i in range(len(halves)):
                joint[size:tall, i * size : (i + 1) * size] = applied
        if single:
            single[-1][size:tall, :] = applied

    return pl.pallas_call(
        kernel,
        out_shape=tuple(outs),
        compiler_params=pltpu.CompilerParams(vmem_limit_bytes=VMEM),
        cost_estimate=pl.CostEstimate(
            flops=2 * len(halves) * size * size * size * count,
            bytes_accessed=12 * len(halves) * size * size,
            transcendentals=0,
        ),
    )(left, *extra, *operands.arrays)


def after(value, *others):
    return lax.optimization_barrier((value, *others))[0]


def plain(*tiles):
    return [(tile, None, 0) for tile in tiles]


def shards(interval_blocks, interval_pivots, boundary_pivots, interval_residuals):
    blocks = interval_blocks[0]
    size, share = blocks.shape[1], interval_residuals.shape[2]
    row, col = lax.axis_index("row"), lax.axis_index("col")
    count = lax.axis_size("row")
    position = lax.axis_index("loop")
    positions = lax.axis_size("loop")

    own = lax.dynamic_index_in_dim(boundary_pivots, position, 0, keepdims=True)
    back = lax.dynamic_index_in_dim(
        boundary_pivots, (position + positions - 1) % positions, 0, keepdims=True
    )
    pivots = jnp.concatenate([interval_pivots[0], own, back], axis=0)
    pivots = (((pivots // size) ^ row) * size + pivots % size).reshape(pivots.shape[0], count, size)
    order = [
        lax.dynamic_index_in_dim(pivots, col ^ flip, 1, keepdims=True) for flip in (0, 1, 3, 2)
    ]
    pivots = jnp.concatenate(order, axis=1)
    places = lax.broadcasted_iota(jnp.int32, (1, size), 1)
    held = ((places < 2 * share) == (col == 1)).astype(jnp.bfloat16)
    pivots = [pivots[turn] for turn in range(5)]

    lefts = blocks[1::2]
    riding = jnp.broadcast_to(interval_residuals[0].reshape(1, -1), (EXTRA, size))
    tiles = [jnp.concatenate([blocks[k], riding], axis=0) for k in (0, 2)]
    rights = jnp.stack(tiles)
    lefts, rights, tiles, held, pivots = lax.optimization_barrier(
        (lefts, rights, tiles, held, pivots)
    )
    ends_left = inward(lefts)
    lefts_other = swap_middle(lefts)
    rights_across = swap_rows(rights, 2)
    end_lower = inward(tiles[0])
    end_upper = inward(tiles[1])
    rights_beside = swap_rows(rights, 1)

    def panel(turn, tiles, onto=None):
        return spread_columns(pivots[turn], tiles, size, count, onto)

    upper_panel, lower_panel = panel(2, [(0, (lefts, 1, 0))]), panel(0, [(0, (lefts, 0, 0))])
    ends_other = swap_middle(after(ends_left, upper_panel, lower_panel))
    rights_last = swap_rows(rights_across, 1)
    lower_panel = panel(0, [(1, (ends_left, 0, 0)), (2, (lefts_other, 0, 0))], lower_panel)
    upper_panel = panel(2, [(1, (ends_left, 1, 0)), (2, (lefts_other, 1, 0))], upper_panel)
    end_lower = after(end_lower, lower_panel, upper_panel)
    lower_across = swap_rows(end_lower, 2)
    lower_ends = [end_lower, swap_rows(end_lower, 1), lower_across, swap_rows(lower_across, 1)]
    upper_across = swap_rows(end_upper, 2)
    upper_ends = [end_upper, swap_rows(end_upper, 1), upper_across]
    lower_panel = panel(0, [(3, (ends_other, 0, 0))], lower_panel)
    upper_panel = panel(2, [(3, (ends_other, 1, 0))], upper_panel)

    def own_tiles(k):
        return [(tile, k, 0) for tile in (rights, rights_beside, rights_across, rights_last)]

    lower, _ = product(
        lower_panel, [own_tiles(0), plain(*lower_ends)], "joint", size, held, own_tiles(0), 0
    )
    upper_panel = after(upper_panel, lower)
    (upper_o,) = product(upper_panel, [own_tiles(1)], "apart", size)
    upper_ends.append(swap_rows(after(upper_across, upper_o), 1))
    upper_e, vector = product(
        upper_panel, [plain(*upper_ends)], "apart", size, held, own_tiles(1), 2
    )

    def right_views(right, tie):
        parts = []
        for tile in right:
            beside, across = swap_rows(tile, 1), swap_rows(tile, 2)
            parts.append([tile, beside, across, swap_rows(after(across, *tie), 1)])
        if len(parts) == 1:
            return [[(tile, None, column) for tile in parts[0]] for column in (0, size)]
        return [plain(*part) for part in parts]

    other_o, other_e = swap_middle(upper_o), swap_middle(upper_e)
    moved = panel(1, [(0, (upper_o, None, 0)), (1, (upper_e, None, 0))])
    moved = panel(1, [(2, (other_o, None, 0))], moved)
    views = right_views([lower], (moved, other_e))
    moved = panel(1, [(3, (other_e, None, 0))], moved)
    whole, whole_o, whole_e, vector = product(moved, views, "both", size, vector)

    def tile_row(tile, across, last_tie):
        return plain(tile, swap_rows(tile, 1), across, swap_rows(after(across, last_tie), 1))

    earlier_e, earlier_o = from_behind(whole_e, "loop", 1), from_behind(whole_o, "loop", 1)
    other = swap_middle(whole)
    across_e, across_o = swap_rows(earlier_e, 2), swap_rows(earlier_o, 2)
    partial = panel(3, [(0, (whole, None, 0)), (1, (whole, None, size))])
    views = tile_row(earlier_e, across_e, partial)
    moved = panel(3, [(2, (other, None, 0)), (3, (other, None, size))], partial)
    views_o = tile_row(earlier_o, across_o, moved)
    halved_e, vector = product(moved, [views], "apart", size, vector)
    (halved_o,) = product(after(moved, halved_e), [views_o], "apart", size)

    distant_e, distant_o = from_behind(halved_e, "loop", 2), from_behind(halved_o, "loop", 2)
    other_e, across_e = swap_middle(halved_e), swap_rows(distant_e, 2)
    other_o, across_o = swap_middle(halved_o), swap_rows(distant_o, 2)
    partial = panel(4, [(0, (halved_o, None, 0)), (1, (halved_e, None, 0))])
    views = tile_row(distant_e, across_e, partial)
    partial = panel(4, [(3, (other_e, None, 0))], partial)
    views_o = tile_row(distant_o, across_o, partial)
    moved = panel(4, [(2, (other_o, None, 0))], partial)
    reduced_e, vector = product(moved, [views], "apart", size, vector)
    (reduced_o,) = product(after(moved, reduced_e), [views_o], "apart", size)

    middle = (col == 1) | (col == 2)
    block = jnp.where(middle, reduced_o, outward(reduced_e)[:size])
    vector = after(vector, reduced_o)[:1]
    vector = vector + swap_middle(vector)
    vector = jnp.where(middle, vector, outward(vector))
    return (block[None], lax.dynamic_slice_in_dim(vector, col * share, share, 1))


def solution(mesh):
    placed = (
        P("loop", None, "row", "col"),
        P("loop", None, None),
        P(),
        P("loop", None, ("row", "col")),
    )
    return jax.shard_map(
        shards,
        mesh=mesh,
        in_specs=placed,
        out_specs=(P("loop", "row", "col"), P("loop", ("row", "col"))),
        check_vma=False,
    )
```

```python
import jax
import jax.numpy as jnp
from jax import lax
from jax.experimental import pallas as pl
from jax.experimental.pallas import tpu as pltpu
from jax.sharding import PartitionSpec as P

EXTRA = 16
VMEM = 14 * 1024 * 1024
NT = (((1,), (1,)), ((), ()))


def from_behind(value, axis, by):
    devices = lax.axis_size(axis)
    if by % devices == 0:
        return value
    return lax.ppermute(value, axis, [(i, (i + by) % devices) for i in range(devices)])


def swap_rows(value, flip):
    rows, cols = lax.axis_size("row"), lax.axis_size("col")
    pairs = [(r * cols + c, (r ^ flip) * cols + c) for r in range(rows) for c in (1, 2)]
    return lax.ppermute(value, ("row", "col"), pairs)


def swap_middle(value):
    return lax.ppermute(value, "col", [(1, 2), (2, 1)])


def inward(value):
    return lax.ppermute(value, "col", [(0, 1), (3, 2)])


def outward(value):
    return lax.ppermute(value, "col", [(1, 0), (2, 3)])


class Operands:
    def __init__(self):
        self.arrays = []

    def add(self, view):
        array, lead, column = view
        for i, known in enumerate(self.arrays):
            if known is array:
                return i, lead, column
        self.arrays.append(array)
        return len(self.arrays) - 1, lead, column


def read(refs, view, size, rows=None):
    which, lead, column = view
    ref = refs[which] if lead is None else refs[which].at[lead]
    return ref[rows or slice(0, size), column : column + size]


def spread(refs, views, q_ref, size, n):
    total = None
    for block, view in views:
        at = lax.broadcasted_iota(jnp.int32, (size, size), 0) + n * size
        hot = jnp.where(at == q_ref[block : block + 1, :], 1.0, 0.0).astype(jnp.bfloat16)
        part = lax.dot_general(
            read(refs, view, size), hot, NT, preferred_element_type=jnp.float32
        )
        total = part if total is None else total + part
    return total


def spread_columns(pivots, tiles, size, count, onto=None, weight=1):
    operands = Operands()
    views = [(block, operands.add(view)) for block, view in tiles]
    extra = [] if onto is None else [onto]

    def kernel(q_ref, *refs):
        out = refs[-1]

        @pl.loop(0, count)
        def _(n):
            here = pl.ds(pl.multiple_of(n * size, size), size)
            moved = spread(refs[len(extra) :], views, q_ref, size, n).astype(out.dtype)
            out[:, here] = moved if onto is None else moved + refs[0][:, here]

    return pl.pallas_call(
        kernel,
        out_shape=jax.ShapeDtypeStruct((size, size * count), jnp.bfloat16),
        compiler_params=pltpu.CompilerParams(vmem_limit_bytes=VMEM),
        cost_estimate=pl.CostEstimate(
            flops=2 * weight * len(tiles) * size * size * size * count,
            bytes_accessed=8 * weight * size * size,
            transcendentals=0,
        ),
    )(pivots, *extra, *operands.arrays)


def product(left, halves, form, size, added=None, own=None, turn=0, weight=1):
    count = left.shape[1] // size
    operands = Operands()
    views = [[operands.add(view) for view in half] for half in halves]
    own_views = [operands.add(view) for view in own or []]
    extra = [] if added is None else [added]
    tall, wide = size + (EXTRA if extra else 0), size * len(halves)
    kind = jnp.float32 if form == "open" else jnp.bfloat16
    shapes = {"joint": [(tall, wide)], "apart": [(tall, size)], "open": [(size, size)]}[form]
    outs = [jax.ShapeDtypeStruct(shape, kind) for shape in shapes]
    if extra:
        outs.append(jax.ShapeDtypeStruct((EXTRA, size), jnp.float32))

    def kernel(left_ref, *rest):
        refs = rest[len(extra) : len(extra) + len(operands.arrays)]
        results = rest[len(extra) + len(refs) :]
        for i, half in enumerate(views):
            total = None
            for b in range(count):
                part = jnp.dot(
                    left_ref[:, b * size : (b + 1) * size],
                    read(refs, half[b], size),
                    preferred_element_type=jnp.float32,
                )
                total = part if total is None else total + part
            results[0][0:size, i * size : (i + 1) * size] = total.astype(kind)
        if not extra:
            return

        def pieces(b, k):
            here = slice(k * (size // 4), (k + 1) * (size // 4))
            near, end = (
                read(refs, kind[b], size, slice(size, tall))[:, here] for kind in (own_views, views[-1])
            )
            return jnp.concatenate([end, near, near, end], axis=1) * rest[0][...]

        applied = rest[0][...] if own is None else pieces(0, turn + 1).astype(jnp.float32)
        for b in range(count):
            if own is None:
                rows = read(refs, views[-1][b], size, slice(size, tall))
            else:
                rows = pieces(b, turn)
            applied = applied + lax.dot_general(
                rows, left_ref[:, b * size : (b + 1) * size], NT, preferred_element_type=jnp.float32
            )
        results[-1][...] = applied
        if form != "open":
            for i in range(len(halves)):
                results[0][size:tall, i * size : (i + 1) * size] = applied.astype(kind)

    return pl.pallas_call(
        kernel,
        out_shape=tuple(outs),
        compiler_params=pltpu.CompilerParams(vmem_limit_bytes=VMEM),
        cost_estimate=pl.CostEstimate(
            flops=2 * weight * len(halves) * size * size * size * count,
            bytes_accessed=12 * weight * len(halves) * size * size,
            transcendentals=0,
        ),
    )(left, *extra, *operands.arrays)


def call(kernel, flops, outs, *operands):
    return pl.pallas_call(
        kernel,
        out_shape=outs,
        compiler_params=pltpu.CompilerParams(vmem_limit_bytes=VMEM),
        cost_estimate=pl.CostEstimate(flops=flops, bytes_accessed=1 << 20, transcendentals=0),
    )(*operands)


def early(value, weight=20):
    def kernel(value_ref, out):
        del value_ref, out

    return pl.pallas_call(
        kernel,
        out_shape=jax.ShapeDtypeStruct(value.shape, value.dtype),
        in_specs=[pl.BlockSpec(memory_space=pl.ANY)],
        out_specs=pl.BlockSpec(memory_space=pl.ANY),
        input_output_aliases={0: 0},
        cost_estimate=pl.CostEstimate(flops=weight << 30, bytes_accessed=0, transcendentals=0),
    )(value)


def beside_each_other(left, right):
    size = left.shape[1]

    def kernel(left_ref, right_ref, out):
        out[:, 0:size] = left_ref[0:size, :]
        out[:, size : 2 * size] = right_ref[0:size, :]

    return call(kernel, 1, jax.ShapeDtypeStruct((size, 2 * size), left.dtype), left, right)


def pick_rows(pivots, block, tiles):
    size = tiles[0].shape[1]

    def kernel(q_ref, *refs):
        out = refs[-1]
        rows, places = None, None
        named = jnp.transpose(jnp.broadcast_to(q_ref[block : block + 1, :], (size, size)))
        for b, ref in enumerate(refs[:-1]):
            at = lax.broadcasted_iota(jnp.int32, (size, size), 1) + b * size
            hot = jnp.where(at == named, 1.0, 0.0).astype(jnp.bfloat16)
            part = jnp.dot(hot, ref[0:size, :], preferred_element_type=jnp.float32)
            rows = part if rows is None else rows + part
            part = lax.dot_general(
                ref[size : size + EXTRA, :], hot, NT, preferred_element_type=jnp.float32
            )
            places = part if places is None else places + part
        out[0:size, :] = rows.astype(out.dtype)
        out[size : size + EXTRA, :] = places.astype(out.dtype)

    flops = 2 * size * size * size * len(tiles)
    return call(kernel, flops, jax.ShapeDtypeStruct(tiles[0].shape, tiles[0].dtype), pivots, *tiles)


def finish(left, picked, base, applied):
    size = left.shape[1]

    def kernel(left_ref, picked_ref, base_ref, applied_ref, out, vector):
        part = jnp.dot(left_ref[...], picked_ref[0:size, :], preferred_element_type=jnp.float32)
        out[...] = (base_ref[...] + part).astype(out.dtype)
        vector[...] = applied_ref[...] + lax.dot_general(
            picked_ref[size : size + EXTRA, :], left_ref[...], NT, preferred_element_type=jnp.float32
        )

    outs = (
        jax.ShapeDtypeStruct((size, size), jnp.bfloat16),
        jax.ShapeDtypeStruct(applied.shape, applied.dtype),
    )
    return call(kernel, 2 * size * size * size, outs, left, picked, base, applied)


def after(value, *others):
    return lax.optimization_barrier((value, *others))[0]


def plain(*tiles):
    return [(tile, None, 0) for tile in tiles]


def shards(interval_blocks, interval_pivots, boundary_pivots, interval_residuals):
    blocks = interval_blocks[0]
    size, share = blocks.shape[1], interval_residuals.shape[2]
    row, col = lax.axis_index("row"), lax.axis_index("col")
    count = lax.axis_size("row")
    position = lax.axis_index("loop")
    positions = lax.axis_size("loop")

    own = lax.dynamic_index_in_dim(boundary_pivots, position, 0, keepdims=True)
    back = lax.dynamic_index_in_dim(
        boundary_pivots, (position + positions - 1) % positions, 0, keepdims=True
    )
    pivots = jnp.concatenate([interval_pivots[0], own, back], axis=0)
    pivots = (((pivots // size) ^ row) * size + pivots % size).reshape(pivots.shape[0], count, size)
    order = [
        lax.dynamic_index_in_dim(pivots, col ^ flip, 1, keepdims=True) for flip in (0, 1, 3, 2)
    ]
    pivots = jnp.concatenate(order, axis=1)
    places = lax.broadcasted_iota(jnp.int32, (1, size), 1)
    held = ((places < 2 * share) == (col == 1)).astype(jnp.bfloat16)
    pivots = [pivots[turn] for turn in range(5)]

    lefts = blocks[1::2]
    riding = jnp.broadcast_to(interval_residuals[0].reshape(1, -1), (EXTRA, size))
    tiles = [jnp.concatenate([blocks[k], riding], axis=0) for k in (0, 2)]
    rights = jnp.stack(tiles)
    lefts, rights, tiles, held, pivots = lax.optimization_barrier(
        (lefts, rights, tiles, held, pivots)
    )
    ends_left = inward(lefts)
    lefts_other = swap_middle(lefts)
    rights_across = swap_rows(rights, 2)
    end_lower = inward(tiles[0])
    end_upper = inward(tiles[1])
    rights_beside = swap_rows(rights, 1)

    def panel(turn, tiles, onto=None, weight=1):
        return spread_columns(pivots[turn], tiles, size, count, onto, weight)

    upper_panel, lower_panel = panel(2, [(0, (lefts, 1, 0))]), panel(0, [(0, (lefts, 0, 0))])
    ends_other = swap_middle(after(ends_left, upper_panel, lower_panel))
    rights_last = swap_rows(rights_across, 1)
    lower_panel = panel(0, [(1, (ends_left, 0, 0)), (2, (lefts_other, 0, 0))], lower_panel)
    upper_panel = panel(2, [(1, (ends_left, 1, 0)), (2, (lefts_other, 1, 0))], upper_panel)
    end_lower = after(end_lower, lower_panel, upper_panel)
    lower_across = swap_rows(end_lower, 2)
    lower_ends = [end_lower, swap_rows(end_lower, 1), lower_across, swap_rows(lower_across, 1)]
    upper_across = swap_rows(end_upper, 2)
    upper_ends = [end_upper, swap_rows(end_upper, 1), upper_across]
    lower_panel = panel(0, [(3, (ends_other, 0, 0))], lower_panel)
    upper_panel = panel(2, [(3, (ends_other, 1, 0))], upper_panel)

    def own_tiles(k):
        return [(tile, k, 0) for tile in (rights, rights_beside, rights_across, rights_last)]

    lower, _ = product(
        lower_panel, [own_tiles(0), plain(*lower_ends)], "joint", size, held, own_tiles(0), 0
    )
    upper_panel = after(upper_panel, lower)
    (upper_o,) = product(upper_panel, [own_tiles(1)], "apart", size)
    upper_ends.append(swap_rows(after(upper_across, upper_o), 1))
    upper_e, vector = product(
        upper_panel, [plain(*upper_ends)], "apart", size, held, own_tiles(1), 2
    )

    def right_views(right, tie):
        parts = []
        for tile in right:
            beside, across = swap_rows(tile, 1), swap_rows(tile, 2)
            parts.append([tile, beside, across, swap_rows(after(across, *tie), 1)])
        if len(parts) == 1:
            return [[(tile, None, column) for tile in parts[0]] for column in (0, size)]
        return [plain(*part) for part in parts]

    other_o, other_e = swap_middle(upper_o), swap_middle(upper_e)
    moved = panel(1, [(0, (upper_o, None, 0)), (1, (upper_e, None, 0))])
    moved = panel(1, [(2, (other_o, None, 0))], moved)
    views = right_views([lower], (moved, other_e))
    moved = panel(1, [(3, (other_e, None, 0))], moved)
    whole_e, vector = product(moved, views[1:], "apart", size, vector)
    (whole_o,) = product(after(moved, whole_e), views[:1], "apart", size)
    whole = beside_each_other(whole_o, whole_e)

    def tile_row(tile, across, *last_ties):
        return plain(tile, swap_rows(tile, 1), across, swap_rows(after(across, *last_ties), 1))

    earlier_e, earlier_o = from_behind(whole_e, "loop", 1), from_behind(whole_o, "loop", 1)
    other = swap_middle(whole)
    across_e, across_o = swap_rows(earlier_e, 2), swap_rows(earlier_o, 2)
    partial = panel(3, [(0, (whole, None, 0)), (1, (whole, None, size))])
    views = tile_row(earlier_e, across_e, partial)
    moved = panel(3, [(2, (other, None, 0)), (3, (other, None, size))], partial)
    views_o = tile_row(earlier_o, across_o, moved)
    halved_e, vector = product(moved, [views], "apart", size, vector)
    (halved_o,) = product(after(moved, halved_e), [views_o], "apart", size)

    distant_e, distant_o = from_behind(halved_e, "loop", 2), from_behind(halved_o, "loop", 2)
    other_e, across_e = early(swap_middle(halved_e)), early(swap_rows(distant_e, 2))
    other_o, across_o = swap_middle(halved_o), swap_rows(distant_o, 2)
    partial = panel(4, [(0, (halved_o, None, 0)), (1, (halved_e, None, 0))])
    views = tile_row(distant_e, across_e, partial)
    partial = panel(4, [(3, (other_e, None, 0))], partial)
    base, applied = product(partial, [views], "open", size, vector)
    picked = pick_rows(pivots[4], 2, [view[0] for view in views])
    views_o = tile_row(distant_o, across_o, base, picked)
    other_o = early(after(other_o, base, picked))
    reduced_e, vector = finish(other_o, picked, base, applied)
    moved = panel(4, [(2, (other_o, None, 0))], after(partial, reduced_e), 0)
    (reduced_o,) = product(moved, [views_o], "apart", size, weight=0)

    middle = (col == 1) | (col == 2)
    block = jnp.where(middle, reduced_o, outward(reduced_e))
    vector = after(vector, reduced_o)[:1]
    vector = vector + swap_middle(vector)
    vector = jnp.where(middle, vector, outward(vector))
    return (block[None], lax.dynamic_slice_in_dim(vector, col * share, share, 1))


def solution(mesh):
    placed = (
        P("loop", None, "row", "col"),
        P("loop", None, None),
        P(),
        P("loop", None, ("row", "col")),
    )
    return jax.shard_map(
        shards,
        mesh=mesh,
        in_specs=placed,
        out_specs=(P("loop", "row", "col"), P("loop", ("row", "col"))),
        check_vma=False,
    )
```

```python
import jax
import jax.numpy as jnp
from jax import lax
from jax.experimental import pallas as pl
from jax.experimental.pallas import tpu as pltpu
from jax.sharding import PartitionSpec as P

EXTRA = 16
VMEM = 14 * 1024 * 1024
NT = (((1,), (1,)), ((), ()))


def from_behind(value, axis, by):
    devices = lax.axis_size(axis)
    if by % devices == 0:
        return value
    return lax.ppermute(value, axis, [(i, (i + by) % devices) for i in range(devices)])


def swap_rows(value, flip):
    rows, cols = lax.axis_size("row"), lax.axis_size("col")
    pairs = [(r * cols + c, (r ^ flip) * cols + c) for r in range(rows) for c in (1, 2)]
    return lax.ppermute(value, ("row", "col"), pairs)


def swap_middle(value):
    return lax.ppermute(value, "col", [(1, 2), (2, 1)])


def inward(value):
    return lax.ppermute(value, "col", [(0, 1), (3, 2)])


def outward(value):
    return lax.ppermute(value, "col", [(1, 0), (2, 3)])


class Operands:
    def __init__(self):
        self.arrays = []

    def add(self, view):
        array, lead, column = view
        for i, known in enumerate(self.arrays):
            if known is array:
                return i, lead, column
        self.arrays.append(array)
        return len(self.arrays) - 1, lead, column


def read(refs, view, size, rows=None):
    which, lead, column = view
    ref = refs[which] if lead is None else refs[which].at[lead]
    return ref[rows or slice(0, size), column : column + size]


def spread(refs, views, q_ref, size, n):
    total = None
    for block, view in views:
        at = lax.broadcasted_iota(jnp.int32, (size, size), 0) + n * size
        hot = jnp.where(at == q_ref[block : block + 1, :], 1.0, 0.0).astype(jnp.bfloat16)
        part = lax.dot_general(
            read(refs, view, size), hot, NT, preferred_element_type=jnp.float32
        )
        total = part if total is None else total + part
    return total


def spread_columns(pivots, tiles, size, count, onto=None, weight=1):
    operands = Operands()
    views = [(block, operands.add(view)) for block, view in tiles]
    extra = [] if onto is None else [onto]

    def kernel(q_ref, *refs):
        out = refs[-1]

        @pl.loop(0, count)
        def _(n):
            here = pl.ds(pl.multiple_of(n * size, size), size)
            moved = spread(refs[len(extra) :], views, q_ref, size, n).astype(out.dtype)
            out[:, here] = moved if onto is None else moved + refs[0][:, here]

    return pl.pallas_call(
        kernel,
        out_shape=jax.ShapeDtypeStruct((size, size * count), jnp.bfloat16),
        compiler_params=pltpu.CompilerParams(vmem_limit_bytes=VMEM),
        cost_estimate=pl.CostEstimate(
            flops=2 * weight * len(tiles) * size * size * size * count,
            bytes_accessed=8 * weight * size * size,
            transcendentals=0,
        ),
    )(pivots, *extra, *operands.arrays)


def product(left, halves, form, size, added=None, own=None, turn=0, weight=1):
    count = left.shape[1] // size
    operands = Operands()
    views = [[operands.add(view) for view in half] for half in halves]
    own_views = [operands.add(view) for view in own or []]
    extra = [] if added is None else [added]
    tall, wide = size + (EXTRA if extra else 0), size * len(halves)
    kind = jnp.float32 if form == "open" else jnp.bfloat16
    shapes = {"joint": [(tall, wide)], "apart": [(tall, size)], "open": [(size, size)]}[form]
    outs = [jax.ShapeDtypeStruct(shape, kind) for shape in shapes]
    if extra:
        outs.append(jax.ShapeDtypeStruct((EXTRA, size), jnp.float32))

    def kernel(left_ref, *rest):
        refs = rest[len(extra) : len(extra) + len(operands.arrays)]
        results = rest[len(extra) + len(refs) :]
        for i, half in enumerate(views):
            total = None
            for b in range(count):
                part = jnp.dot(
                    left_ref[:, b * size : (b + 1) * size],
                    read(refs, half[b], size),
                    preferred_element_type=jnp.float32,
                )
                total = part if total is None else total + part
            results[0][0:size, i * size : (i + 1) * size] = total.astype(kind)
        if not extra:
            return

        def pieces(b, k):
            here = slice(k * (size // 4), (k + 1) * (size // 4))
            near, end = (
                read(refs, kind[b], size, slice(size, tall))[:, here] for kind in (own_views, views[-1])
            )
            return jnp.concatenate([end, near, near, end], axis=1) * rest[0][...]

        applied = rest[0][...] if own is None else pieces(0, turn + 1).astype(jnp.float32)
        for b in range(count):
            if own is None:
                rows = read(refs, views[-1][b], size, slice(size, tall))
            else:
                rows = pieces(b, turn)
            applied = applied + lax.dot_general(
                rows, left_ref[:, b * size : (b + 1) * size], NT, preferred_element_type=jnp.float32
            )
        results[-1][...] = applied
        if form != "open":
            for i in range(len(halves)):
                results[0][size:tall, i * size : (i + 1) * size] = applied.astype(kind)

    return pl.pallas_call(
        kernel,
        out_shape=tuple(outs),
        compiler_params=pltpu.CompilerParams(vmem_limit_bytes=VMEM),
        cost_estimate=pl.CostEstimate(
            flops=2 * weight * len(halves) * size * size * size * count,
            bytes_accessed=12 * weight * len(halves) * size * size,
            transcendentals=0,
        ),
    )(left, *extra, *operands.arrays)


def call(kernel, flops, outs, *operands):
    return pl.pallas_call(
        kernel,
        out_shape=outs,
        compiler_params=pltpu.CompilerParams(vmem_limit_bytes=VMEM),
        cost_estimate=pl.CostEstimate(flops=flops, bytes_accessed=1 << 20, transcendentals=0),
    )(*operands)


def early(value, weight=20):
    def kernel(value_ref, out):
        del value_ref, out

    return pl.pallas_call(
        kernel,
        out_shape=jax.ShapeDtypeStruct(value.shape, value.dtype),
        in_specs=[pl.BlockSpec(memory_space=pl.ANY)],
        out_specs=pl.BlockSpec(memory_space=pl.ANY),
        input_output_aliases={0: 0},
        compiler_params=pltpu.CompilerParams(vmem_limit_bytes=1024 * 1024),
        cost_estimate=pl.CostEstimate(flops=weight << 30, bytes_accessed=0, transcendentals=0),
    )(value)


def beside_each_other(left, right):
    size = left.shape[1]

    def kernel(left_ref, right_ref, out):
        out[:, 0:size] = left_ref[0:size, :]
        out[:, size : 2 * size] = right_ref[0:size, :]

    return call(kernel, 1, jax.ShapeDtypeStruct((size, 2 * size), left.dtype), left, right)


def pick_rows(pivots, block, tiles):
    size = tiles[0].shape[1]

    def kernel(q_ref, *refs):
        out = refs[-1]
        rows, places = None, None
        named = jnp.transpose(jnp.broadcast_to(q_ref[block : block + 1, :], (size, size)))
        for b, ref in enumerate(refs[:-1]):
            at = lax.broadcasted_iota(jnp.int32, (size, size), 1) + b * size
            hot = jnp.where(at == named, 1.0, 0.0).astype(jnp.bfloat16)
            part = jnp.dot(hot, ref[0:size, :], preferred_element_type=jnp.float32)
            rows = part if rows is None else rows + part
            part = lax.dot_general(
                ref[size : size + EXTRA, :], hot, NT, preferred_element_type=jnp.float32
            )
            places = part if places is None else places + part
        out[0:size, :] = rows.astype(out.dtype)
        out[size : size + EXTRA, :] = places.astype(out.dtype)

    flops = 2 * size * size * size * len(tiles)
    return call(kernel, flops, jax.ShapeDtypeStruct(tiles[0].shape, tiles[0].dtype), pivots, *tiles)


def finish(left, picked, base, applied):
    size = left.shape[1]

    def kernel(left_ref, picked_ref, base_ref, applied_ref, out, vector):
        part = jnp.dot(left_ref[...], picked_ref[0:size, :], preferred_element_type=jnp.float32)
        out[...] = (base_ref[...] + part).astype(out.dtype)
        vector[...] = applied_ref[...] + lax.dot_general(
            picked_ref[size : size + EXTRA, :], left_ref[...], NT, preferred_element_type=jnp.float32
        )

    outs = (
        jax.ShapeDtypeStruct((size, size), jnp.bfloat16),
        jax.ShapeDtypeStruct(applied.shape, applied.dtype),
    )
    return call(kernel, 2 * size * size * size, outs, left, picked, base, applied)


def after(value, *others):
    return lax.optimization_barrier((value, *others))[0]


def plain(*tiles):
    return [(tile, None, 0) for tile in tiles]


def shards(interval_blocks, interval_pivots, boundary_pivots, interval_residuals):
    blocks = interval_blocks[0]
    size, share = blocks.shape[1], interval_residuals.shape[2]
    row, col = lax.axis_index("row"), lax.axis_index("col")
    count = lax.axis_size("row")
    position = lax.axis_index("loop")
    positions = lax.axis_size("loop")

    own = lax.dynamic_index_in_dim(boundary_pivots, position, 0, keepdims=True)
    back = lax.dynamic_index_in_dim(
        boundary_pivots, (position + positions - 1) % positions, 0, keepdims=True
    )
    pivots = jnp.concatenate([interval_pivots[0], own, back], axis=0)
    pivots = (((pivots // size) ^ row) * size + pivots % size).reshape(pivots.shape[0], count, size)
    order = [
        lax.dynamic_index_in_dim(pivots, col ^ flip, 1, keepdims=True) for flip in (0, 1, 3, 2)
    ]
    pivots = jnp.concatenate(order, axis=1)
    places = lax.broadcasted_iota(jnp.int32, (1, size), 1)
    held = ((places < 2 * share) == (col == 1)).astype(jnp.bfloat16)
    pivots = [pivots[turn] for turn in range(5)]

    lefts = blocks[1::2]
    riding = jnp.broadcast_to(interval_residuals[0].reshape(1, -1), (EXTRA, size))
    tiles = [jnp.concatenate([blocks[k], riding], axis=0) for k in (0, 2)]
    rights = jnp.stack(tiles)
    lefts, rights, tiles, held, pivots = lax.optimization_barrier(
        (lefts, rights, tiles, held, pivots)
    )
    ends_left = inward(lefts)
    lefts_other = swap_middle(lefts)
    rights_across = swap_rows(rights, 2)
    end_lower = inward(tiles[0])
    end_upper = inward(tiles[1])
    rights_beside = swap_rows(rights, 1)

    def panel(turn, tiles, onto=None, weight=1):
        return spread_columns(pivots[turn], tiles, size, count, onto, weight)

    upper_panel, lower_panel = panel(2, [(0, (lefts, 1, 0))]), panel(0, [(0, (lefts, 0, 0))])
    ends_other = swap_middle(after(ends_left, upper_panel, lower_panel))
    rights_last = swap_rows(rights_across, 1)
    lower_panel = panel(0, [(1, (ends_left, 0, 0)), (2, (lefts_other, 0, 0))], lower_panel)
    upper_panel = panel(2, [(1, (ends_left, 1, 0)), (2, (lefts_other, 1, 0))], upper_panel)
    end_lower = after(end_lower, lower_panel, upper_panel)
    lower_across = swap_rows(end_lower, 2)
    lower_ends = [end_lower, swap_rows(end_lower, 1), lower_across, swap_rows(lower_across, 1)]
    upper_across = swap_rows(end_upper, 2)
    upper_ends = [end_upper, swap_rows(end_upper, 1), upper_across]
    lower_panel = panel(0, [(3, (ends_other, 0, 0))], lower_panel)
    upper_panel = panel(2, [(3, (ends_other, 1, 0))], upper_panel)

    def own_tiles(k):
        return [(tile, k, 0) for tile in (rights, rights_beside, rights_across, rights_last)]

    lower, _ = product(
        lower_panel, [own_tiles(0), plain(*lower_ends)], "joint", size, held, own_tiles(0), 0
    )
    upper_panel = after(upper_panel, lower)
    (upper_o,) = product(upper_panel, [own_tiles(1)], "apart", size)
    upper_ends.append(swap_rows(after(upper_across, upper_o), 1))
    upper_e, vector = product(
        upper_panel, [plain(*upper_ends)], "apart", size, held, own_tiles(1), 2
    )

    def right_views(right, tie):
        parts = []
        for tile in right:
            beside, across = swap_rows(tile, 1), swap_rows(tile, 2)
            parts.append([tile, beside, across, swap_rows(after(across, *tie), 1)])
        if len(parts) == 1:
            return [[(tile, None, column) for tile in parts[0]] for column in (0, size)]
        return [plain(*part) for part in parts]

    other_o, other_e = swap_middle(upper_o), swap_middle(upper_e)
    moved = panel(1, [(0, (upper_o, None, 0)), (1, (upper_e, None, 0))])
    moved = panel(1, [(2, (other_o, None, 0))], moved)
    views = right_views([lower], (moved, other_e))
    moved = panel(1, [(3, (other_e, None, 0))], moved)
    whole_e, vector = product(moved, views[1:], "apart", size, vector)
    (whole_o,) = product(after(moved, whole_e), views[:1], "apart", size)
    whole = beside_each_other(whole_o, whole_e)

    def tile_row(tile, across, *last_ties):
        return plain(tile, swap_rows(tile, 1), across, swap_rows(after(across, *last_ties), 1))

    earlier_e, earlier_o = from_behind(whole_e, "loop", 1), from_behind(whole_o, "loop", 1)
    other = swap_middle(whole)
    across_e, across_o = swap_rows(earlier_e, 2), swap_rows(earlier_o, 2)
    partial = panel(3, [(0, (whole, None, 0)), (1, (whole, None, size))])
    views = tile_row(earlier_e, across_e, partial)
    moved = panel(3, [(2, (other, None, 0)), (3, (other, None, size))], partial)
    views_o = tile_row(earlier_o, across_o, moved)
    halved_e, vector = product(moved, [views], "apart", size, vector)
    (halved_o,) = product(after(moved, halved_e), [views_o], "apart", size)

    distant_e, distant_o = from_behind(halved_e, "loop", 2), from_behind(halved_o, "loop", 2)
    other_e, across_e = early(swap_middle(halved_e)), early(swap_rows(distant_e, 2))
    other_o, across_o = swap_middle(halved_o), swap_rows(distant_o, 2)
    partial = panel(4, [(0, (halved_o, None, 0)), (1, (halved_e, None, 0))])
    views = tile_row(distant_e, across_e, partial)
    partial = panel(4, [(3, (other_e, None, 0))], partial)
    base, applied = product(partial, [views], "open", size, vector)
    picked = pick_rows(pivots[4], 2, [view[0] for view in views])
    views_o = tile_row(distant_o, across_o, base, picked)
    other_o = early(after(other_o, base, picked))
    reduced_e, vector = finish(other_o, picked, base, applied)
    moved = panel(4, [(2, (other_o, None, 0))], after(partial, reduced_e), 0)
    (reduced_o,) = product(moved, [views_o], "apart", size, weight=0)

    middle = (col == 1) | (col == 2)
    block = jnp.where(middle, reduced_o, outward(reduced_e))
    vector = after(vector, reduced_o)[:1]
    vector = vector + swap_middle(vector)
    vector = jnp.where(middle, vector, outward(vector))
    return (block[None], lax.dynamic_slice_in_dim(vector, col * share, share, 1))


def solution(mesh):
    placed = (
        P("loop", None, "row", "col"),
        P("loop", None, None),
        P(),
        P("loop", None, ("row", "col")),
    )
    return jax.shard_map(
        shards,
        mesh=mesh,
        in_specs=placed,
        out_specs=(P("loop", "row", "col"), P("loop", ("row", "col"))),
        check_vma=False,
    )
```

```python
import jax
import jax.numpy as jnp
from jax import lax
from jax.experimental import pallas as pl
from jax.experimental.pallas import tpu as pltpu
from jax.sharding import PartitionSpec as P

EXTRA = 16
VMEM = 14 * 1024 * 1024
NT = (((1,), (1,)), ((), ()))


def from_behind(value, axis, by):
    devices = lax.axis_size(axis)
    if by % devices == 0:
        return value
    return lax.ppermute(value, axis, [(i, (i + by) % devices) for i in range(devices)])


def swap_rows(value, flip):
    rows, cols = lax.axis_size("row"), lax.axis_size("col")
    pairs = [(r * cols + c, (r ^ flip) * cols + c) for r in range(rows) for c in (1, 2)]
    return lax.ppermute(value, ("row", "col"), pairs)


def swap_middle(value):
    return lax.ppermute(value, "col", [(1, 2), (2, 1)])


def inward(value):
    return lax.ppermute(value, "col", [(0, 1), (3, 2)])


def outward(value):
    return lax.ppermute(value, "col", [(1, 0), (2, 3)])


class Operands:
    def __init__(self):
        self.arrays = []

    def add(self, view):
        array, lead, column = view
        for i, known in enumerate(self.arrays):
            if known is array:
                return i, lead, column
        self.arrays.append(array)
        return len(self.arrays) - 1, lead, column


def read(refs, view, size, rows=None):
    which, lead, column = view
    ref = refs[which] if lead is None else refs[which].at[lead]
    return ref[rows or slice(0, size), column : column + size]


def spread(refs, views, q_ref, size, n):
    total = None
    for block, view in views:
        at = lax.broadcasted_iota(jnp.int32, (size, size), 0) + n * size
        hot = jnp.where(at == q_ref[block : block + 1, :], 1.0, 0.0).astype(jnp.bfloat16)
        part = lax.dot_general(
            read(refs, view, size), hot, NT, preferred_element_type=jnp.float32
        )
        total = part if total is None else total + part
    return total


def spread_columns(pivots, tiles, size, count, onto=None, weight=1):
    operands = Operands()
    views = [(block, operands.add(view)) for block, view in tiles]
    extra = [] if onto is None else [onto]

    def kernel(q_ref, *refs):
        out = refs[-1]

        @pl.loop(0, count)
        def _(n):
            here = pl.ds(pl.multiple_of(n * size, size), size)
            moved = spread(refs[len(extra) :], views, q_ref, size, n).astype(out.dtype)
            out[:, here] = moved if onto is None else moved + refs[0][:, here]

    return pl.pallas_call(
        kernel,
        out_shape=jax.ShapeDtypeStruct((size, size * count), jnp.bfloat16),
        compiler_params=pltpu.CompilerParams(vmem_limit_bytes=VMEM),
        cost_estimate=pl.CostEstimate(
            flops=2 * weight * len(tiles) * size * size * size * count,
            bytes_accessed=8 * weight * size * size,
            transcendentals=0,
        ),
    )(pivots, *extra, *operands.arrays)


def product(left, halves, form, size, added=None, own=None, turn=0, weight=1):
    count = left.shape[1] // size
    operands = Operands()
    views = [[operands.add(view) for view in half] for half in halves]
    own_views = [operands.add(view) for view in own or []]
    extra = [] if added is None else [added]
    tall, wide = size + (EXTRA if extra else 0), size * len(halves)
    kind = jnp.float32 if form == "open" else jnp.bfloat16
    shapes = {"joint": [(tall, wide)], "apart": [(tall, size)], "open": [(size, size)]}[form]
    outs = [jax.ShapeDtypeStruct(shape, kind) for shape in shapes]
    if extra:
        outs.append(jax.ShapeDtypeStruct((EXTRA, size), jnp.float32))

    def kernel(left_ref, *rest):
        refs = rest[len(extra) : len(extra) + len(operands.arrays)]
        results = rest[len(extra) + len(refs) :]
        for i, half in enumerate(views):
            total = None
            for b in range(count):
                part = jnp.dot(
                    left_ref[:, b * size : (b + 1) * size],
                    read(refs, half[b], size),
                    preferred_element_type=jnp.float32,
                )
                total = part if total is None else total + part
            results[0][0:size, i * size : (i + 1) * size] = total.astype(kind)
        if not extra:
            return

        def pieces(b, k):
            here = slice(k * (size // 4), (k + 1) * (size // 4))
            near, end = (
                read(refs, kind[b], size, slice(size, tall))[:, here] for kind in (own_views, views[-1])
            )
            return jnp.concatenate([end, near, near, end], axis=1) * rest[0][...]

        applied = rest[0][...] if own is None else pieces(0, turn + 1).astype(jnp.float32)
        for b in range(count):
            if own is None:
                rows = read(refs, views[-1][b], size, slice(size, tall))
            else:
                rows = pieces(b, turn)
            applied = applied + lax.dot_general(
                rows, left_ref[:, b * size : (b + 1) * size], NT, preferred_element_type=jnp.float32
            )
        results[-1][...] = applied
        if form != "open":
            for i in range(len(halves)):
                results[0][size:tall, i * size : (i + 1) * size] = applied.astype(kind)

    return pl.pallas_call(
        kernel,
        out_shape=tuple(outs),
        compiler_params=pltpu.CompilerParams(vmem_limit_bytes=VMEM),
        cost_estimate=pl.CostEstimate(
            flops=2 * weight * len(halves) * size * size * size * count,
            bytes_accessed=12 * weight * len(halves) * size * size,
            transcendentals=0,
        ),
    )(left, *extra, *operands.arrays)


def call(kernel, flops, outs, *operands):
    return pl.pallas_call(
        kernel,
        out_shape=outs,
        compiler_params=pltpu.CompilerParams(vmem_limit_bytes=VMEM),
        cost_estimate=pl.CostEstimate(flops=flops, bytes_accessed=1 << 20, transcendentals=0),
    )(*operands)


def early(value, weight=20):
    def kernel(value_ref, out):
        del value_ref, out

    return pl.pallas_call(
        kernel,
        out_shape=jax.ShapeDtypeStruct(value.shape, value.dtype),
        in_specs=[pl.BlockSpec(memory_space=pl.ANY)],
        out_specs=pl.BlockSpec(memory_space=pl.ANY),
        input_output_aliases={0: 0},
        compiler_params=pltpu.CompilerParams(vmem_limit_bytes=1024 * 1024),
        cost_estimate=pl.CostEstimate(flops=weight << 30, bytes_accessed=0, transcendentals=0),
    )(value)


def beside_each_other(left, right):
    size = left.shape[1]

    def kernel(left_ref, right_ref, out):
        out[:, 0:size] = left_ref[0:size, :]
        out[:, size : 2 * size] = right_ref[0:size, :]

    return call(kernel, 1, jax.ShapeDtypeStruct((size, 2 * size), left.dtype), left, right)


def pick_rows(pivots, block, tiles):
    size = tiles[0].shape[1]

    def kernel(q_ref, *refs):
        out = refs[-1]
        rows, places = None, None
        named = jnp.transpose(jnp.broadcast_to(q_ref[block : block + 1, :], (size, size)))
        for b, ref in enumerate(refs[:-1]):
            at = lax.broadcasted_iota(jnp.int32, (size, size), 1) + b * size
            hot = jnp.where(at == named, 1.0, 0.0).astype(jnp.bfloat16)
            part = jnp.dot(hot, ref[0:size, :], preferred_element_type=jnp.float32)
            rows = part if rows is None else rows + part
            part = lax.dot_general(
                ref[size : size + EXTRA, :], hot, NT, preferred_element_type=jnp.float32
            )
            places = part if places is None else places + part
        out[0:size, :] = rows.astype(out.dtype)
        out[size : size + EXTRA, :] = places.astype(out.dtype)

    flops = 2 * size * size * size * len(tiles)
    return call(kernel, flops, jax.ShapeDtypeStruct(tiles[0].shape, tiles[0].dtype), pivots, *tiles)


def finish(left, picked, base, applied):
    size = left.shape[1]

    def kernel(left_ref, picked_ref, base_ref, applied_ref, out, vector):
        part = jnp.dot(left_ref[...], picked_ref[0:size, :], preferred_element_type=jnp.float32)
        out[...] = (base_ref[...] + part).astype(out.dtype)
        vector[...] = applied_ref[...] + lax.dot_general(
            picked_ref[size : size + EXTRA, :], left_ref[...], NT, preferred_element_type=jnp.float32
        )

    outs = (
        jax.ShapeDtypeStruct((size, size), jnp.bfloat16),
        jax.ShapeDtypeStruct(applied.shape, applied.dtype),
    )
    return call(kernel, 2 * size * size * size, outs, left, picked, base, applied)


def after(value, *others):
    return lax.optimization_barrier((value, *others))[0]


def plain(*tiles):
    return [(tile, None, 0) for tile in tiles]


def shards(interval_blocks, interval_pivots, boundary_pivots, interval_residuals):
    blocks = interval_blocks[0]
    size, share = blocks.shape[1], interval_residuals.shape[2]
    row, col = lax.axis_index("row"), lax.axis_index("col")
    count = lax.axis_size("row")
    position = lax.axis_index("loop")
    positions = lax.axis_size("loop")

    own = lax.dynamic_index_in_dim(boundary_pivots, position, 0, keepdims=True)
    back = lax.dynamic_index_in_dim(
        boundary_pivots, (position + positions - 1) % positions, 0, keepdims=True
    )
    pivots = jnp.concatenate([interval_pivots[0], own, back], axis=0)
    pivots = (((pivots // size) ^ row) * size + pivots % size).reshape(pivots.shape[0], count, size)
    order = [
        lax.dynamic_index_in_dim(pivots, col ^ flip, 1, keepdims=True) for flip in (0, 1, 3, 2)
    ]
    pivots = jnp.concatenate(order, axis=1)
    places = lax.broadcasted_iota(jnp.int32, (1, size), 1)
    held = ((places < 2 * share) == (col == 1)).astype(jnp.bfloat16)
    pivots = [pivots[turn] for turn in range(5)]

    lefts = blocks[1::2]
    riding = jnp.broadcast_to(interval_residuals[0].reshape(1, -1), (EXTRA, size))
    tiles = [jnp.concatenate([blocks[k], riding], axis=0) for k in (0, 2)]
    rights = jnp.stack(tiles)
    lefts, rights, tiles, held, pivots = lax.optimization_barrier(
        (lefts, rights, tiles, held, pivots)
    )
    ends_left = inward(lefts)
    lefts_other = swap_middle(lefts)
    rights_across = swap_rows(rights, 2)
    end_lower = inward(tiles[0])
    end_upper = inward(tiles[1])
    rights_beside = swap_rows(rights, 1)

    def panel(turn, tiles, onto=None, weight=1):
        return spread_columns(pivots[turn], tiles, size, count, onto, weight)

    upper_panel, lower_panel = panel(2, [(0, (lefts, 1, 0))]), panel(0, [(0, (lefts, 0, 0))])
    ends_other = swap_middle(after(ends_left, upper_panel, lower_panel))
    rights_last = swap_rows(rights_across, 1)
    lower_panel = panel(0, [(1, (ends_left, 0, 0)), (2, (lefts_other, 0, 0))], lower_panel)
    upper_panel = panel(2, [(1, (ends_left, 1, 0)), (2, (lefts_other, 1, 0))], upper_panel)
    end_lower = after(end_lower, lower_panel, upper_panel)
    lower_across = swap_rows(end_lower, 2)
    lower_ends = [end_lower, swap_rows(end_lower, 1), lower_across, swap_rows(lower_across, 1)]
    upper_across = swap_rows(end_upper, 2)
    upper_ends = [end_upper, swap_rows(end_upper, 1), upper_across]
    lower_panel = panel(0, [(3, (ends_other, 0, 0))], lower_panel)
    upper_panel = panel(2, [(3, (ends_other, 1, 0))], upper_panel)

    def own_tiles(k):
        return [(tile, k, 0) for tile in (rights, rights_beside, rights_across, rights_last)]

    lower, _ = product(
        lower_panel, [own_tiles(0), plain(*lower_ends)], "joint", size, held, own_tiles(0), 0
    )
    upper_panel = after(upper_panel, lower)
    (upper_o,) = product(upper_panel, [own_tiles(1)], "apart", size)
    upper_ends.append(swap_rows(after(upper_across, upper_o), 1))
    upper_e, vector = product(
        upper_panel, [plain(*upper_ends)], "apart", size, held, own_tiles(1), 2
    )

    def right_views(right, tie):
        parts = []
        for tile in right:
            beside, across = swap_rows(tile, 1), swap_rows(tile, 2)
            parts.append([tile, beside, across, swap_rows(after(across, *tie), 1)])
        if len(parts) == 1:
            return [[(tile, None, column) for tile in parts[0]] for column in (0, size)]
        return [plain(*part) for part in parts]

    other_o, other_e = swap_middle(upper_o), swap_middle(upper_e)
    moved = panel(1, [(0, (upper_o, None, 0)), (1, (upper_e, None, 0))])
    moved = panel(1, [(2, (other_o, None, 0))], moved)
    views = right_views([lower], (moved, other_e))
    moved = panel(1, [(3, (other_e, None, 0))], moved)
    whole_e, vector = product(moved, views[1:], "apart", size, vector)
    (whole_o,) = product(after(moved, whole_e), views[:1], "apart", size)
    whole = beside_each_other(whole_o, whole_e)

    def tile_row(tile, across, *last_ties):
        return plain(tile, swap_rows(tile, 1), across, swap_rows(after(across, *last_ties), 1))

    earlier_e, earlier_o = from_behind(whole_e, "loop", 1), from_behind(whole_o, "loop", 1)
    other = swap_middle(whole)
    partial = panel(3, [(0, (whole, None, 0)), (1, (whole, None, size))])
    earlier_e = after(earlier_e, partial)
    across_e, across_o = swap_rows(earlier_e, 2), swap_rows(earlier_o, 2)
    views = tile_row(earlier_e, across_e, partial)
    moved = panel(3, [(2, (other, None, 0)), (3, (other, None, size))], partial)
    views_o = tile_row(earlier_o, across_o, moved)
    halved_e, vector = product(moved, [views], "apart", size, vector)
    (halved_o,) = product(after(moved, halved_e), [views_o], "apart", size)

    distant_e, distant_o = from_behind(halved_e, "loop", 2), from_behind(halved_o, "loop", 2)
    other_e, across_e = early(swap_middle(halved_e)), early(swap_rows(distant_e, 2))
    other_o, across_o = swap_middle(halved_o), swap_rows(distant_o, 2)
    partial = panel(4, [(0, (halved_o, None, 0)), (1, (halved_e, None, 0))])
    views = tile_row(after(distant_e, partial), across_e, partial)
    partial = panel(4, [(3, (other_e, None, 0))], partial)
    base, applied = product(partial, [views], "open", size, vector)
    picked = pick_rows(pivots[4], 2, [view[0] for view in views])
    views_o = tile_row(distant_o, across_o, base, picked)
    other_o = early(after(other_o, base, picked))
    reduced_e, vector = finish(other_o, picked, base, applied)
    moved = panel(4, [(2, (other_o, None, 0))], after(partial, reduced_e), 0)
    (reduced_o,) = product(moved, [views_o], "apart", size, weight=0)

    middle = (col == 1) | (col == 2)
    block = jnp.where(middle, reduced_o, outward(reduced_e))
    vector = after(vector, reduced_o)[:1]
    vector = vector + swap_middle(vector)
    vector = jnp.where(middle, vector, outward(vector))
    return (block[None], lax.dynamic_slice_in_dim(vector, col * share, share, 1))


def solution(mesh):
    placed = (
        P("loop", None, "row", "col"),
        P("loop", None, None),
        P(),
        P("loop", None, ("row", "col")),
    )
    return jax.shard_map(
        shards,
        mesh=mesh,
        in_specs=placed,
        out_specs=(P("loop", "row", "col"), P("loop", ("row", "col"))),
        check_vma=False,
    )
```

```python
import jax
import jax.numpy as jnp
from jax import lax
from jax.experimental import pallas as pl
from jax.experimental.pallas import tpu as pltpu
from jax.sharding import PartitionSpec as P

EXTRA = 16
VMEM = 14 * 1024 * 1024
NT = (((1,), (1,)), ((), ()))


def from_behind(value, axis, by):
    devices = lax.axis_size(axis)
    if by % devices == 0:
        return value
    return lax.ppermute(value, axis, [(i, (i + by) % devices) for i in range(devices)])


def swap_rows(value, flip):
    rows, cols = lax.axis_size("row"), lax.axis_size("col")
    pairs = [(r * cols + c, (r ^ flip) * cols + c) for r in range(rows) for c in (1, 2)]
    return lax.ppermute(value, ("row", "col"), pairs)


def swap_middle(value):
    return lax.ppermute(value, "col", [(1, 2), (2, 1)])


def inward(value):
    return lax.ppermute(value, "col", [(0, 1), (3, 2)])


def outward(value):
    return lax.ppermute(value, "col", [(1, 0), (2, 3)])


class Operands:
    def __init__(self):
        self.arrays = []

    def add(self, view):
        array, lead, column = view
        for i, known in enumerate(self.arrays):
            if known is array:
                return i, lead, column
        self.arrays.append(array)
        return len(self.arrays) - 1, lead, column


def read(refs, view, size, rows=None):
    which, lead, column = view
    ref = refs[which] if lead is None else refs[which].at[lead]
    return ref[rows or slice(0, size), column : column + size]


def spread(refs, views, q_ref, size, n):
    total = None
    for block, view in views:
        at = lax.broadcasted_iota(jnp.int32, (size, size), 0) + n * size
        hot = jnp.where(at == q_ref[block : block + 1, :], 1.0, 0.0).astype(jnp.bfloat16)
        part = lax.dot_general(
            read(refs, view, size), hot, NT, preferred_element_type=jnp.float32
        )
        total = part if total is None else total + part
    return total


def spread_columns(pivots, tiles, size, count, onto=None, weight=1):
    operands = Operands()
    views = [(block, operands.add(view)) for block, view in tiles]
    extra = [] if onto is None else [onto]

    def kernel(q_ref, *refs):
        out = refs[-1]

        @pl.loop(0, count)
        def _(n):
            here = pl.ds(pl.multiple_of(n * size, size), size)
            moved = spread(refs[len(extra) :], views, q_ref, size, n).astype(out.dtype)
            out[:, here] = moved if onto is None else moved + refs[0][:, here]

    return pl.pallas_call(
        kernel,
        out_shape=jax.ShapeDtypeStruct((size, size * count), jnp.bfloat16),
        compiler_params=pltpu.CompilerParams(vmem_limit_bytes=VMEM),
        cost_estimate=pl.CostEstimate(
            flops=2 * weight * len(tiles) * size * size * size * count,
            bytes_accessed=8 * weight * size * size,
            transcendentals=0,
        ),
    )(pivots, *extra, *operands.arrays)


def product(left, halves, form, size, added=None, own=None, turn=0, weight=1):
    count = left.shape[1] // size
    operands = Operands()
    views = [[operands.add(view) for view in half] for half in halves]
    own_views = [operands.add(view) for view in own or []]
    extra = [] if added is None else [added]
    tall, wide = size + (EXTRA if extra else 0), size * len(halves)
    kind = jnp.float32 if form == "open" else jnp.bfloat16
    shapes = {"joint": [(tall, wide)], "apart": [(tall, size)], "open": [(size, size)]}[form]
    outs = [jax.ShapeDtypeStruct(shape, kind) for shape in shapes]
    if extra:
        outs.append(jax.ShapeDtypeStruct((EXTRA, size), jnp.float32))

    def kernel(left_ref, *rest):
        refs = rest[len(extra) : len(extra) + len(operands.arrays)]
        results = rest[len(extra) + len(refs) :]
        for i, half in enumerate(views):
            total = None
            for b in range(count):
                part = jnp.dot(
                    left_ref[:, b * size : (b + 1) * size],
                    read(refs, half[b], size),
                    preferred_element_type=jnp.float32,
                )
                total = part if total is None else total + part
            results[0][0:size, i * size : (i + 1) * size] = total.astype(kind)
        if not extra:
            return

        def pieces(b, k):
            here = slice(k * (size // 4), (k + 1) * (size // 4))
            near, end = (
                read(refs, kind[b], size, slice(size, tall))[:, here] for kind in (own_views, views[-1])
            )
            return jnp.concatenate([end, near, near, end], axis=1) * rest[0][...]

        applied = rest[0][...] if own is None else pieces(0, turn + 1).astype(jnp.float32)
        for b in range(count):
            if own is None:
                rows = read(refs, views[-1][b], size, slice(size, tall))
            else:
                rows = pieces(b, turn)
            applied = applied + lax.dot_general(
                rows, left_ref[:, b * size : (b + 1) * size], NT, preferred_element_type=jnp.float32
            )
        results[-1][...] = applied
        if form != "open":
            for i in range(len(halves)):
                results[0][size:tall, i * size : (i + 1) * size] = applied.astype(kind)

    return pl.pallas_call(
        kernel,
        out_shape=tuple(outs),
        compiler_params=pltpu.CompilerParams(vmem_limit_bytes=VMEM),
        cost_estimate=pl.CostEstimate(
            flops=2 * weight * len(halves) * size * size * size * count,
            bytes_accessed=12 * weight * len(halves) * size * size,
            transcendentals=0,
        ),
    )(left, *extra, *operands.arrays)


def call(kernel, flops, outs, *operands):
    return pl.pallas_call(
        kernel,
        out_shape=outs,
        compiler_params=pltpu.CompilerParams(vmem_limit_bytes=VMEM),
        cost_estimate=pl.CostEstimate(flops=flops, bytes_accessed=1 << 20, transcendentals=0),
    )(*operands)


def early(value, weight=20):
    def kernel(value_ref, out):
        del value_ref, out

    return pl.pallas_call(
        kernel,
        out_shape=jax.ShapeDtypeStruct(value.shape, value.dtype),
        in_specs=[pl.BlockSpec(memory_space=pl.ANY)],
        out_specs=pl.BlockSpec(memory_space=pl.ANY),
        input_output_aliases={0: 0},
        compiler_params=pltpu.CompilerParams(vmem_limit_bytes=1024 * 1024),
        cost_estimate=pl.CostEstimate(flops=weight << 30, bytes_accessed=0, transcendentals=0),
    )(value)


def beside_each_other(left, right):
    size = left.shape[1]

    def kernel(left_ref, right_ref, out):
        out[:, 0:size] = left_ref[0:size, :]
        out[:, size : 2 * size] = right_ref[0:size, :]

    return call(kernel, 1, jax.ShapeDtypeStruct((size, 2 * size), left.dtype), left, right)


def pick_rows(pivots, block, tiles):
    size = tiles[0].shape[1]

    def kernel(q_ref, *refs):
        out = refs[-1]
        rows, places = None, None
        named = jnp.transpose(jnp.broadcast_to(q_ref[block : block + 1, :], (size, size)))
        for b, ref in enumerate(refs[:-1]):
            at = lax.broadcasted_iota(jnp.int32, (size, size), 1) + b * size
            hot = jnp.where(at == named, 1.0, 0.0).astype(jnp.bfloat16)
            part = jnp.dot(hot, ref[0:size, :], preferred_element_type=jnp.float32)
            rows = part if rows is None else rows + part
            part = lax.dot_general(
                ref[size : size + EXTRA, :], hot, NT, preferred_element_type=jnp.float32
            )
            places = part if places is None else places + part
        out[0:size, :] = rows.astype(out.dtype)
        out[size : size + EXTRA, :] = places.astype(out.dtype)

    flops = 2 * size * size * size * len(tiles)
    return call(kernel, flops, jax.ShapeDtypeStruct(tiles[0].shape, tiles[0].dtype), pivots, *tiles)


def finish(left, picked, base, applied):
    size = left.shape[1]

    def kernel(left_ref, picked_ref, base_ref, applied_ref, out, vector):
        part = jnp.dot(left_ref[...], picked_ref[0:size, :], preferred_element_type=jnp.float32)
        out[...] = (base_ref[...] + part).astype(out.dtype)
        vector[...] = applied_ref[...] + lax.dot_general(
            picked_ref[size : size + EXTRA, :], left_ref[...], NT, preferred_element_type=jnp.float32
        )

    outs = (
        jax.ShapeDtypeStruct((size, size), jnp.bfloat16),
        jax.ShapeDtypeStruct(applied.shape, applied.dtype),
    )
    return call(kernel, 2 * size * size * size, outs, left, picked, base, applied)


def after(value, *others):
    return lax.optimization_barrier((value, *others))[0]


def plain(*tiles):
    return [(tile, None, 0) for tile in tiles]


def shards(interval_blocks, interval_pivots, boundary_pivots, interval_residuals):
    blocks = interval_blocks[0]
    size, share = blocks.shape[1], interval_residuals.shape[2]
    row, col = lax.axis_index("row"), lax.axis_index("col")
    count = lax.axis_size("row")
    position = lax.axis_index("loop")
    positions = lax.axis_size("loop")

    own = lax.dynamic_index_in_dim(boundary_pivots, position, 0, keepdims=True)
    back = lax.dynamic_index_in_dim(
        boundary_pivots, (position + positions - 1) % positions, 0, keepdims=True
    )
    pivots = jnp.concatenate([interval_pivots[0], own, back], axis=0)
    pivots = (((pivots // size) ^ row) * size + pivots % size).reshape(pivots.shape[0], count, size)
    order = [
        lax.dynamic_index_in_dim(pivots, col ^ flip, 1, keepdims=True) for flip in (0, 1, 3, 2)
    ]
    pivots = jnp.concatenate(order, axis=1)
    places = lax.broadcasted_iota(jnp.int32, (1, size), 1)
    held = ((places < 2 * share) == (col == 1)).astype(jnp.bfloat16)
    pivots = [pivots[turn] for turn in range(5)]

    lefts = blocks[1::2]
    riding = jnp.broadcast_to(interval_residuals[0].reshape(1, -1), (EXTRA, size))
    tiles = [jnp.concatenate([blocks[k], riding], axis=0) for k in (0, 2)]
    rights = jnp.stack(tiles)
    lefts, rights, tiles, held, pivots = lax.optimization_barrier(
        (lefts, rights, tiles, held, pivots)
    )
    ends_left = inward(lefts)
    lefts_other = swap_middle(lefts)
    rights_across = swap_rows(rights, 2)
    end_lower = inward(tiles[0])
    end_upper = inward(tiles[1])
    rights_beside = swap_rows(rights, 1)

    def panel(turn, tiles, onto=None, weight=1):
        return spread_columns(pivots[turn], tiles, size, count, onto, weight)

    upper_panel, lower_panel = panel(2, [(0, (lefts, 1, 0))]), panel(0, [(0, (lefts, 0, 0))])
    ends_other = swap_middle(after(ends_left, upper_panel, lower_panel))
    rights_last = swap_rows(rights_across, 1)
    lower_panel = panel(0, [(1, (ends_left, 0, 0)), (2, (lefts_other, 0, 0))], lower_panel)
    upper_panel = panel(2, [(1, (ends_left, 1, 0)), (2, (lefts_other, 1, 0))], upper_panel)
    end_lower = after(end_lower, lower_panel, upper_panel)
    lower_across = swap_rows(end_lower, 2)
    lower_ends = [end_lower, swap_rows(end_lower, 1), lower_across, swap_rows(lower_across, 1)]
    upper_across = swap_rows(end_upper, 2)
    upper_ends = [end_upper, swap_rows(end_upper, 1), upper_across]
    lower_panel = panel(0, [(3, (ends_other, 0, 0))], lower_panel)
    upper_panel = panel(2, [(3, (ends_other, 1, 0))], upper_panel)

    def own_tiles(k):
        return [(tile, k, 0) for tile in (rights, rights_beside, rights_across, rights_last)]

    lower, _ = product(
        lower_panel, [own_tiles(0), plain(*lower_ends)], "joint", size, held, own_tiles(0), 0
    )
    upper_panel = after(upper_panel, lower)
    (upper_o,) = product(upper_panel, [own_tiles(1)], "apart", size)
    upper_ends.append(swap_rows(after(upper_across, upper_o), 1))
    upper_e, vector = product(
        upper_panel, [plain(*upper_ends)], "apart", size, held, own_tiles(1), 2
    )

    def right_views(right, tie):
        parts = []
        for tile in right:
            beside, across = swap_rows(tile, 1), early(swap_rows(tile, 2), 6)
            parts.append([tile, beside, across, swap_rows(after(across, *tie), 1)])
        if len(parts) == 1:
            return [[(tile, None, column) for tile in parts[0]] for column in (0, size)]
        return [plain(*part) for part in parts]

    other_o, other_e = early(swap_middle(upper_o), 4), swap_middle(upper_e)
    moved = panel(1, [(0, (upper_o, None, 0)), (1, (upper_e, None, 0))])
    moved = panel(1, [(2, (other_o, None, 0))], moved)
    views = right_views([lower], (moved, other_e))
    moved = panel(1, [(3, (other_e, None, 0))], moved)
    whole_e, vector = product(moved, views[1:], "apart", size, vector)
    (whole_o,) = product(after(moved, whole_e), views[:1], "apart", size)
    whole = beside_each_other(whole_o, whole_e)

    def tile_row(tile, across, *last_ties):
        return plain(tile, swap_rows(tile, 1), across, swap_rows(after(across, *last_ties), 1))

    earlier_e, earlier_o = from_behind(whole_e, "loop", 1), from_behind(whole_o, "loop", 1)
    other = swap_middle(whole)
    partial = panel(3, [(0, (whole, None, 0)), (1, (whole, None, size))])
    earlier_e = after(earlier_e, partial)
    across_e, across_o = swap_rows(earlier_e, 2), swap_rows(earlier_o, 2)
    views = tile_row(earlier_e, across_e, partial)
    moved = panel(3, [(2, (other, None, 0)), (3, (other, None, size))], partial)
    views_o = tile_row(earlier_o, across_o, moved)
    halved_e, vector = product(moved, [views], "apart", size, vector)
    (halved_o,) = product(after(moved, halved_e), [views_o], "apart", size)

    distant_e, distant_o = from_behind(halved_e, "loop", 2), from_behind(halved_o, "loop", 2)
    other_e, across_e = early(swap_middle(halved_e)), swap_rows(distant_e, 2)
    other_o, across_o = swap_middle(halved_o), swap_rows(distant_o, 2)
    partial = panel(4, [(0, (halved_o, None, 0)), (1, (halved_e, None, 0))])
    views = tile_row(after(distant_e, partial), across_e, partial)
    partial = panel(4, [(3, (other_e, None, 0))], partial)
    base, applied = product(partial, [views], "open", size, vector)
    picked = pick_rows(pivots[4], 2, [view[0] for view in views])
    views_o = tile_row(distant_o, across_o, base, picked)
    other_o = early(after(other_o, base, picked))
    reduced_e, vector = finish(other_o, picked, base, applied)
    moved = panel(4, [(2, (other_o, None, 0))], after(partial, reduced_e), 0)
    (reduced_o,) = product(moved, [views_o], "apart", size, weight=0)

    middle = (col == 1) | (col == 2)
    block = jnp.where(middle, reduced_o, outward(reduced_e))
    vector = after(vector, reduced_o)[:1]
    vector = vector + swap_middle(vector)
    vector = jnp.where(middle, vector, outward(vector))
    return (block[None], lax.dynamic_slice_in_dim(vector, col * share, share, 1))


def solution(mesh):
    placed = (
        P("loop", None, "row", "col"),
        P("loop", None, None),
        P(),
        P("loop", None, ("row", "col")),
    )
    return jax.shard_map(
        shards,
        mesh=mesh,
        in_specs=placed,
        out_specs=(P("loop", "row", "col"), P("loop", ("row", "col"))),
        check_vma=False,
    )
```

```python
import jax
import jax.numpy as jnp
from jax import lax
from jax.experimental import pallas as pl
from jax.experimental.pallas import tpu as pltpu
from jax.sharding import PartitionSpec as P

EXTRA = 16
VMEM = 14 * 1024 * 1024
NT = (((1,), (1,)), ((), ()))


def from_behind(value, axis, by):
    devices = lax.axis_size(axis)
    if by % devices == 0:
        return value
    return lax.ppermute(value, axis, [(i, (i + by) % devices) for i in range(devices)])


def swap_rows(value, flip):
    rows, cols = lax.axis_size("row"), lax.axis_size("col")
    pairs = [(r * cols + c, (r ^ flip) * cols + c) for r in range(rows) for c in (1, 2)]
    return lax.ppermute(value, ("row", "col"), pairs)


def swap_middle(value):
    return lax.ppermute(value, "col", [(1, 2), (2, 1)])


def inward(value):
    return lax.ppermute(value, "col", [(0, 1), (3, 2)])


def outward(value):
    return lax.ppermute(value, "col", [(1, 0), (2, 3)])


class Operands:
    def __init__(self):
        self.arrays = []

    def add(self, view):
        array, lead, column = view
        for i, known in enumerate(self.arrays):
            if known is array:
                return i, lead, column
        self.arrays.append(array)
        return len(self.arrays) - 1, lead, column


def read(refs, view, size, rows=None):
    which, lead, column = view
    ref = refs[which] if lead is None else refs[which].at[lead]
    return ref[rows or slice(0, size), column : column + size]


def spread(refs, views, q_ref, size, n):
    total = None
    for block, view in views:
        at = lax.broadcasted_iota(jnp.int32, (size, size), 0) + n * size
        hot = jnp.where(at == q_ref[block : block + 1, :], 1.0, 0.0).astype(jnp.bfloat16)
        part = lax.dot_general(
            read(refs, view, size), hot, NT, preferred_element_type=jnp.float32
        )
        total = part if total is None else total + part
    return total


def spread_columns(pivots, tiles, size, count, onto=None, weight=1):
    operands = Operands()
    views = [(block, operands.add(view)) for block, view in tiles]
    extra = [] if onto is None else [onto]

    def kernel(q_ref, *refs):
        out = refs[-1]

        @pl.loop(0, count)
        def _(n):
            here = pl.ds(pl.multiple_of(n * size, size), size)
            moved = spread(refs[len(extra) :], views, q_ref, size, n).astype(out.dtype)
            out[:, here] = moved if onto is None else moved + refs[0][:, here]

    return pl.pallas_call(
        kernel,
        out_shape=jax.ShapeDtypeStruct((size, size * count), jnp.bfloat16),
        compiler_params=pltpu.CompilerParams(vmem_limit_bytes=VMEM),
        cost_estimate=pl.CostEstimate(
            flops=2 * weight * len(tiles) * size * size * size * count,
            bytes_accessed=8 * weight * size * size,
            transcendentals=0,
        ),
    )(pivots, *extra, *operands.arrays)


def product(left, halves, form, size, added=None, own=None, turn=0, weight=1):
    count = left.shape[1] // size
    operands = Operands()
    views = [[operands.add(view) for view in half] for half in halves]
    own_views = [operands.add(view) for view in own or []]
    extra = [] if added is None else [added]
    tall, wide = size + (EXTRA if extra else 0), size * len(halves)
    kind = jnp.float32 if form == "open" else jnp.bfloat16
    shapes = {"joint": [(tall, wide)], "apart": [(tall, size)], "open": [(size, size)]}[form]
    outs = [jax.ShapeDtypeStruct(shape, kind) for shape in shapes]
    if extra:
        outs.append(jax.ShapeDtypeStruct((EXTRA, size), jnp.float32))

    def kernel(left_ref, *rest):
        refs = rest[len(extra) : len(extra) + len(operands.arrays)]
        results = rest[len(extra) + len(refs) :]
        for i, half in enumerate(views):
            total = None
            for b in range(count):
                part = jnp.dot(
                    left_ref[:, b * size : (b + 1) * size],
                    read(refs, half[b], size),
                    preferred_element_type=jnp.float32,
                )
                total = part if total is None else total + part
            results[0][0:size, i * size : (i + 1) * size] = total.astype(kind)
        if not extra:
            return

        def pieces(b, k):
            here = slice(k * (size // 4), (k + 1) * (size // 4))
            near, end = (
                read(refs, kind[b], size, slice(size, tall))[:, here] for kind in (own_views, views[-1])
            )
            return jnp.concatenate([end, near, near, end], axis=1) * rest[0][...]

        applied = rest[0][...] if own is None else pieces(0, turn + 1).astype(jnp.float32)
        for b in range(count):
            if own is None:
                rows = read(refs, views[-1][b], size, slice(size, tall))
            else:
                rows = pieces(b, turn)
            applied = applied + lax.dot_general(
                rows, left_ref[:, b * size : (b + 1) * size], NT, preferred_element_type=jnp.float32
            )
        results[-1][...] = applied
        if form != "open":
            for i in range(len(halves)):
                results[0][size:tall, i * size : (i + 1) * size] = applied.astype(kind)

    return pl.pallas_call(
        kernel,
        out_shape=tuple(outs),
        compiler_params=pltpu.CompilerParams(vmem_limit_bytes=VMEM),
        cost_estimate=pl.CostEstimate(
            flops=2 * weight * len(halves) * size * size * size * count,
            bytes_accessed=12 * weight * len(halves) * size * size,
            transcendentals=0,
        ),
    )(left, *extra, *operands.arrays)


def call(kernel, flops, outs, *operands):
    return pl.pallas_call(
        kernel,
        out_shape=outs,
        compiler_params=pltpu.CompilerParams(vmem_limit_bytes=VMEM),
        cost_estimate=pl.CostEstimate(flops=flops, bytes_accessed=1 << 20, transcendentals=0),
    )(*operands)


def early(value, weight=20):
    def kernel(value_ref, out):
        del value_ref, out

    return pl.pallas_call(
        kernel,
        out_shape=jax.ShapeDtypeStruct(value.shape, value.dtype),
        in_specs=[pl.BlockSpec(memory_space=pl.ANY)],
        out_specs=pl.BlockSpec(memory_space=pl.ANY),
        input_output_aliases={0: 0},
        compiler_params=pltpu.CompilerParams(vmem_limit_bytes=1024 * 1024),
        cost_estimate=pl.CostEstimate(flops=weight << 30, bytes_accessed=0, transcendentals=0),
    )(value)


def beside_each_other(left, right):
    size = left.shape[1]

    def kernel(left_ref, right_ref, out):
        out[:, 0:size] = left_ref[0:size, :]
        out[:, size : 2 * size] = right_ref[0:size, :]

    return call(kernel, 1, jax.ShapeDtypeStruct((size, 2 * size), left.dtype), left, right)


def pick_rows(pivots, block, tiles):
    size = tiles[0].shape[1]

    def kernel(q_ref, *refs):
        out = refs[-1]
        rows, places = None, None
        named = jnp.transpose(jnp.broadcast_to(q_ref[block : block + 1, :], (size, size)))
        for b, ref in enumerate(refs[:-1]):
            at = lax.broadcasted_iota(jnp.int32, (size, size), 1) + b * size
            hot = jnp.where(at == named, 1.0, 0.0).astype(jnp.bfloat16)
            part = jnp.dot(hot, ref[0:size, :], preferred_element_type=jnp.float32)
            rows = part if rows is None else rows + part
            part = lax.dot_general(
                ref[size : size + EXTRA, :], hot, NT, preferred_element_type=jnp.float32
            )
            places = part if places is None else places + part
        out[0:size, :] = rows.astype(out.dtype)
        out[size : size + EXTRA, :] = places.astype(out.dtype)

    flops = 2 * size * size * size * len(tiles)
    return call(kernel, flops, jax.ShapeDtypeStruct(tiles[0].shape, tiles[0].dtype), pivots, *tiles)


def finish(left, picked, base, applied):
    size = left.shape[1]

    def kernel(left_ref, picked_ref, base_ref, applied_ref, out, vector):
        part = jnp.dot(left_ref[...], picked_ref[0:size, :], preferred_element_type=jnp.float32)
        out[...] = (base_ref[...] + part).astype(out.dtype)
        vector[...] = applied_ref[...] + lax.dot_general(
            picked_ref[size : size + EXTRA, :], left_ref[...], NT, preferred_element_type=jnp.float32
        )

    outs = (
        jax.ShapeDtypeStruct((size, size), jnp.bfloat16),
        jax.ShapeDtypeStruct(applied.shape, applied.dtype),
    )
    return call(kernel, 2 * size * size * size, outs, left, picked, base, applied)


def after(value, *others):
    return lax.optimization_barrier((value, *others))[0]


def plain(*tiles):
    return [(tile, None, 0) for tile in tiles]


def shards(interval_blocks, interval_pivots, boundary_pivots, interval_residuals):
    blocks = interval_blocks[0]
    size, share = blocks.shape[1], interval_residuals.shape[2]
    row, col = lax.axis_index("row"), lax.axis_index("col")
    count = lax.axis_size("row")
    position = lax.axis_index("loop")
    positions = lax.axis_size("loop")

    own = lax.dynamic_index_in_dim(boundary_pivots, position, 0, keepdims=True)
    back = lax.dynamic_index_in_dim(
        boundary_pivots, (position + positions - 1) % positions, 0, keepdims=True
    )
    pivots = jnp.concatenate([interval_pivots[0], own, back], axis=0)
    pivots = (((pivots // size) ^ row) * size + pivots % size).reshape(pivots.shape[0], count, size)
    order = [
        lax.dynamic_index_in_dim(pivots, col ^ flip, 1, keepdims=True) for flip in (0, 1, 3, 2)
    ]
    pivots = jnp.concatenate(order, axis=1)
    places = lax.broadcasted_iota(jnp.int32, (1, size), 1)
    held = ((places < 2 * share) == (col == 1)).astype(jnp.bfloat16)
    pivots = [pivots[turn] for turn in range(5)]

    lefts = blocks[1::2]
    riding = jnp.broadcast_to(interval_residuals[0].reshape(1, -1), (EXTRA, size))
    tiles = [jnp.concatenate([blocks[k], riding], axis=0) for k in (0, 2)]
    rights = jnp.stack(tiles)
    lefts, rights, tiles, held, pivots = lax.optimization_barrier(
        (lefts, rights, tiles, held, pivots)
    )
    ends_left = inward(lefts)
    lefts_other = swap_middle(lefts)
    rights_across = swap_rows(rights, 2)
    end_lower = inward(tiles[0])
    end_upper = inward(tiles[1])
    rights_beside = swap_rows(rights, 1)

    def panel(turn, tiles, onto=None, weight=1):
        return spread_columns(pivots[turn], tiles, size, count, onto, weight)

    upper_panel, lower_panel = panel(2, [(0, (lefts, 1, 0))]), panel(0, [(0, (lefts, 0, 0))])
    ends_other = swap_middle(after(ends_left, upper_panel, lower_panel))
    rights_last = swap_rows(rights_across, 1)
    lower_panel = panel(0, [(1, (ends_left, 0, 0)), (2, (lefts_other, 0, 0))], lower_panel)
    upper_panel = panel(2, [(1, (ends_left, 1, 0)), (2, (lefts_other, 1, 0))], upper_panel)
    end_lower = after(end_lower, lower_panel, upper_panel)
    lower_across = swap_rows(end_lower, 2)
    lower_ends = [end_lower, swap_rows(end_lower, 1), lower_across, swap_rows(lower_across, 1)]
    upper_across = swap_rows(end_upper, 2)
    upper_ends = [end_upper, swap_rows(end_upper, 1), upper_across]
    lower_panel = panel(0, [(3, (ends_other, 0, 0))], lower_panel)
    upper_panel = panel(2, [(3, (ends_other, 1, 0))], upper_panel)

    def own_tiles(k):
        return [(tile, k, 0) for tile in (rights, rights_beside, rights_across, rights_last)]

    lower, _ = product(
        lower_panel, [own_tiles(0), plain(*lower_ends)], "joint", size, held, own_tiles(0), 0
    )
    upper_panel = after(upper_panel, lower)
    (upper_o,) = product(upper_panel, [own_tiles(1)], "apart", size)
    upper_ends.append(swap_rows(after(upper_across, upper_o), 1))
    upper_e, vector = product(
        upper_panel, [plain(*upper_ends)], "apart", size, held, own_tiles(1), 2
    )

    def right_views(right, tie):
        parts = []
        for tile in right:
            beside, across = swap_rows(tile, 1), early(swap_rows(tile, 2), 6)
            parts.append([tile, beside, across, swap_rows(after(across, *tie), 1)])
        if len(parts) == 1:
            return [[(tile, None, column) for tile in parts[0]] for column in (0, size)]
        return [plain(*part) for part in parts]

    other_o, other_e = early(swap_middle(upper_o), 4), early(swap_middle(upper_e), 10)
    moved = panel(1, [(0, (upper_o, None, 0)), (1, (upper_e, None, 0))])
    moved = panel(1, [(2, (other_o, None, 0))], moved)
    views = right_views([lower], (moved,))
    moved = panel(1, [(3, (other_e, None, 0))], moved)
    whole_e, vector = product(moved, views[1:], "apart", size, vector)
    (whole_o,) = product(after(moved, whole_e), views[:1], "apart", size)
    whole = beside_each_other(whole_o, whole_e)

    def tile_row(tile, across, *last_ties):
        return plain(tile, swap_rows(tile, 1), across, swap_rows(after(across, *last_ties), 1))

    earlier_e, earlier_o = from_behind(whole_e, "loop", 1), from_behind(whole_o, "loop", 1)
    other = swap_middle(whole)
    partial = panel(3, [(0, (whole, None, 0)), (1, (whole, None, size))])
    earlier_e = after(earlier_e, partial)
    across_e, across_o = swap_rows(earlier_e, 2), swap_rows(earlier_o, 2)
    views = tile_row(earlier_e, across_e, partial)
    moved = panel(3, [(2, (other, None, 0)), (3, (other, None, size))], partial)
    views_o = tile_row(earlier_o, across_o, moved)
    halved_e, vector = product(moved, [views], "apart", size, vector)
    (halved_o,) = product(after(moved, halved_e), [views_o], "apart", size)

    distant_e, distant_o = from_behind(halved_e, "loop", 2), from_behind(halved_o, "loop", 2)
    other_e, across_e = early(swap_middle(halved_e)), swap_rows(distant_e, 2)
    other_o, across_o = swap_middle(halved_o), swap_rows(distant_o, 2)
    partial = panel(4, [(0, (halved_o, None, 0)), (1, (halved_e, None, 0))])
    views = tile_row(after(distant_e, partial), across_e, partial)
    partial = panel(4, [(3, (other_e, None, 0))], partial)
    base, applied = product(partial, [views], "open", size, vector)
    picked = pick_rows(pivots[4], 2, [view[0] for view in views])
    views_o = tile_row(distant_o, across_o, base, picked)
    other_o = early(after(other_o, base, picked))
    reduced_e, vector = finish(other_o, picked, base, applied)
    moved = panel(4, [(2, (other_o, None, 0))], after(partial, reduced_e), 0)
    (reduced_o,) = product(moved, [views_o], "apart", size, weight=0)

    middle = (col == 1) | (col == 2)
    block = jnp.where(middle, reduced_o, outward(reduced_e))
    vector = after(vector, reduced_o)[:1]
    vector = vector + swap_middle(vector)
    vector = jnp.where(middle, vector, outward(vector))
    return (block[None], lax.dynamic_slice_in_dim(vector, col * share, share, 1))


def solution(mesh):
    placed = (
        P("loop", None, "row", "col"),
        P("loop", None, None),
        P(),
        P("loop", None, ("row", "col")),
    )
    return jax.shard_map(
        shards,
        mesh=mesh,
        in_specs=placed,
        out_specs=(P("loop", "row", "col"), P("loop", ("row", "col"))),
        check_vma=False,
    )
```

```python
import jax
import jax.numpy as jnp
from jax import lax
from jax.experimental import pallas as pl
from jax.experimental.pallas import tpu as pltpu
from jax.sharding import PartitionSpec as P

EXTRA = 16
VMEM = 14 * 1024 * 1024
NT = (((1,), (1,)), ((), ()))


def from_behind(value, axis, by):
    devices = lax.axis_size(axis)
    if by % devices == 0:
        return value
    return lax.ppermute(value, axis, [(i, (i + by) % devices) for i in range(devices)])


def swap_rows(value, flip):
    rows, cols = lax.axis_size("row"), lax.axis_size("col")
    pairs = [(r * cols + c, (r ^ flip) * cols + c) for r in range(rows) for c in (1, 2)]
    return lax.ppermute(value, ("row", "col"), pairs)


def swap_middle(value):
    return lax.ppermute(value, "col", [(1, 2), (2, 1)])


def inward(value):
    return lax.ppermute(value, "col", [(0, 1), (3, 2)])


def outward(value):
    return lax.ppermute(value, "col", [(1, 0), (2, 3)])


class Operands:
    def __init__(self):
        self.arrays = []

    def add(self, view):
        array, lead, column = view
        for i, known in enumerate(self.arrays):
            if known is array:
                return i, lead, column
        self.arrays.append(array)
        return len(self.arrays) - 1, lead, column


def read(refs, view, size, rows=None):
    which, lead, column = view
    ref = refs[which] if lead is None else refs[which].at[lead]
    return ref[rows or slice(0, size), column : column + size]


def spread(refs, views, q_ref, size, n):
    total = None
    for block, view in views:
        at = lax.broadcasted_iota(jnp.int32, (size, size), 0) + n * size
        hot = jnp.where(at == q_ref[block : block + 1, :], 1.0, 0.0).astype(jnp.bfloat16)
        part = lax.dot_general(
            read(refs, view, size), hot, NT, preferred_element_type=jnp.float32
        )
        total = part if total is None else total + part
    return total


def spread_columns(pivots, tiles, size, count, onto=None, weight=1):
    operands = Operands()
    views = [(block, operands.add(view)) for block, view in tiles]
    extra = [] if onto is None else [onto]

    def kernel(q_ref, *refs):
        out = refs[-1]

        @pl.loop(0, count)
        def _(n):
            here = pl.ds(pl.multiple_of(n * size, size), size)
            moved = spread(refs[len(extra) :], views, q_ref, size, n).astype(out.dtype)
            out[:, here] = moved if onto is None else moved + refs[0][:, here]

    return pl.pallas_call(
        kernel,
        out_shape=jax.ShapeDtypeStruct((size, size * count), jnp.bfloat16),
        compiler_params=pltpu.CompilerParams(vmem_limit_bytes=VMEM),
        cost_estimate=pl.CostEstimate(
            flops=2 * weight * len(tiles) * size * size * size * count,
            bytes_accessed=8 * weight * size * size,
            transcendentals=0,
        ),
    )(pivots, *extra, *operands.arrays)


def product(left, halves, form, size, added=None, own=None, turn=0, weight=1):
    count = left.shape[1] // size
    operands = Operands()
    views = [[operands.add(view) for view in half] for half in halves]
    own_views = [operands.add(view) for view in own or []]
    extra = [] if added is None else [added]
    tall, wide = size + (EXTRA if extra else 0), size * len(halves)
    kind = jnp.float32 if form == "open" else jnp.bfloat16
    shapes = {"joint": [(tall, wide)], "apart": [(tall, size)], "open": [(size, size)], "twice": [(tall, size), (size, size)]}[form]
    outs = [jax.ShapeDtypeStruct(shape, kind) for shape in shapes]
    if extra:
        outs.append(jax.ShapeDtypeStruct((EXTRA, size), jnp.float32))

    def kernel(left_ref, *rest):
        refs = rest[len(extra) : len(extra) + len(operands.arrays)]
        results = rest[len(extra) + len(refs) :]
        for i, half in enumerate(views):
            total = None
            for b in range(count):
                part = jnp.dot(
                    left_ref[:, b * size : (b + 1) * size],
                    read(refs, half[b], size),
                    preferred_element_type=jnp.float32,
                )
                total = part if total is None else total + part
            results[0][0:size, i * size : (i + 1) * size] = total.astype(kind)
            if form == "twice":
                results[1][...] = total.astype(kind)
        if not extra:
            return

        def pieces(b, k):
            here = slice(k * (size // 4), (k + 1) * (size // 4))
            near, end = (
                read(refs, kind[b], size, slice(size, tall))[:, here] for kind in (own_views, views[-1])
            )
            return jnp.concatenate([end, near, near, end], axis=1) * rest[0][...]

        applied = rest[0][...] if own is None else pieces(0, turn + 1).astype(jnp.float32)
        for b in range(count):
            if own is None:
                rows = read(refs, views[-1][b], size, slice(size, tall))
            else:
                rows = pieces(b, turn)
            applied = applied + lax.dot_general(
                rows, left_ref[:, b * size : (b + 1) * size], NT, preferred_element_type=jnp.float32
            )
        results[-1][...] = applied
        if form != "open":
            for i in range(len(halves)):
                results[0][size:tall, i * size : (i + 1) * size] = applied.astype(kind)

    return pl.pallas_call(
        kernel,
        out_shape=tuple(outs),
        compiler_params=pltpu.CompilerParams(vmem_limit_bytes=VMEM),
        cost_estimate=pl.CostEstimate(
            flops=2 * weight * len(halves) * size * size * size * count,
            bytes_accessed=12 * weight * len(halves) * size * size,
            transcendentals=0,
        ),
    )(left, *extra, *operands.arrays)


def call(kernel, flops, outs, *operands):
    return pl.pallas_call(
        kernel,
        out_shape=outs,
        compiler_params=pltpu.CompilerParams(vmem_limit_bytes=VMEM),
        cost_estimate=pl.CostEstimate(flops=flops, bytes_accessed=1 << 20, transcendentals=0),
    )(*operands)


def early(value, weight=20):
    def kernel(value_ref, out):
        del value_ref, out

    return pl.pallas_call(
        kernel,
        out_shape=jax.ShapeDtypeStruct(value.shape, value.dtype),
        in_specs=[pl.BlockSpec(memory_space=pl.ANY)],
        out_specs=pl.BlockSpec(memory_space=pl.ANY),
        input_output_aliases={0: 0},
        compiler_params=pltpu.CompilerParams(vmem_limit_bytes=1024 * 1024),
        cost_estimate=pl.CostEstimate(flops=weight << 30, bytes_accessed=0, transcendentals=0),
    )(value)


def beside_each_other(left, right):
    size = left.shape[1]

    def kernel(left_ref, right_ref, out):
        out[:, 0:size] = left_ref[0:size, :]
        out[:, size : 2 * size] = right_ref[0:size, :]

    return call(kernel, 1, jax.ShapeDtypeStruct((size, 2 * size), left.dtype), left, right)


def pick_rows(pivots, block, tiles):
    size = tiles[0].shape[1]

    def kernel(q_ref, *refs):
        out = refs[-1]
        rows, places = None, None
        named = jnp.transpose(jnp.broadcast_to(q_ref[block : block + 1, :], (size, size)))
        for b, ref in enumerate(refs[:-1]):
            at = lax.broadcasted_iota(jnp.int32, (size, size), 1) + b * size
            hot = jnp.where(at == named, 1.0, 0.0).astype(jnp.bfloat16)
            part = jnp.dot(hot, ref[0:size, :], preferred_element_type=jnp.float32)
            rows = part if rows is None else rows + part
            part = lax.dot_general(
                ref[size : size + EXTRA, :], hot, NT, preferred_element_type=jnp.float32
            )
            places = part if places is None else places + part
        out[0:size, :] = rows.astype(out.dtype)
        out[size : size + EXTRA, :] = places.astype(out.dtype)

    flops = 2 * size * size * size * len(tiles)
    return call(kernel, flops, jax.ShapeDtypeStruct(tiles[0].shape, tiles[0].dtype), pivots, *tiles)


def finish(left, picked, base, applied):
    size = left.shape[1]

    def kernel(left_ref, picked_ref, base_ref, applied_ref, out, vector):
        part = jnp.dot(left_ref[...], picked_ref[0:size, :], preferred_element_type=jnp.float32)
        out[...] = (base_ref[...] + part).astype(out.dtype)
        vector[...] = applied_ref[...] + lax.dot_general(
            picked_ref[size : size + EXTRA, :], left_ref[...], NT, preferred_element_type=jnp.float32
        )

    outs = (
        jax.ShapeDtypeStruct((size, size), jnp.bfloat16),
        jax.ShapeDtypeStruct(applied.shape, applied.dtype),
    )
    return call(kernel, 2 * size * size * size, outs, left, picked, base, applied)


def after(value, *others):
    return lax.optimization_barrier((value, *others))[0]


def plain(*tiles):
    return [(tile, None, 0) for tile in tiles]


def shards(interval_blocks, interval_pivots, boundary_pivots, interval_residuals):
    blocks = interval_blocks[0]
    size, share = blocks.shape[1], interval_residuals.shape[2]
    row, col = lax.axis_index("row"), lax.axis_index("col")
    count = lax.axis_size("row")
    position = lax.axis_index("loop")
    positions = lax.axis_size("loop")

    own = lax.dynamic_index_in_dim(boundary_pivots, position, 0, keepdims=True)
    back = lax.dynamic_index_in_dim(
        boundary_pivots, (position + positions - 1) % positions, 0, keepdims=True
    )
    pivots = jnp.concatenate([interval_pivots[0], own, back], axis=0)
    pivots = (((pivots // size) ^ row) * size + pivots % size).reshape(pivots.shape[0], count, size)
    order = [
        lax.dynamic_index_in_dim(pivots, col ^ flip, 1, keepdims=True) for flip in (0, 1, 3, 2)
    ]
    pivots = jnp.concatenate(order, axis=1)
    places = lax.broadcasted_iota(jnp.int32, (1, size), 1)
    held = ((places < 2 * share) == (col == 1)).astype(jnp.bfloat16)
    pivots = [pivots[turn] for turn in range(5)]

    lefts = blocks[1::2]
    riding = jnp.broadcast_to(interval_residuals[0].reshape(1, -1), (EXTRA, size))
    tiles = [jnp.concatenate([blocks[k], riding], axis=0) for k in (0, 2)]
    rights = jnp.stack(tiles)
    lefts, rights, tiles, held, pivots = lax.optimization_barrier(
        (lefts, rights, tiles, held, pivots)
    )
    ends_left = inward(lefts)
    lefts_other = swap_middle(lefts)
    rights_across = swap_rows(rights, 2)
    end_lower = inward(tiles[0])
    end_upper = inward(tiles[1])
    rights_beside = swap_rows(rights, 1)

    def panel(turn, tiles, onto=None, weight=1):
        return spread_columns(pivots[turn], tiles, size, count, onto, weight)

    upper_panel, lower_panel = panel(2, [(0, (lefts, 1, 0))]), panel(0, [(0, (lefts, 0, 0))])
    ends_other = swap_middle(after(ends_left, upper_panel, lower_panel))
    rights_last = swap_rows(rights_across, 1)
    lower_panel = panel(0, [(1, (ends_left, 0, 0)), (2, (lefts_other, 0, 0))], lower_panel)
    upper_panel = panel(2, [(1, (ends_left, 1, 0)), (2, (lefts_other, 1, 0))], upper_panel)
    end_lower = after(end_lower, lower_panel, upper_panel)
    lower_across = swap_rows(end_lower, 2)
    lower_ends = [end_lower, swap_rows(end_lower, 1), lower_across, swap_rows(lower_across, 1)]
    upper_across = swap_rows(end_upper, 2)
    upper_ends = [end_upper, swap_rows(end_upper, 1), upper_across]
    lower_panel = panel(0, [(3, (ends_other, 0, 0))], lower_panel)
    upper_panel = panel(2, [(3, (ends_other, 1, 0))], upper_panel)

    def own_tiles(k):
        return [(tile, k, 0) for tile in (rights, rights_beside, rights_across, rights_last)]

    lower, _ = product(
        lower_panel, [own_tiles(0), plain(*lower_ends)], "joint", size, held, own_tiles(0), 0
    )
    upper_panel = after(upper_panel, lower)
    (upper_o,) = product(upper_panel, [own_tiles(1)], "apart", size)
    upper_ends.append(swap_rows(after(upper_across, upper_o), 1))
    upper_e, vector = product(
        upper_panel, [plain(*upper_ends)], "apart", size, held, own_tiles(1), 2
    )

    def right_views(right, tie):
        parts = []
        for tile in right:
            beside, across = swap_rows(tile, 1), early(swap_rows(tile, 2), 6)
            parts.append([tile, beside, across, swap_rows(after(across, *tie), 1)])
        if len(parts) == 1:
            return [[(tile, None, column) for tile in parts[0]] for column in (0, size)]
        return [plain(*part) for part in parts]

    other_o, other_e = early(swap_middle(upper_o), 4), early(swap_middle(upper_e), 10)
    moved = panel(1, [(0, (upper_o, None, 0)), (1, (upper_e, None, 0))])
    moved = panel(1, [(2, (other_o, None, 0))], moved)
    views = right_views([lower], (moved,))
    moved = panel(1, [(3, (other_e, None, 0))], moved)
    whole_e, vector = product(moved, views[1:], "apart", size, vector)
    (whole_o,) = product(after(moved, whole_e), views[:1], "apart", size)
    whole = beside_each_other(whole_o, whole_e)

    def tile_row(tile, across, *last_ties):
        return plain(tile, swap_rows(tile, 1), across, swap_rows(after(across, *last_ties), 1))

    earlier_e, earlier_o = from_behind(whole_e, "loop", 1), from_behind(whole_o, "loop", 1)
    other = swap_middle(whole)
    partial = panel(3, [(0, (whole, None, 0)), (1, (whole, None, size))])
    earlier_e = after(earlier_e, partial)
    across_e, across_o = swap_rows(earlier_e, 2), swap_rows(earlier_o, 2)
    views = tile_row(earlier_e, across_e, partial)
    moved = panel(3, [(2, (other, None, 0)), (3, (other, None, size))], partial)
    views_o = tile_row(earlier_o, across_o, moved)
    halved_e, plain_e, vector = product(moved, [views], "twice", size, vector)
    (halved_o,) = product(after(moved, halved_e), [views_o], "apart", size)

    distant_e, distant_o = from_behind(halved_e, "loop", 2), from_behind(halved_o, "loop", 2)
    other_e, across_e = early(swap_middle(plain_e)), swap_rows(distant_e, 2)
    other_o, across_o = swap_middle(halved_o), swap_rows(distant_o, 2)
    partial = panel(4, [(0, (halved_o, None, 0)), (1, (halved_e, None, 0))])
    views = tile_row(after(distant_e, partial), across_e, partial)
    partial = panel(4, [(3, (other_e, None, 0))], partial)
    base, applied = product(partial, [views], "open", size, vector)
    picked = pick_rows(pivots[4], 2, [view[0] for view in views])
    views_o = tile_row(distant_o, across_o, base, picked)
    other_o = early(after(other_o, base, picked))
    reduced_e, vector = finish(other_o, picked, base, applied)
    moved = panel(4, [(2, (other_o, None, 0))], after(partial, reduced_e), 0)
    (reduced_o,) = product(moved, [views_o], "apart", size, weight=0)

    middle = (col == 1) | (col == 2)
    block = jnp.where(middle, reduced_o, outward(reduced_e))
    vector = after(vector, reduced_o)[:1]
    vector = vector + swap_middle(vector)
    vector = jnp.where(middle, vector, outward(vector))
    return (block[None], lax.dynamic_slice_in_dim(vector, col * share, share, 1))


def solution(mesh):
    placed = (
        P("loop", None, "row", "col"),
        P("loop", None, None),
        P(),
        P("loop", None, ("row", "col")),
    )
    return jax.shard_map(
        shards,
        mesh=mesh,
        in_specs=placed,
        out_specs=(P("loop", "row", "col"), P("loop", ("row", "col"))),
        check_vma=False,
    )
```
